32 devices in a mesh: fsdp: 16 (over z, y, core), ctx: 2 (over x).
Axes of the slice: x: 2, y: 2, z: 4, core: 2. Of those that a mesh axis runs over, the one named last changes fastest.
Arguments:
- hidden_in: bfloat16 [16, 1024, 1024], P('fsdp', 'ctx'), may hold values from -6 to 6
- positions: int32 [16, 1024], P('fsdp', 'ctx'), may hold values from 0 to 1023, as said below
- cotangent: bfloat16 [16, 1024, 1024], P('fsdp', 'ctx'), may hold values from -6 to 6
- norm_gain: float32 [1024], replicated, may hold values from 0.1 to 1.9
- w_query: bfloat16 [1024, 2048], P('fsdp'), may hold values from -0.1875 to 0.1875
- w_key: bfloat16 [1024, 1024], P('fsdp'), may hold values from -0.1875 to 0.1875
- w_value: bfloat16 [1024, 1024], P('fsdp'), may hold values from -0.1875 to 0.1875
- query_gain: float32 [128], replicated, may hold values from 0.1 to 1.9
- key_gain: float32 [128], replicated, may hold values from 0.1 to 1.9
- w_out: bfloat16 [2048, 1024], P('fsdp'), may hold values from -1 to 1
- mlp_gain: float32 [1024], replicated, may hold values from 0.1 to 1.9
- w_gate: bfloat16 [1024, 3072], P('fsdp'), may hold values from -0.1875 to 0.1875
- w_up: bfloat16 [1024, 3072], P('fsdp'), may hold values from -0.1875 to 0.1875
- w_down: bfloat16 [3072, 1024], P('fsdp'), may hold values from -0.109375 to 0.109375
Outputs:
- output: bfloat16 [16, 1024, 1024], P('fsdp', 'ctx')
- grad_input: bfloat16 [16, 1024, 1024], P('fsdp', 'ctx')
- grad_norm_gain: float32 [1024], replicated
- grad_w_query: float32 [1024, 2048], P('fsdp')
- grad_w_key: float32 [1024, 1024], P('fsdp')
- grad_w_value: float32 [1024, 1024], P('fsdp')
- grad_query_gain: float32 [128], replicated
- grad_key_gain: float32 [128], replicated
- grad_w_out: float32 [2048, 1024], P('fsdp')
- grad_mlp_gain: float32 [1024], replicated
- grad_w_gate: float32 [1024, 3072], P('fsdp')
- grad_w_up: float32 [1024, 3072], P('fsdp')
- grad_w_down: float32 [3072, 1024], P('fsdp')
The draws below stay inside these ranges and needn't reach their ends.
Inputs may be any that keep to these rules, and one draw needn't show every extreme that they name: `positions`: positions start at 0 at each document's first token and rise by one within it. Documents in a sequence have 1024 // 10 to 1024 tokens, but a sequence may begin inside a document with fewer than 102 of its earlier tokens counted, and such a first piece may be shorter. Among the 1 sequence of each index of fsdp one holds a document that starts within its first 512 tokens and runs to its end.
All inputs are finite; a program needn't handle non-finite values.
Results may differ from the reference program's by a relative error of at most 0.02.
Values may be sent and summed in bfloat16 or wider, within the bound.
A program may use at most 256 MiB of HBM per device.

```python
import jax
import jax.numpy as jnp
from jax import lax

D = 1024
HQ = 16
KV = 8
HD = 128
FF = 3072
SEQ_LEN = 1024
BLK = 512
SEQS_DEV = 1
SEQS = 16


def draw_positions(key, part):
    key = jax.random.fold_in(key, 7)
    shortest = max(SEQ_LEN // 10, 2)
    slot_count = SEQ_LEN // shortest + 2
    key_lengths, key_offset, key_pick, key_begin, key_before = jax.random.split(key, 5)
    lengths = jax.random.randint(key_lengths, (SEQS, slot_count), shortest, SEQ_LEN + 1)
    offset = jax.random.randint(key_offset, (SEQS, 1), 0, shortest)
    first_len = jnp.minimum(lengths[:, :1], SEQ_LEN - offset)
    lengths = jnp.concatenate([first_len, lengths[:, 1:]], axis=1)
    starts = jnp.cumsum(lengths, axis=1) - lengths - offset
    token_index = jnp.arange(SEQ_LEN, dtype=jnp.int32)
    started = starts[:, None, :] <= token_index[None, :, None]
    doc_start = jnp.max(jnp.where(started, starts[:, None, :], -SEQ_LEN), axis=-1)
    packed = token_index[None, :] - doc_start
    group_count = SEQS // SEQS_DEV
    chosen = jax.random.randint(key_pick, (group_count,), 0, SEQS_DEV)
    row_index = jnp.arange(SEQS, dtype=jnp.int32)
    single = row_index % SEQS_DEV == jnp.repeat(chosen, SEQS_DEV)
    begin = jax.random.randint(key_begin, (SEQS, 1), 0, BLK)
    before = jax.random.randint(key_before, (SEQS, 1), 0, shortest)
    long_doc = jnp.where(token_index[None, :] < begin, before + token_index[None, :], token_index[None, :] - begin)
    return jnp.where(single[:, None], long_doc, packed).astype(jnp.int32)


def block_scale(key, extent, cuts, least, high):
    def one(dim, blocks):
        steps = jax.random.uniform(jax.random.fold_in(jax.random.fold_in(key, 6), dim), (blocks,), jnp.float32, least / len(cuts), high / len(cuts))
        return jnp.repeat(jnp.exp(steps), extent[dim] // blocks).reshape((-1,) + (1,) * (len(extent) - dim - 1))

    level = one(*cuts[0])
    for cut in cuts[1:]:
        level = level * one(*cut)
    return level


def gaussian(key, dims, deviation, reach, cuts=(), held_as=jnp.bfloat16):
    drawn = deviation * jax.random.normal(key, dims, jnp.float32)
    if cuts:
        drawn = drawn * block_scale(key, dims, cuts, -0.22, 0.18)
    return jnp.clip(drawn, -reach, reach).astype(held_as)


def setup_inputs(seed: int = 0) -> dict:
    streams_of = jax.random.split(jax.random.key(seed), 15)
    return {
        "hidden_in": gaussian(streams_of[0], (SEQS, SEQ_LEN, D), 1.0, 6.0, ((0, 16), (1, 2))),
        "positions": draw_positions(jax.random.fold_in(streams_of[14], 71), 0),
        "cotangent": gaussian(streams_of[2], (SEQS, SEQ_LEN, D), 1.0, 6.0, ((0, 16), (1, 2))),
        "norm_gain": jnp.clip(1.0 + 0.18 * jax.random.normal(streams_of[3], (D,), jnp.float32), 0.1, 1.9),
        "w_query": gaussian(streams_of[4], (D, HQ * HD), D ** -0.5, 0.1875, ((0, 16),)),
        "w_key": gaussian(streams_of[5], (D, KV * HD), D ** -0.5, 0.1875, ((0, 16),)),
        "w_value": gaussian(streams_of[6], (D, KV * HD), D ** -0.5, 0.1875, ((0, 16),)),
        "query_gain": jnp.clip(1.0 + 0.18 * jax.random.normal(streams_of[7], (HD,), jnp.float32), 0.1, 1.9),
        "key_gain": jnp.clip(1.0 + 0.18 * jax.random.normal(streams_of[8], (HD,), jnp.float32), 0.1, 1.9),
        "w_out": gaussian(streams_of[9], (HQ * HD, D), (HQ * HD // 64) ** -0.5, 1.0, ((0, 16),)),
        "mlp_gain": jnp.clip(1.0 + 0.18 * jax.random.normal(streams_of[10], (D,), jnp.float32), 0.1, 1.9),
        "w_gate": gaussian(streams_of[11], (D, FF), D ** -0.5, 0.1875, ((0, 16),)),
        "w_up": gaussian(streams_of[12], (D, FF), D ** -0.5, 0.1875, ((0, 16),)),
        "w_down": gaussian(streams_of[13], (FF, D), FF ** -0.5, 0.109375, ((0, 16),)),
    }


epsilon = 1e-06
theta_base = 1000000.0
highest = lax.Precision.HIGHEST

@jax.custom_vjp
def low(v):
    return lax.optimization_barrier(v.astype(jnp.bfloat16)).astype(jnp.float32)

@jax.custom_vjp
def low_back(v):
    return v

def low_keep(v):
    return (low(v), None)

def low_pass(kept, grad):
    return (grad,)

def back_keep(v):
    return (v, None)

def back_low(kept, grad):
    return (low(grad),)
low.defvjp(low_keep, low_pass)
low_back.defvjp(back_keep, back_low)

def matmul(left, right):
    return jnp.dot(left, right, preferred_element_type=jnp.float32, precision=highest)

def norm_rows(values, gain_vec):
    return values * lax.rsqrt(lax.optimization_barrier(jnp.mean(values * values, axis=-1, keepdims=True)) + epsilon) * gain_vec

def rope_tables(positions, head_dim):
    frequency = theta_base ** (-jnp.arange(0, head_dim, 2).astype(jnp.float32) / head_dim)
    angles = positions.astype(jnp.float32)[:, None] * frequency[None, :]
    angles = jnp.concatenate([angles, angles], axis=-1)
    return (jnp.cos(angles), jnp.sin(angles))

def rotate(values, cosine, sine_tab):
    half_dim = values.shape[-1] // 2
    turned = jnp.concatenate([-values[..., half_dim:], values[..., :half_dim]], axis=-1)
    return values * cosine[:, None, :] + turned * sine_tab[:, None, :]

def one_sequence(params, residual, positions):
    norm_gain, w_query, w_key, w_value, query_gain, key_gain, w_out, mlp_gain, w_gate, w_up, w_down = params
    seq_rows = residual.shape[0]
    groups = HQ // KV
    attn_in = low(norm_rows(residual, norm_gain))
    query_raw = low_back(matmul(attn_in, w_query)).reshape(seq_rows, HQ, HD)
    key_raw = low_back(matmul(attn_in, w_key)).reshape(seq_rows, KV, HD)
    value_rows = low(low_back(matmul(attn_in, w_value))).reshape(seq_rows, KV, HD)
    cosine, sine_tab = rope_tables(positions, HD)
    query_rot = low(rotate(norm_rows(query_raw, query_gain), cosine, sine_tab))
    key_rot = low(rotate(norm_rows(key_raw, key_gain), cosine, sine_tab))
    token_index = jnp.arange(seq_rows, dtype=jnp.int32)
    doc_start = token_index - positions.astype(jnp.int32)
    allowed = (token_index[None, :] <= token_index[:, None]) & (token_index[None, :] >= doc_start[:, None])
    grouped = query_rot.reshape(seq_rows, KV, groups, HD)
    scores = jnp.einsum('qkgd,pkd->kgqp', grouped, key_rot, precision=highest, preferred_element_type=jnp.float32)
    scores = low_back(scores * HD ** (-0.5))
    scores = jnp.where(allowed[None, None], scores, -1e+30)
    row_max = lax.optimization_barrier(jnp.max(scores, axis=-1, keepdims=True))
    exponent = jnp.exp(scores - row_max)
    soft_probs = exponent / lax.optimization_barrier(jnp.sum(exponent, axis=-1, keepdims=True))
    attn_out = jnp.einsum('kgqp,pkd->qkgd', low(soft_probs), value_rows, precision=highest, preferred_element_type=jnp.float32)
    attn_out = low(low_back(attn_out.reshape(seq_rows, HQ * HD)))
    middle = residual + low_back(matmul(attn_out, w_out))
    mlp_in = low(norm_rows(middle, mlp_gain))
    gate_pre = low_back(matmul(mlp_in, w_gate))
    up_pre = low_back(matmul(mlp_in, w_up))
    hidden_act = low(jax.nn.silu(gate_pre) * up_pre)
    return middle + low_back(matmul(hidden_act, w_down))

def reference(hidden_in, positions, cotangent, norm_gain, w_query, w_key, w_value, query_gain, key_gain, w_out, mlp_gain, w_gate, w_up, w_down):
    params = tuple((member.astype(jnp.float32) for member in (norm_gain, w_query, w_key, w_value, query_gain, key_gain, w_out, mlp_gain, w_gate, w_up, w_down)))
    inputs = hidden_in.astype(jnp.float32)

    def forward(layer_in, layer_params):

        def scan_step(scan_carry, sequence_pair):
            return (scan_carry, jax.checkpoint(one_sequence)(layer_params, sequence_pair[0], sequence_pair[1]))
        scan_carry, outputs = lax.scan(scan_step, jnp.zeros((), jnp.float32), (layer_in, positions))
        return outputs
    outputs, pullback = jax.vjp(forward, inputs, params)
    grad_inputs, grad_params = pullback(cotangent.astype(jnp.float32))
    return (outputs.astype(jnp.bfloat16), grad_inputs.astype(jnp.bfloat16), grad_params[0], grad_params[1], grad_params[2], grad_params[3], grad_params[4], grad_params[5], grad_params[6], grad_params[7], grad_params[8], grad_params[9], grad_params[10])
```

```python
import functools

import jax
import jax.numpy as jnp
from jax import lax
from jax.experimental import pallas as pl
from jax.experimental.pallas import tpu as pltpu
from jax.sharding import PartitionSpec as P

MESH = pl.DeviceIdType.MESH

epsilon = 1e-06
theta_base = 1000000.0


def as_sent(shard):

    def short(part):
        return part.astype(jnp.bfloat16) if part.dtype == jnp.float32 else part

    return jax.tree.map(short, shard)


def norm_rows(values, gain_vec):
    inverse = lax.rsqrt(jnp.mean(values * values, axis=-1, keepdims=True) + epsilon)
    normed = values * inverse
    return (normed * gain_vec, normed, inverse)


def norm_back(grad_out, gain_vec, normed, inverse):
    scaled = grad_out * gain_vec
    grad_in = inverse * (scaled - normed * jnp.mean(scaled * normed, axis=-1, keepdims=True))
    return (grad_in, grad_out * normed)


def rope_tables(positions, head_dim):
    frequency = theta_base ** (-jnp.arange(0, head_dim, 2).astype(jnp.float32) / head_dim)
    angles = positions.astype(jnp.float32)[:, None] * frequency[None, :]
    angles = jnp.concatenate([angles, angles], axis=-1)
    return (jnp.cos(angles), jnp.sin(angles))


def rotate(values, cosine, sine_tab):
    half_dim = values.shape[-1] // 2
    turned = jnp.concatenate([-values[..., half_dim:], values[..., :half_dim]], axis=-1)
    return values * cosine[:, None, :] + turned * sine_tab[:, None, :]


def rotate_back(grad_out, cosine, sine_tab):
    half_dim = grad_out.shape[-1] // 2
    weighted = grad_out * sine_tab[:, None, :]
    turned = jnp.concatenate([weighted[..., half_dim:], -weighted[..., :half_dim]], axis=-1)
    return grad_out * cosine[:, None, :] + turned


def back_dot(grad_rows, weight):
    return lax.dot_general(
        grad_rows, weight, (((1,), (1,)), ((), ())), preferred_element_type=jnp.float32
    )


def weight_term(acts_in, grad_out):
    return lax.dot_general(
        acts_in, grad_out, (((0,), (0,)), ((), ())), preferred_element_type=jnp.float32
    )


def place():
    f = lax.axis_index("fsdp")
    return f // 4, (f // 2) % 2, f % 2, lax.axis_index("ctx")


def enter(z, y, c, x):
    bar = pltpu.get_barrier_semaphore()

    def hail(z2, y2, c2, x2):
        pl.semaphore_signal(bar, inc=1, device_id=(z2 * 4 + y2 * 2 + c2, x2), device_id_type=MESH)

    hail(z, y, c, 1 - x)
    hail(z, 1 - y, c, x)
    hail(z, y, 1 - c, x)

    @pl.when(z > 0)
    def _():
        hail(z - 1, y, c, x)

    @pl.when(z < 3)
    def _():
        hail(z + 1, y, c, x)

    pl.semaphore_wait(bar, 4 + (z * (3 - z)) // 2)


class Gather:
    def __init__(self, index, own, full, sems, at):
        self.g, self.own, self.full = index, own, full
        self.zr, self.yr, self.xr, self.cr, self.zs, self.ys, self.xs, self.cs, self.ls = sems
        self.z, self.y, self.c, self.x = at
        self.rows, self.cols = own.shape
        unit = self.cols // 8
        x = self.x
        self.ywin = pl.ds(pl.multiple_of(x * 3 * unit, 128), 5 * unit)
        self.xwin = pl.ds(pl.multiple_of(x * 5 * unit, 128), 3 * unit)
        self.xgot = pl.ds(pl.multiple_of((1 - x) * 5 * unit, 128), 3 * unit)
        self.all = pl.ds(0, self.cols)
        self.ends = []

    def part(self, z2, y2, c2, win):
        f2 = z2 * 4 + y2 * 2 + c2
        return self.full.at[pl.ds(pl.multiple_of(f2 * self.rows, 16), self.rows), win]

    def send(self, src, dst, ssem, rsem, to):
        z2, y2, c2, x2 = to
        return pltpu.make_async_remote_copy(
            src_ref=src, dst_ref=dst, send_sem=ssem, recv_sem=rsem,
            device_id=(z2 * 4 + y2 * 2 + c2, x2), device_id_type=MESH)

    def z_copy(self, zs, up, first):
        dst = self.part(zs, self.y, self.c, self.ywin)
        src = self.own.at[:, self.ywin] if first else dst
        z2 = self.z + 1 if up else self.z - 1
        return self.send(src, dst, self.zs.at[self.g, zs, 1 if up else 0], self.zr.at[self.g, zs], (z2, self.y, self.c, self.x))

    def y_copy(self, zs, first):
        dst = self.part(zs, self.y, self.c, self.ywin)
        src = self.own.at[:, self.ywin] if first else dst
        return self.send(src, dst, self.ys.at[self.g, zs], self.yr.at[self.g, zs], (self.z, 1 - self.y, self.c, self.x))

    def x_copy(self, zs, y2):
        dst = self.part(zs, y2, self.c, self.xwin)
        s = zs * 2 + y2
        return self.send(dst, dst, self.xs.at[self.g, s], self.xr.at[self.g, s], (self.z, self.y, self.c, 1 - self.x))

    def c_copy(self, zs, y2, win, piece, first=False):
        dst = self.part(zs, y2, self.c, win)
        src = self.own if first else dst
        s = (zs * 2 + y2) * 2 + piece
        return self.send(src, dst, self.cs.at[self.g, s], self.cr.at[self.g, s], (self.z, self.y, 1 - self.c, self.x))

    def await_(self, dst, sem):
        pltpu.make_async_copy(dst, dst, sem).wait()

    def local(self):
        return pltpu.make_async_copy(self.own, self.part(self.z, self.y, self.c, self.all), self.ls.at[self.g])

    def begin(self):
        z = self.z

        @pl.when(z < 3)
        def _():
            self.z_copy(z, True, True).start()

        @pl.when(z > 0)
        def _():
            self.z_copy(z, False, True).start()

        self.y_copy(z, True).start()
        self.c_copy(z, self.y, self.all, 0, True).start()
        self.local().start()

    def spread(self, zs, up):
        self.await_(self.part(zs, self.y, self.c, self.ywin), self.zr.at[self.g, zs])

        @pl.when(self.z < 3 if up else self.z > 0)
        def _():
            self.z_copy(zs, up, False).start()

        self.y_copy(zs, False).start()
        self.x_copy(zs, self.y).start()
        self.c_copy(zs, self.y, self.ywin, 0).start()

    def along_z(self, k):
        @pl.when(self.z >= k)
        def _():
            self.spread(self.z - k, True)

        @pl.when(self.z + k <= 3)
        def _():
            self.spread(self.z + k, False)

    def over_y(self, zs):
        self.await_(self.part(zs, 1 - self.y, self.c, self.ywin), self.yr.at[self.g, zs])
        self.x_copy(zs, 1 - self.y).start()
        self.c_copy(zs, 1 - self.y, self.ywin, 0).start()

    def along_y(self, k):
        if k == 0:
            self.over_y(self.z)
            return

        @pl.when(self.z >= k)
        def _():
            self.over_y(self.z - k)

        @pl.when(self.z + k <= 3)
        def _():
            self.over_y(self.z + k)

    def over_x(self, zs, y2):
        self.await_(self.part(zs, y2, self.c, self.xgot), self.xr.at[self.g, zs * 2 + y2])
        self.c_copy(zs, y2, self.xgot, 1).start()

    def along_x(self, k):
        if k == 0:
            self.over_x(self.z, 1 - self.y)
            return

        for y2 in (self.y, 1 - self.y):
            @pl.when(self.z >= k)
            def _():
                self.over_x(self.z - k, y2)

            @pl.when(self.z + k <= 3)
            def _():
                self.over_x(self.z + k, y2)

    def finish(self):
        z, y = self.z, self.y
        self.local().wait()
        c = 1 - self.c
        self.await_(self.part(z, y, c, self.all), self.cr.at[self.g, (z * 2 + y) * 2])
        for k in range(0, 4):
            for y2 in ((y, 1 - y) if k else (1 - y,)):
                for zs, ok in ((z - k, z >= k), (z + k, z + k <= 3))[: 2 if k else 1]:
                    @pl.when(ok)
                    def _():
                        s = (zs * 2 + y2) * 2
                        self.await_(self.part(zs, y2, c, self.ywin), self.cr.at[self.g, s])
                        self.await_(self.part(zs, y2, c, self.xgot), self.cr.at[self.g, s + 1])

    def drain(self):
        z, y = self.z, self.y

        @pl.when(z < 3)
        def _():
            self.z_copy(z, True, True).wait_send()

        @pl.when(z > 0)
        def _():
            self.z_copy(z, False, True).wait_send()

        self.y_copy(z, True).wait_send()
        self.c_copy(z, y, self.all, 0, True).wait_send()
        self.x_copy(z, 1 - y).wait_send()
        self.c_copy(z, 1 - y, self.ywin, 0).wait_send()
        self.c_copy(z, 1 - y, self.xgot, 1).wait_send()
        for k in range(1, 4):
            for zs, ok, more, up in ((z - k, z >= k, z < 3, True), (z + k, z + k <= 3, z > 0, False)):
                @pl.when(ok)
                def _():
                    @pl.when(more)
                    def _():
                        self.z_copy(zs, up, False).wait_send()

                    self.y_copy(zs, False).wait_send()
                    for y2 in (y, 1 - y):
                        self.x_copy(zs, y2).wait_send()
                        self.c_copy(zs, y2, self.ywin, 0).wait_send()
                        self.c_copy(zs, y2, self.xgot, 1).wait_send()


def gather_sems(n):
    return [pltpu.SemaphoreType.DMA(s) for s in ((n, 4), (n, 4), (n, 8), (n, 16), (n, 4, 2), (n, 4), (n, 8), (n, 16), (n,))]


def gather_kernel(n, *refs):
    owns, fulls, sems = refs[:n], refs[n:2 * n], refs[2 * n:]
    at = place()
    enter(*at)
    gs = [Gather(i, owns[i], fulls[i], sems, at) for i in range(n)]
    plan = []
    steps = ["begin", ("along_z", 1), ("along_z", 2), ("along_z", 3), ("along_y", 0), ("along_y", 1), ("along_y", 2), ("along_y", 3),
             ("along_x", 0), ("along_x", 1), ("along_x", 2), ("along_x", 3)]
    lag = 4
    slots = {}
    for i in range(n):
        for j, s in enumerate(steps):
            slots.setdefault(i * lag + j, []).append((i, s))
    for t in sorted(slots):
        for i, s in sorted(slots[t], key=lambda e: e[0]):
            if isinstance(s, str):
                getattr(gs[i], s)()
            else:
                getattr(gs[i], s[0])(s[1])
    for g in gs:
        g.finish()
    for g in gs:
        g.drain()


def gather_all(shards):
    n = len(shards)
    return pl.pallas_call(
        functools.partial(gather_kernel, n),
        out_shape=[jax.ShapeDtypeStruct((s.shape[0] * 16, s.shape[1]), s.dtype) for s in shards],
        in_specs=[pl.BlockSpec(memory_space=pl.ANY)] * n,
        out_specs=[pl.BlockSpec(memory_space=pl.ANY)] * n,
        scratch_shapes=gather_sems(n),
        compiler_params=pltpu.CompilerParams(collective_id=1, has_side_effects=True),
        name="gather_weights",
    )(*shards)


class Reduce:
    def __init__(self, index, part, out, bufs, sems, at):
        self.g, self.p, self.out = index, part, out
        self.a, self.cb, self.xb, self.yb, self.zb, self.fb = bufs
        self.sc, self.sx, self.sy, self.sz, self.sf, self.ls = sems
        self.z, self.y, self.c, self.x = at
        self.rows, self.cols = part.shape[-2:]
        u = self.u = self.cols // 8
        x = self.x
        self.ywin = pl.ds(pl.multiple_of(x * 2 * u, 128), 6 * u)
        self.xsend = pl.ds(pl.multiple_of((1 - x) * 6 * u, 128), 2 * u)
        self.xgot = pl.ds(pl.multiple_of(x * 6 * u, 128), 2 * u)

    def send(self, src, dst, sem, to):
        z2, y2, c2, x2 = to
        return pltpu.make_async_remote_copy(
            src_ref=src, dst_ref=dst, send_sem=sem[0], recv_sem=sem[1],
            device_id=(z2 * 4 + y2 * 2 + c2, x2), device_id_type=MESH)

    def c_copy(self):
        return self.send(self.p.at[:, :, 1 - self.c], self.cb, (self.sc.at[self.g, 0], self.sc.at[self.g, 1]), (self.z, self.y, 1 - self.c, self.x))

    def load(self):
        return pltpu.make_async_copy(self.p.at[:, :, self.c], self.a, self.ls.at[self.g])

    def x_copy(self):
        return self.send(self.a.at[:, :, :, self.xsend], self.xb, (self.sx.at[self.g, 0], self.sx.at[self.g, 1]), (self.z, self.y, self.c, 1 - self.x))

    def y_copy(self):
        return self.send(self.a.at[:, 1 - self.y, :, self.ywin], self.yb, (self.sy.at[self.g, 0], self.sy.at[self.g, 1]), (self.z, 1 - self.y, self.c, self.x))

    def z_copy(self, zs, up):
        z2 = self.z + 1 if up else self.z - 1
        slot = zs if up else jnp.where(zs == z2, 4, zs)
        return self.send(self.a.at[zs, self.y, :, self.ywin], self.zb.at[slot], (self.sz.at[self.g, 0, zs], self.sz.at[self.g, 1, slot]), (z2, self.y, self.c, self.x))

    def f_copy(self):
        return self.send(self.a.at[self.z, self.y, :, self.ywin], self.fb, (self.sf.at[self.g, 0], self.sf.at[self.g, 1]), (self.z, self.y, self.c, 1 - self.x))

    def add(self, dst, win, src):
        step = 16

        @pl.loop(0, self.rows, step=step)
        def _(r):
            rr = pl.ds(pl.multiple_of(r, step), step)
            dst[rr, win] = dst[rr, win] + src[rr, :]

    def add_all(self, zs_, ys_, win, src):
        @pl.loop(0, 4)
        def _(zz):
            for yy in ys_:
                self.add(self.a.at[zz, yy], win, src(zz, yy))

    def go(self):
        self.c_copy().start()
        self.load().start()

    def s_c(self):
        self.load().wait()
        self.c_copy().wait_recv()
        self.add_all(4, (0, 1), pl.ds(0, self.cols), lambda zz, yy: self.cb.at[zz, yy])
        self.x_copy().start()

    def s_x(self):
        self.x_copy().wait_recv()
        self.add_all(4, (0, 1), self.xgot, lambda zz, yy: self.xb.at[zz, yy])
        self.y_copy().start()

    def s_y(self):
        self.y_copy().wait_recv()
        self.add_all(4, (self.y,), self.ywin, lambda zz, yy: self.yb.at[zz])

    def await_(self, dst, sem):
        pltpu.make_async_copy(dst, dst, sem).wait()

    def take(self, zs, slot):
        self.await_(self.zb.at[slot], self.sz.at[self.g, 1, slot])
        self.add(self.a.at[zs, self.y], self.ywin, self.zb.at[slot])

    def s_z(self, k):
        z = self.z
        up = 4 - k
        for zs, ok, first, d in ((up, up > z, z == 0, True), (3 - up, 3 - up < z, z == 3, False)):
            @pl.when(ok)
            def _():
                @pl.when(jnp.logical_not(first))
                def _():
                    self.take(zs, zs)

                self.z_copy(zs, d).start()

    def s_own(self):
        @pl.when(self.z > 0)
        def _():
            self.take(self.z, self.z)

        @pl.when(self.z < 3)
        def _():
            self.take(self.z, 4)

        self.f_copy().start()

    def s_f(self):
        u = self.u
        self.f_copy().wait_recv()
        mine = self.a.at[self.z, self.y]
        f32 = jnp.float32
        for xx, solo, both_f, got, got_f in ((0, 0, 0, 6, 4), (1, 6, 2, 0, 0)):
            @pl.when(self.x == xx)
            def _():
                @pl.loop(0, self.rows, step=16)
                def _(r):
                    rr = pl.ds(pl.multiple_of(r, 16), 16)
                    self.out[rr, solo * u:(solo + 2) * u] = mine[rr, solo * u:(solo + 2) * u].astype(f32)
                    self.out[rr, 2 * u:6 * u] = mine[rr, 2 * u:6 * u].astype(f32) + self.fb[rr, both_f * u:(both_f + 4) * u].astype(f32)
                    self.out[rr, got * u:(got + 2) * u] = self.fb[rr, got_f * u:(got_f + 2) * u].astype(f32)

    def drain(self):
        self.c_copy().wait_send()
        self.x_copy().wait_send()
        self.y_copy().wait_send()
        self.f_copy().wait_send()
        for k in (1, 2, 3):
            up = 4 - k
            for zs, ok, d in ((up, up > self.z, True), (3 - up, 3 - up < self.z, False)):
                @pl.when(ok)
                def _():
                    self.z_copy(zs, d).wait_send()


def reduce_bufs(shape):
    r, c = shape
    u = c // 8
    return [pltpu.VMEM(s, jnp.bfloat16) for s in ((4, 2, r, c), (4, 2, r, c), (4, 2, r, 2 * u), (4, r, 6 * u), (5, r, 6 * u), (r, 6 * u))]


def reduce_sems(n):
    return [pltpu.SemaphoreType.DMA(s) for s in ((n, 2), (n, 2), (n, 2), (n, 2, 5), (n, 2), (n,))]


def reduce_kernel(n, lag, *refs):
    parts, outs, bufs, sems = refs[:n], refs[n:2 * n], refs[2 * n:2 * n + 6 * n], refs[8 * n:]
    at = place()
    enter(*at)
    rs = [Reduce(i, parts[i], outs[i], bufs[6 * i:6 * i + 6], sems, at) for i in range(n)]
    steps = [("go",), ("s_c",), ("s_x",), ("s_y",), ("s_z", 1), ("s_z", 2), ("s_z", 3), ("s_own",), ("s_f",)]
    slots = {}
    for i in range(n):
        for j, s in enumerate(steps):
            slots.setdefault(i * lag + j, []).append((i, s))
    for t in sorted(slots):
        for i, s in sorted(slots[t], key=lambda e: e[0]):
            getattr(rs[i], s[0])(*s[1:])
    for r in rs:
        r.drain()


def reduce_all(parts, lag=1):
    n = len(parts)
    parts = [p.reshape(4, 2, 2, p.shape[0] // 16, p.shape[1]) for p in parts]
    return pl.pallas_call(
        functools.partial(reduce_kernel, n, lag),
        out_shape=[jax.ShapeDtypeStruct(p.shape[-2:], jnp.float32) for p in parts],
        in_specs=[pl.BlockSpec(memory_space=pl.ANY)] * n,
        out_specs=[pl.BlockSpec(memory_space=pltpu.VMEM)] * n,
        scratch_shapes=[b for p in parts for b in reduce_bufs(p.shape[-2:])] + reduce_sems(n),
        compiler_params=pltpu.CompilerParams(collective_id=2, has_side_effects=True, vmem_limit_bytes=60 * 2**20),
        name="reduce_grads",
    )(*parts)


def per_device(
    gather_weights,
    reduce_grads,
    hidden_in,
    positions,
    cotangent,
    norm_gain,
    w_query,
    w_key,
    w_value,
    query_gain,
    key_gain,
    w_out,
    mlp_gain,
    w_gate,
    w_up,
    w_down,
):
    seqs_here, block_len, model_width = hidden_in.shape
    head_dim = query_gain.shape[0]
    kv_heads = w_key.shape[1] // head_dim
    q_heads = w_query.shape[1] // head_dim
    groups = q_heads // kv_heads
    ctx_count = lax.axis_size("ctx")
    ctx_rank = lax.axis_index("ctx")
    seq_total = block_len * ctx_count
    row_count = seqs_here * block_len
    scale_val = head_dim ** (-0.5)
    shards = (w_query, w_key, w_value, w_out, w_gate, w_up, w_down)
    full_weights = gather_weights(shards)
    full_query, full_key, full_value, full_out, full_gate, full_up, full_down = full_weights
    residual = hidden_in.astype(jnp.float32).reshape(row_count, model_width)
    scaled_one, normed_one, inverse_one = norm_rows(residual, norm_gain)
    attn_in = scaled_one.astype(jnp.bfloat16)
    query_raw = jnp.dot(attn_in, full_query, preferred_element_type=jnp.float32).reshape(
        row_count, q_heads, head_dim
    )
    key_raw = jnp.dot(attn_in, full_key, preferred_element_type=jnp.float32).reshape(
        row_count, kv_heads, head_dim
    )
    value_bf = jnp.dot(attn_in, full_value, preferred_element_type=jnp.float32).astype(jnp.bfloat16)
    flat_pos = positions.reshape(row_count)
    cosine, sine_tab = rope_tables(flat_pos, head_dim)
    query_scaled, query_normed, query_inverse = norm_rows(query_raw, query_gain)
    query_bf = rotate(query_scaled, cosine, sine_tab).astype(jnp.bfloat16)
    key_scaled, key_normed, key_inverse = norm_rows(key_raw, key_gain)
    key_bf = rotate(key_scaled, cosine, sine_tab).astype(jnp.bfloat16)
    key_flat = key_bf.reshape(seqs_here, block_len, kv_heads * head_dim)
    value_flat = value_bf.reshape(seqs_here, block_len, kv_heads * head_dim)
    keys_all, values_all = (
        lax.all_gather(key_flat, "ctx", axis=1, tiled=True),
        lax.all_gather(value_flat, "ctx", axis=1, tiled=True),
    )
    query_five = query_bf.reshape(seqs_here, block_len, kv_heads, groups, head_dim)
    query_index = ctx_rank * block_len + jnp.arange(block_len, dtype=jnp.int32)
    doc_start = query_index[None, :] - positions

    def block_scores(key_source, block_idx):
        key_block = lax.dynamic_slice_in_dim(key_source, block_idx * block_len, block_len, 1)
        scores = (
            jnp.einsum(
                "sqkgd,spkd->skgqp", query_five, key_block, preferred_element_type=jnp.float32
            )
            * scale_val
        )
        key_index = block_idx * block_len + jnp.arange(block_len, dtype=jnp.int32)
        allowed = (key_index[None, None, :] <= query_index[None, :, None]) & (
            key_index[None, None, :] >= doc_start[:, :, None]
        )
        return (jnp.where(allowed[:, None, None, :, :], scores, -1e30), key_block)

    keys_four = keys_all.reshape(seqs_here, seq_total, kv_heads, head_dim)
    values_four = values_all.reshape(seqs_here, seq_total, kv_heads, head_dim)

    def stats_step(block_idx, carry_stats):
        running_max, running_sum = carry_stats
        scores, key_block = block_scores(keys_four, block_idx)
        new_max = jnp.maximum(running_max, jnp.max(scores, axis=-1))
        running_sum = running_sum * jnp.exp(running_max - new_max) + jnp.sum(
            jnp.exp(scores - new_max[..., None]), axis=-1
        )
        return (new_max, running_sum)

    stat_shape = (seqs_here, kv_heads, groups, block_len)
    row_max, row_sum = lax.fori_loop(
        0,
        ctx_rank + 1,
        stats_step,
        (jnp.full(stat_shape, -1e30, jnp.float32), jnp.zeros(stat_shape, jnp.float32)),
    )

    def output_step(block_idx, accum):
        scores, key_block = block_scores(keys_four, block_idx)
        probs_bf = (jnp.exp(scores - row_max[..., None]) / row_sum[..., None]).astype(jnp.bfloat16)
        value_block = lax.dynamic_slice_in_dim(values_four, block_idx * block_len, block_len, 1)
        return accum + jnp.einsum(
            "skgqp,spkd->sqkgd", probs_bf, value_block, preferred_element_type=jnp.float32
        )

    attn_f32 = lax.fori_loop(
        0,
        ctx_rank + 1,
        output_step,
        jnp.zeros((seqs_here, block_len, kv_heads, groups, head_dim), jnp.float32),
    )
    attn_bf = attn_f32.reshape(row_count, q_heads * head_dim).astype(jnp.bfloat16)
    middle = residual + jnp.dot(attn_bf, full_out, preferred_element_type=jnp.float32)
    scaled_two, normed_two, inverse_two = norm_rows(middle, mlp_gain)
    mlp_in = scaled_two.astype(jnp.bfloat16)
    gate_pre = jnp.dot(mlp_in, full_gate, preferred_element_type=jnp.float32)
    up_pre = jnp.dot(mlp_in, full_up, preferred_element_type=jnp.float32)
    sigmoid_gate = jax.nn.sigmoid(gate_pre)
    silu_gate = gate_pre * sigmoid_gate
    hidden_bf = (silu_gate * up_pre).astype(jnp.bfloat16)
    layer_out = middle + jnp.dot(hidden_bf, full_down, preferred_element_type=jnp.float32)
    output = layer_out.astype(jnp.bfloat16).reshape(seqs_here, block_len, model_width)
    back_weights = full_weights
    keys_back, values_back = (
        lax.all_gather(key_flat, "ctx", axis=1, tiled=True),
        lax.all_gather(value_flat, "ctx", axis=1, tiled=True),
    )
    back_query, back_key, back_value, back_out, back_gate, back_up, back_down = back_weights
    keys_again = keys_back.reshape(seqs_here, seq_total, kv_heads, head_dim)
    values_again = values_back.reshape(seqs_here, seq_total, kv_heads, head_dim)
    grad_rows = cotangent.reshape(row_count, model_width)
    down_grad = back_dot(grad_rows, back_down)
    grad_gate = (
        down_grad * up_pre * sigmoid_gate * (1.0 + gate_pre * (1.0 - sigmoid_gate))
    ).astype(jnp.bfloat16)
    grad_up = (down_grad * silu_gate).astype(jnp.bfloat16)
    grad_mlp_in = back_dot(grad_gate, back_gate) + back_dot(grad_up, back_up)
    grad_norm_two, mlp_gain_terms = norm_back(grad_mlp_in, mlp_gain, normed_two, inverse_two)
    grad_mid = grad_rows.astype(jnp.float32) + grad_norm_two
    grad_proj = grad_mid.astype(jnp.bfloat16)
    grad_attn = back_dot(grad_proj, back_out).astype(jnp.bfloat16)
    grad_five = grad_attn.reshape(seqs_here, block_len, kv_heads, groups, head_dim)
    delta = jnp.einsum("sqkgd,sqkgd->skgq", grad_five.astype(jnp.float32), attn_f32)

    def grad_step(block_idx, carry_grads):
        grad_query, grad_keys, grad_values = carry_grads
        scores, key_block = block_scores(keys_again, block_idx)
        probs = jnp.exp(scores - row_max[..., None]) / row_sum[..., None]
        value_block = lax.dynamic_slice_in_dim(values_again, block_idx * block_len, block_len, 1)
        grad_probs = jnp.einsum(
            "sqkgd,spkd->skgqp", grad_five, value_block, preferred_element_type=jnp.float32
        )
        grad_scores = (probs * (grad_probs - delta[..., None])).astype(jnp.bfloat16)
        grad_query = (
            grad_query
            + jnp.einsum(
                "skgqp,spkd->sqkgd", grad_scores, key_block, preferred_element_type=jnp.float32
            )
            * scale_val
        )
        key_part = (
            jnp.einsum(
                "skgqp,sqkgd->spkd", grad_scores, query_five, preferred_element_type=jnp.float32
            )
            * scale_val
        )
        value_part = jnp.einsum(
            "skgqp,sqkgd->spkd",
            probs.astype(jnp.bfloat16),
            grad_five,
            preferred_element_type=jnp.float32,
        )
        grad_keys = lax.dynamic_update_slice_in_dim(grad_keys, key_part, block_idx * block_len, 1)
        grad_values = lax.dynamic_update_slice_in_dim(
            grad_values, value_part, block_idx * block_len, 1
        )
        return (grad_query, grad_keys, grad_values)

    whole_shape = (seqs_here, seq_total, kv_heads, head_dim)
    grad_query, grad_keys, grad_values = lax.fori_loop(
        0,
        ctx_rank + 1,
        grad_step,
        (
            jnp.zeros((seqs_here, block_len, kv_heads, groups, head_dim), jnp.float32),
            jnp.zeros(whole_shape, jnp.float32),
            jnp.zeros(whole_shape, jnp.float32),
        ),
    )
    key_grad_own, value_grad_own = (
        lax.psum_scatter(
            grad_keys.reshape(seqs_here, seq_total, kv_heads * head_dim).astype(jnp.bfloat16),
            "ctx",
            scatter_dimension=1,
            tiled=True,
        ).astype(jnp.float32),
        lax.psum_scatter(
            grad_values.reshape(seqs_here, seq_total, kv_heads * head_dim).astype(jnp.bfloat16),
            "ctx",
            scatter_dimension=1,
            tiled=True,
        ).astype(jnp.float32),
    )
    key_unrot = rotate_back(key_grad_own.reshape(row_count, kv_heads, head_dim), cosine, sine_tab)
    key_raw_grad, key_gain_terms = norm_back(key_unrot, key_gain, key_normed, key_inverse)
    key_raw_bf = key_raw_grad.reshape(row_count, kv_heads * head_dim).astype(jnp.bfloat16)
    query_unrot = rotate_back(grad_query.reshape(row_count, q_heads, head_dim), cosine, sine_tab)
    query_raw_grad, query_gain_terms = norm_back(
        query_unrot, query_gain, query_normed, query_inverse
    )
    query_raw_bf = query_raw_grad.reshape(row_count, q_heads * head_dim).astype(jnp.bfloat16)
    value_raw_bf = value_grad_own.reshape(row_count, kv_heads * head_dim).astype(jnp.bfloat16)
    grad_attn_in = (
        back_dot(query_raw_bf, back_query)
        + back_dot(key_raw_bf, back_key)
        + back_dot(value_raw_bf, back_value)
    )
    grad_norm_one, norm_gain_terms = norm_back(grad_attn_in, norm_gain, normed_one, inverse_one)
    grad_input = (
        (grad_mid + grad_norm_one).astype(jnp.bfloat16).reshape(seqs_here, block_len, model_width)
    )
    gain_one, gain_query, gain_key, gain_two = lax.psum(
        (
            jnp.sum(norm_gain_terms, axis=0),
            jnp.sum(query_gain_terms, axis=(0, 1)),
            jnp.sum(key_gain_terms, axis=(0, 1)),
            jnp.sum(mlp_gain_terms, axis=0),
        ),
        ("fsdp", "ctx"),
    )
    weight_pairs = (
        (attn_in, query_raw_bf),
        (attn_in, key_raw_bf),
        (attn_in, value_raw_bf),
        (attn_bf, grad_proj),
        (mlp_in, grad_gate),
        (mlp_in, grad_up),
        (hidden_bf, grad_rows),
    )
    partials = tuple(
        weight_term(acts_in, grad_out).astype(jnp.bfloat16) for acts_in, grad_out in weight_pairs
    )
    weight_grads = reduce_grads(partials)
    grad_wq, grad_wk, grad_wv, grad_wo, grad_wg, grad_wu, grad_wd = weight_grads
    return (
        output,
        grad_input,
        gain_one,
        grad_wq,
        grad_wk,
        grad_wv,
        gain_query,
        gain_key,
        grad_wo,
        gain_two,
        grad_wg,
        grad_wu,
        grad_wd,
    )


def gather_plain(shards):
    return tuple(lax.all_gather(shard, "fsdp", axis=0, tiled=True) for shard in shards)


def reduce_plain(partials):
    pieces = tuple(
        lax.psum_scatter(part, "fsdp", scatter_dimension=0, tiled=True) for part in partials
    )
    return tuple(part.astype(jnp.float32) for part in lax.psum(pieces, "ctx"))


def gather_grid(shards):
    order = (1, 2, 0, 3, 4, 5, 6)
    full = gather_all([shards[i] for i in order])
    return tuple(full[order.index(i)] for i in range(7))


def reduce_grid(partials):
    order = (6, 5, 4, 3, 0, 1, 2)
    done = reduce_all([partials[i] for i in order])
    return tuple(done[order.index(i)] for i in range(7))


def is_grid(mesh):
    if dict(mesh.shape) != {"fsdp": 16, "ctx": 2}:
        return False
    for f in range(16):
        for x in range(2):
            device = mesh.devices[f, x]
            if tuple(device.coords) != (x, (f // 2) % 2, f // 4) or device.core_on_chip != f % 2:
                return False
    return True


def solution(mesh):
    in_specs = (
        P("fsdp", "ctx", None),
        P("fsdp", "ctx"),
        P("fsdp", "ctx", None),
        P(),
        P("fsdp", None),
        P("fsdp", None),
        P("fsdp", None),
        P(),
        P(),
        P("fsdp", None),
        P(),
        P("fsdp", None),
        P("fsdp", None),
        P("fsdp", None),
    )
    out_specs = (
        P("fsdp", "ctx", None),
        P("fsdp", "ctx", None),
        P(),
        P("fsdp", None),
        P("fsdp", None),
        P("fsdp", None),
        P(),
        P(),
        P("fsdp", None),
        P(),
        P("fsdp", None),
        P("fsdp", None),
        P("fsdp", None),
    )
    plan = (gather_grid, reduce_grid) if is_grid(mesh) else (gather_plain, reduce_plain)
    return jax.shard_map(
        functools.partial(per_device, *plan), mesh=mesh, in_specs=in_specs, out_specs=out_specs, check_vma=False
    )
```

```python
import jax
import jax.numpy as jnp
from jax import lax
from jax.experimental import pallas as pl
from jax.experimental.pallas import tpu as pltpu
from jax.sharding import PartitionSpec as P

MESH = pl.DeviceIdType.MESH

epsilon = 1e-06
theta_base = 1000000.0
log2e = 1.4426950408889634
bf16, f32 = jnp.bfloat16, jnp.float32
HBM = pl.BlockSpec(memory_space=pl.ANY)
VMEM = pl.BlockSpec(memory_space=pltpu.VMEM)


def place():
    f = lax.axis_index("fsdp")
    return f // 4, (f // 2) % 2, f % 2, lax.axis_index("ctx")


def enter(z, y, c, x, ends=False):
    bar = pltpu.get_barrier_semaphore()

    def hail(z2, y2, c2, x2):
        pl.semaphore_signal(bar, inc=1, device_id=(z2 * 4 + y2 * 2 + c2, x2), device_id_type=MESH)

    hail(z, y, c, 1 - x)
    hail(z, 1 - y, c, x)
    hail(z, y, 1 - c, x)

    @pl.when(z > 0)
    def _():
        hail(z - 1, y, c, x)

    @pl.when(z < 3)
    def _():
        hail(z + 1, y, c, x)

    if ends:
        @pl.when(z % 3 == 0)
        def _():
            hail(3 - z, y, c, x)

    pl.semaphore_wait(bar, 5 if ends else 4 + (z * (3 - z)) // 2)


class Gather:
    def __init__(self, index, own, full, sems, at):
        self.g, self.own, self.full = index, own, full
        self.zr, self.yr, self.xr, self.cr, self.zs, self.ys, self.xs, self.cs, self.ls = sems
        self.z, self.y, self.c, self.x = at
        self.rows, self.cols = own.shape
        unit = self.cols // 8
        x = self.x
        self.ywin = pl.ds(pl.multiple_of(x * 3 * unit, 128), 5 * unit)
        self.xwin = pl.ds(pl.multiple_of(x * 5 * unit, 128), 3 * unit)
        self.xgot = pl.ds(pl.multiple_of((1 - x) * 5 * unit, 128), 3 * unit)
        self.all = pl.ds(0, self.cols)
        self.ends = []

    def part(self, z2, y2, c2, win):
        f2 = z2 * 4 + y2 * 2 + c2
        return self.full.at[pl.ds(pl.multiple_of(f2 * self.rows, 16), self.rows), win]

    def send(self, src, dst, ssem, rsem, to):
        z2, y2, c2, x2 = to
        return pltpu.make_async_remote_copy(
            src_ref=src, dst_ref=dst, send_sem=ssem, recv_sem=rsem,
            device_id=(z2 * 4 + y2 * 2 + c2, x2), device_id_type=MESH)

    def z_copy(self, zs, up, first):
        dst = self.part(zs, self.y, self.c, self.ywin)
        src = self.own.at[:, self.ywin] if first else dst
        z2 = self.z + 1 if up else self.z - 1
        return self.send(src, dst, self.zs.at[self.g, zs, 1 if up else 0], self.zr.at[self.g, zs], (z2, self.y, self.c, self.x))

    def y_copy(self, zs, first):
        dst = self.part(zs, self.y, self.c, self.ywin)
        src = self.own.at[:, self.ywin] if first else dst
        return self.send(src, dst, self.ys.at[self.g, zs], self.yr.at[self.g, zs], (self.z, 1 - self.y, self.c, self.x))

    def x_copy(self, zs, y2):
        dst = self.part(zs, y2, self.c, self.xwin)
        s = zs * 2 + y2
        return self.send(dst, dst, self.xs.at[self.g, s], self.xr.at[self.g, s], (self.z, self.y, self.c, 1 - self.x))

    def c_copy(self, zs, y2, win, piece, first=False):
        dst = self.part(zs, y2, self.c, win)
        src = self.own if first else dst
        s = (zs * 2 + y2) * 2 + piece
        return self.send(src, dst, self.cs.at[self.g, s], self.cr.at[self.g, s], (self.z, self.y, 1 - self.c, self.x))

    def await_(self, dst, sem):
        pltpu.make_async_copy(dst, dst, sem).wait()

    def local(self):
        return pltpu.make_async_copy(self.own, self.part(self.z, self.y, self.c, self.all), self.ls.at[self.g])

    def begin(self):
        z = self.z

        @pl.when(z < 3)
        def _():
            self.z_copy(z, True, True).start()

        @pl.when(z > 0)
        def _():
            self.z_copy(z, False, True).start()

        self.y_copy(z, True).start()
        self.c_copy(z, self.y, self.all, 0, True).start()
        self.local().start()

    def spread(self, zs, up):
        self.await_(self.part(zs, self.y, self.c, self.ywin), self.zr.at[self.g, zs])

        @pl.when(self.z < 3 if up else self.z > 0)
        def _():
            self.z_copy(zs, up, False).start()

        self.y_copy(zs, False).start()
        self.x_copy(zs, self.y).start()
        self.c_copy(zs, self.y, self.ywin, 0).start()

    def along_z(self, k):
        @pl.when(self.z >= k)
        def _():
            self.spread(self.z - k, True)

        @pl.when(self.z + k <= 3)
        def _():
            self.spread(self.z + k, False)

    def over_y(self, zs):
        self.await_(self.part(zs, 1 - self.y, self.c, self.ywin), self.yr.at[self.g, zs])
        self.x_copy(zs, 1 - self.y).start()
        self.c_copy(zs, 1 - self.y, self.ywin, 0).start()

    def along_y(self, k):
        if k == 0:
            self.over_y(self.z)
            return

        @pl.when(self.z >= k)
        def _():
            self.over_y(self.z - k)

        @pl.when(self.z + k <= 3)
        def _():
            self.over_y(self.z + k)

    def over_x(self, zs, y2):
        self.await_(self.part(zs, y2, self.c, self.xgot), self.xr.at[self.g, zs * 2 + y2])
        self.c_copy(zs, y2, self.xgot, 1).start()

    def along_x(self, k):
        if k == 0:
            self.over_x(self.z, 1 - self.y)
            return

        for y2 in (self.y, 1 - self.y):
            @pl.when(self.z >= k)
            def _():
                self.over_x(self.z - k, y2)

            @pl.when(self.z + k <= 3)
            def _():
                self.over_x(self.z + k, y2)

    def finish(self):
        z, y = self.z, self.y
        self.local().wait()
        c = 1 - self.c
        self.await_(self.part(z, y, c, self.all), self.cr.at[self.g, (z * 2 + y) * 2])
        for k in range(0, 4):
            for y2 in ((y, 1 - y) if k else (1 - y,)):
                for zs, ok in ((z - k, z >= k), (z + k, z + k <= 3))[: 2 if k else 1]:
                    @pl.when(ok)
                    def _():
                        s = (zs * 2 + y2) * 2
                        self.await_(self.part(zs, y2, c, self.ywin), self.cr.at[self.g, s])
                        self.await_(self.part(zs, y2, c, self.xgot), self.cr.at[self.g, s + 1])

    def drain(self):
        z, y = self.z, self.y

        @pl.when(z < 3)
        def _():
            self.z_copy(z, True, True).wait_send()

        @pl.when(z > 0)
        def _():
            self.z_copy(z, False, True).wait_send()

        self.y_copy(z, True).wait_send()
        self.c_copy(z, y, self.all, 0, True).wait_send()
        self.x_copy(z, 1 - y).wait_send()
        self.c_copy(z, 1 - y, self.ywin, 0).wait_send()
        self.c_copy(z, 1 - y, self.xgot, 1).wait_send()
        for k in range(1, 4):
            for zs, ok, more, up in ((z - k, z >= k, z < 3, True), (z + k, z + k <= 3, z > 0, False)):
                @pl.when(ok)
                def _():
                    @pl.when(more)
                    def _():
                        self.z_copy(zs, up, False).wait_send()

                    self.y_copy(zs, False).wait_send()
                    for y2 in (y, 1 - y):
                        self.x_copy(zs, y2).wait_send()
                        self.c_copy(zs, y2, self.ywin, 0).wait_send()
                        self.c_copy(zs, y2, self.xgot, 1).wait_send()


def gather_sems(n):
    return [pltpu.SemaphoreType.DMA(s) for s in ((n, 4), (n, 4), (n, 8), (n, 16), (n, 4, 2), (n, 4), (n, 8), (n, 16), (n,))]


def dot_nn(a, b):
    return lax.dot_general(a, b, (((1,), (0,)), ((), ())), preferred_element_type=f32)


def dot_nt(a, b):
    return lax.dot_general(a, b, (((1,), (1,)), ((), ())), preferred_element_type=f32)


def dot_tn(a, b):
    return lax.dot_general(a, b, (((0,), (0,)), ((), ())), preferred_element_type=f32)


def rows_loop(count, step, body):
    @pl.loop(0, count // step)
    def _(i):
        body(pl.multiple_of(i * step, step), step)


class Writes:
    def __init__(self, sem):
        self.sem, self.all, self.open = sem, [], set()

    def start(self, src, dst):
        copy = pltpu.make_async_copy(src, dst, self.sem.at[len(self.all)])
        copy.start()
        self.open.add(len(self.all))
        self.all.append(copy)
        return len(self.all) - 1

    def wait(self, i):
        if i in self.open:
            self.all[i].wait()
            self.open.remove(i)

    def wait_all(self):
        for i in sorted(self.open):
            self.wait(i)


def unit_rows(values):
    inverse = lax.rsqrt(jnp.mean(values * values, axis=-1, keepdims=True) + epsilon)
    return values * inverse, inverse


def turn(u, cos, sin):
    return u * cos + pltpu.roll(u, u.shape[-1] // 2, 1) * sin


def turn_back(u, cos, sin):
    return u * cos - pltpu.roll(u, u.shape[-1] // 2, 1) * sin


def mask_bias(bias, start_ref, rows):
    block = 128

    @pl.loop(0, bias.shape[0] // block)
    def _(i):
        rr = pl.ds(pl.multiple_of(i * block, block), block)
        key = lax.broadcasted_iota(jnp.int32, (block, rows), 0) + i * block
        query = lax.broadcasted_iota(jnp.int32, (block, rows), 1) + rows
        ok = (key >= start_ref[...]) & (key <= query)
        bias[rr, :] = jnp.where(ok, 0.0, -1e30)


class Schedule:
    def __init__(self, gathers, lag):
        steps = [("begin",)] + [("along_z", k) for k in (1, 2, 3)] + [("along_y", k) for k in range(4)] + [("along_x", k) for k in range(4)] + [("finish",)]
        self.slots = {}
        for i, g in enumerate(gathers):
            for j, s in enumerate(steps):
                self.slots.setdefault(i * lag + j, []).append((g, s))
        self.now = 0

    def to(self, slot):
        while self.now <= slot:
            for g, s in self.slots.get(self.now, []):
                getattr(g, s[0])(*s[1:])
            self.now += 1


def forward_kernel(hid, cos, sin, start, norm_gain, query_gain, key_gain, mlp_gain, *refs):
    owns, refs = refs[:7], refs[7:]
    outs, refs = refs[:7], refs[7:]
    (out_o, q_o, k_o, v_o, qraw_o, kraw_o, ain_o, attn_o, lse_o, mid_o, mlp_o, gate_o, up_o, hidden_o), refs = refs[:14], refs[14:]
    fulls, refs = refs[:7], refs[7:]
    (ain, q, k, vt, attn, bias, tmp, mid, stage, ain_sem, out_sem), sems = refs[:11], refs[11:]
    w_q, w_k, w_v, w_o, w_g, w_u, w_d = fulls
    at = place()
    z, y, c, x = at
    rows, width = hid.shape
    hd = cos.shape[1]
    kv = w_k.shape[1] // hd
    qh = w_q.shape[1] // hd
    group = qh // kv
    span = tmp.shape[1]
    first, second = pl.ds(0, rows), pl.ds(rows, rows)
    enter(*at)
    gs = [Gather(i, owns[i], fulls[i], sems, at) for i in range(7)]
    sched = Schedule(gs, 4)
    writes = Writes(out_sem)
    sched.to(0)

    def norm_one(r, n):
        unit, _ = unit_rows(hid[pl.ds(r, n), :].astype(f32))
        ain[pl.ds(pl.multiple_of(r + rows, n), n), :] = (unit * norm_gain[...]).astype(bf16)

    rows_loop(rows, 64, norm_one)
    handed = pltpu.make_async_remote_copy(
        src_ref=ain.at[second, :], dst_ref=ain.at[first, :], send_sem=ain_sem.at[0], recv_sem=ain_sem.at[1],
        device_id=(z * 4 + y * 2 + c, 1 - x), device_id_type=MESH)

    @pl.when(x == 0)
    def _():
        handed.start()
        ain[first, :] = jnp.zeros((rows, width), bf16)

    mask_bias(bias, start, rows)
    sched.to(12)

    def heads(lhs, weight, base, count, gain, into, col):
        tmp[:count, :] = dot_nn(lhs, weight)

        @pl.loop(0, span // hd)
        def _(h):
            cc = pl.ds(pl.multiple_of(h * hd, hd), hd)
            to = pl.ds(pl.multiple_of(col + h * hd, hd), hd)
            for r in range(0, count, 256):
                raw = tmp[r:r + 256, cc]
                stage[r:r + 256, cc] = raw.astype(bf16)
                unit, _ = unit_rows(raw)
                t = slice(base + r, base + r + 256)
                into[r:r + 256, to] = turn(unit * gain[...], cos[t, :], sin[t, :]).astype(bf16)

    last = None
    for b in range(w_q.shape[1] // span):
        if last is not None:
            writes.wait(last)
        heads(ain[second, :], w_q[:, b * span:(b + 1) * span], rows, rows, query_gain, q, b * span)
        last = writes.start(stage.at[first, :], qraw_o.at[:, pl.ds(b * span, span)])
        sched.to(sched.now)
    sched.to(16)

    @pl.when(x == 1)
    def _():
        handed.wait_recv()

    writes.wait(last)
    heads(ain[...], w_k[...], 0, 2 * rows, key_gain, k, 0)
    last = writes.start(stage, kraw_o)
    writes.start(ain, ain_o)
    writes.start(q, q_o)
    writes.start(k, k_o)
    sched.to(20)
    tmp[...] = dot_nn(ain[...], w_v[...])
    writes.wait(last)
    stage[...] = tmp[...].astype(bf16)
    last = writes.start(stage, v_o)

    @pl.loop(0, kv)
    def _(h):
        cc = pl.ds(pl.multiple_of(h * hd, hd), hd)
        vt[cc, :] = tmp[:, cc].astype(bf16).T

    sched.to(sched.now)

    c2 = hd ** (-0.5) * log2e
    for part in range(4):
        @pl.loop(part * kv // 4, (part + 1) * kv // 4)
        def _(h):
            cc = pl.ds(pl.multiple_of(h * hd, hd), hd)
            for g in range(group):
                n = h * group + g
                qc = pl.ds(pl.multiple_of(n * hd, hd), hd)
                p = jnp.exp2(dot_nt(k[:, cc], q[:, qc]) * c2 + bias[...])
                total = jnp.sum(p, axis=0, keepdims=True)
                o = dot_nn(vt[cc, :], p.astype(bf16))
                attn[qc, :] = (o * (1.0 / total)).astype(bf16)
                lse_o[pl.ds(n, 1), :] = jnp.log2(total)

        sched.to(sched.now)
    writes.start(attn, attn_o)
    sched.to(24)
    mid[...] = hid[...].astype(f32) + dot_tn(attn[...], w_o[...])

    for i in range(3):
        gs[i].drain()
        last_w = writes.start(fulls[i], outs[i])
        writes.wait(last_w)
    writes.wait(last)
    blocks = w_g.shape[1] // span
    hidden = [w_q.at[first, pl.ds(0, span)], w_q.at[second, pl.ds(0, span)], w_q.at[first, pl.ds(span, span)]]
    mlp_in = w_q.at[second, pl.ds(span, span)]
    gates = [w_k.at[first, :], w_v.at[first, :], stage.at[first, :]]
    ups = [w_k.at[second, :], w_v.at[second, :], stage.at[second, :]]

    def norm_two(r, n):
        unit, _ = unit_rows(mid[pl.ds(r, n), :])
        mlp_in[pl.ds(r, n), :] = (unit * mlp_gain[...]).astype(bf16)

    rows_loop(rows, 64, norm_two)
    writes.start(mid, mid_o)
    writes.start(mlp_in, mlp_o)
    sched.to(32)
    for j in range(blocks):
        cols = pl.ds(j * span, span)
        tmp[first, :] = dot_nn(mlp_in[...], w_g[:, cols])
        tmp[second, :] = dot_nn(mlp_in[...], w_u[:, cols])

        def act(r, n):
            rr = pl.ds(r, n)
            gate, up = tmp[rr, :], tmp[pl.ds(pl.multiple_of(r + rows, n), n), :]
            hidden[j][rr, :] = (gate * jax.nn.sigmoid(gate) * up).astype(bf16)
            gates[j][rr, :] = gate.astype(bf16)
            ups[j][rr, :] = up.astype(bf16)

        rows_loop(rows, 64, act)
        writes.start(gates[j], gate_o.at[:, cols])
        writes.start(ups[j], up_o.at[:, cols])
        writes.start(hidden[j], hidden_o.at[:, cols])
        sched.to(sched.now)
    for i in (3, 4, 5):
        writes.start(fulls[i], outs[i])
    sched.to(36)
    writes.start(w_d, outs[6])
    total = mid[...]
    for j in range(blocks):
        total = total + dot_nn(hidden[j][...], w_d[j * span:(j + 1) * span, :])
    out_o[...] = total.astype(bf16)
    for g in gs[3:]:
        g.drain()

    @pl.when(x == 0)
    def _():
        handed.wait_send()

    writes.wait_all()


def forward(hid, cos, sin, start, gains, shards):
    rows, width = hid.shape
    hd = cos.shape[1]
    fulls = [(s.shape[0] * 16, s.shape[1]) for s in shards]
    heads, keys, ff = shards[0].shape[1], shards[1].shape[1], shards[4].shape[1]
    shape = jax.ShapeDtypeStruct
    vm = pltpu.VMEM
    outs = [shape(s, bf16) for s in fulls] + [
        shape((rows, width), bf16), shape((rows, heads), bf16), shape((2 * rows, keys), bf16), shape((2 * rows, keys), bf16),
        shape((rows, heads), bf16), shape((2 * rows, keys), bf16), shape((2 * rows, width), bf16), shape((heads, rows), bf16),
        shape((heads // hd, rows), f32), shape((rows, width), f32), shape((rows, width), bf16),
        shape((rows, ff), bf16), shape((rows, ff), bf16), shape((rows, ff), bf16)]
    specs = [HBM] * 7 + [VMEM if i in (0, 8) else HBM for i in range(14)]
    return pl.pallas_call(
        forward_kernel,
        out_shape=outs,
        in_specs=[VMEM] * 8 + [HBM] * 7,
        out_specs=specs,
        scratch_shapes=[vm(s, bf16) for s in fulls] + [
            vm((2 * rows, width), bf16), vm((rows, heads), bf16), vm((2 * rows, keys), bf16), vm((keys, 2 * rows), bf16),
            vm((heads, rows), bf16), vm((2 * rows, rows), f32), vm((2 * rows, keys), f32), vm((rows, width), f32),
            vm((2 * rows, keys), bf16), pltpu.SemaphoreType.DMA((2,)), pltpu.SemaphoreType.DMA((32,))] + gather_sems(7),
        compiler_params=pltpu.CompilerParams(collective_id=1, has_side_effects=True, vmem_limit_bytes=62 * 2**20),
        name="forward_gather",
    )(hid, cos, sin, start, *gains, *shards)


class Chunk:
    def __init__(self, index, bufs, sems, at, out):
        self.i, self.out = index, out
        ring = [index % b.shape[0] for b in bufs]
        self.g, self.cb, self.xb, self.yb, self.zb, self.fb, self.st = [b.at[r] for b, r in zip(bufs, ring)]
        self.sc, self.sx, self.sy, self.zs, self.zr, self.sf, self.so = [s.at[index] for s in sems]
        self.z, self.y, self.c, self.x = at
        x = self.x
        part = self.part = self.g.shape[3] // 4
        self.ywin = pl.ds(pl.multiple_of(x * part, 16), 3 * part)
        self.xsend = pl.ds(pl.multiple_of((1 - x) * 3 * part, 16), part)
        self.xgot = pl.ds(pl.multiple_of(x * 3 * part, 16), part)

    def send(self, src, dst, ssem, rsem, z2, y2, c2, x2):
        return pltpu.make_async_remote_copy(
            src_ref=src, dst_ref=dst, send_sem=ssem, recv_sem=rsem,
            device_id=(z2 * 4 + y2 * 2 + c2, x2), device_id_type=MESH)

    def c_copy(self):
        return self.send(self.g.at[:, :, 1 - self.c], self.cb, self.sc.at[0], self.sc.at[1], self.z, self.y, 1 - self.c, self.x)

    def x_copy(self):
        return self.send(self.g.at[:, :, self.c, self.xsend], self.xb, self.sx.at[0], self.sx.at[1], self.z, self.y, self.c, 1 - self.x)

    def y_copy(self):
        return self.send(self.g.at[:, 1 - self.y, self.c, self.ywin], self.yb, self.sy.at[0], self.sy.at[1], self.z, 1 - self.y, self.c, self.x)

    def z_copy(self, here, to, up):
        there = here + 1 if up else here - 1
        slot = 4 if to == there and not up else to
        return self.send(self.g.at[to, self.y, self.c, self.ywin], self.zb.at[slot], self.zs.at[to], self.zr.at[slot], there, self.y, self.c, self.x)

    def f_copy(self):
        return self.send(self.g.at[self.z, self.y, self.c, self.ywin], self.fb, self.sf.at[0], self.sf.at[1], self.z, self.y, self.c, 1 - self.x)

    def o_copy(self):
        return pltpu.make_async_copy(self.st, self.out, self.so)

    def add(self, zz, yy, win, src):
        dst = self.g.at[zz, yy, self.c, win]
        dst[...] = dst[...] + src[...]

    def go(self):
        self.c_copy().start()

    def over_c(self):
        self.c_copy().wait_recv()

        @pl.loop(0, 4)
        def _(zz):
            for yy in (0, 1):
                self.add(zz, yy, slice(None), self.cb.at[zz, yy])

        self.x_copy().start()

    def over_x(self):
        self.x_copy().wait_recv()

        @pl.loop(0, 4)
        def _(zz):
            for yy in (0, 1):
                self.add(zz, yy, self.xgot, self.xb.at[zz, yy])

        self.y_copy().start()

    def over_y(self):
        self.y_copy().wait_recv()

        @pl.loop(0, 4)
        def _(zz):
            self.add(zz, self.y, self.ywin, self.yb.at[zz])

    def take(self, zz, slot):
        pltpu.make_async_copy(self.zb.at[slot], self.zb.at[slot], self.zr.at[slot]).wait()
        self.add(zz, self.y, self.ywin, self.zb.at[slot])

    def over_z(self, k):
        for up in (True, False):
            here = k if up else 3 - k

            @pl.when(self.z == here)
            def _():
                for to in (range(3, here, -1) if up else range(here)):
                    if k:
                        self.take(to, to)
                    self.z_copy(here, to, up).start()
                if k:
                    self.take(here, here if up else 4)

    def hand(self):
        self.f_copy().start()

    def finish(self, before):
        p = self.part
        self.f_copy().wait_recv()
        if before is not None:
            before.o_copy().wait()
        mine = self.g.at[self.z, self.y, self.c]
        for xx, solo, shared, got, other in ((0, 0, 0, 3, 2), (1, 3, 1, 0, 0)):
            @pl.when(self.x == xx)
            def _():
                self.st[solo * p:(solo + 1) * p, :] = mine[solo * p:(solo + 1) * p, :].astype(f32)
                self.st[p:3 * p, :] = mine[p:3 * p, :].astype(f32) + self.fb[shared * p:(shared + 2) * p, :].astype(f32)
                self.st[got * p:(got + 1) * p, :] = self.fb[other * p:(other + 1) * p, :].astype(f32)

        self.o_copy().start()
        self.c_copy().wait_send()
        self.x_copy().wait_send()
        self.y_copy().wait_send()
        self.f_copy().wait_send()
        for here in range(4):
            @pl.when(self.z == here)
            def _():
                for to in range(4):
                    if to != here:
                        self.z_copy(here, to, to > here).wait_send()


def chunk_bufs(rows, cols):
    part = rows // 4
    sizes = ((10, 4, 2, 2, rows, cols), (4, 4, 2, rows, cols), (4, 4, 2, part, cols), (4, 4, 3 * part, cols), (6, 5, 3 * part, cols), (4, 3 * part, cols))
    return [pltpu.VMEM(s, bf16) for s in sizes] + [pltpu.VMEM((2, rows, cols), f32)]


def chunk_sems(n):
    return [pltpu.SemaphoreType.DMA(s) for s in ((n, 2), (n, 2), (n, 2), (n, 4), (n, 5), (n, 2), (n,))]


class Totals:
    def __init__(self, mine, got, sem, at):
        self.mine, self.got, self.sem = mine, got, sem
        z, y, c, x = at
        self.to = [(z, y, 1 - c, x), (z, y, c, 1 - x), (z, 1 - y, c, x), (z + 1 - 2 * (z % 2), y, c, x), (3 - z, y, c, x)]

    def copy(self, s):
        z, y, c, x = self.to[s]
        return pltpu.make_async_remote_copy(
            src_ref=self.mine.at[s], dst_ref=self.got.at[s], send_sem=self.sem.at[s, 0], recv_sem=self.sem.at[s, 1],
            device_id=(z * 4 + y * 2 + c, x), device_id_type=MESH)

    def step(self, s):
        if s > 0:
            self.copy(s - 1).wait()
            self.mine[s] = self.mine[s - 1] + self.got[s - 1]
        if s < 5:
            self.copy(s).start()


def backward_kernel(cot, cos, sin, start, norm_gain, query_gain, key_gain, mlp_gain, lse, *refs):
    full, refs = refs[:7], refs[7:]
    (hid_i, q_i, k_i, v_i, qraw_i, kraw_i, ain_i, attn_i, mid_i, mlp_i, gate_i, up_i, hidden_i), refs = refs[:13], refs[13:]
    grads, refs = refs[:7], refs[7:]
    (gin_o, norm_o, query_o, key_o, mlp_o), refs = refs[:5], refs[5:]
    (hidden, mlp, ggate, gup, mid, acc, gproj, attn, q, k, v, qraw, kraw, ain, dk, dv, kt, bias, wbuf, earlier, sum_one, sum_two, sum_q, sum_k,
     gain_mine, gain_got, gain_sem, load_sem, w_sem, early_sem), refs = refs[:30], refs[30:]
    bufs, sems = refs[:7], refs[7:]
    at = place()
    z, y, c, x = at
    rows, width = cot.shape
    hd = cos.shape[1]
    kv, qh = k.shape[1] // hd, q.shape[1] // hd
    group = qh // kv
    span = wbuf.shape[1]
    ff = ggate.shape[1]
    cols = bufs[0].shape[-1]
    first, second = pl.ds(0, rows), pl.ds(rows, rows)
    scale = hd ** (-0.5)
    enter(*at, True)

    loads = Writes(load_sem)
    hidden_l = loads.start(hidden_i, hidden)
    blocks = [full[6].at[pl.ds(j * span, span), :] for j in range(ff // span)]
    for j in range(ff // span):
        blocks += [full[4].at[:, pl.ds(j * span, span)], full[5].at[:, pl.ds(j * span, span)]]
    blocks += [full[3].at[pl.ds(j * span, span), :] for j in range(qh * hd // span)]
    blocks += [full[1], full[2]] + [full[0].at[:, pl.ds(j * span, span)] for j in range(qh * hd // span)]

    def fetch(n):
        return pltpu.make_async_copy(blocks[n], wbuf.at[n % 2], w_sem.at[n % 2])

    def weight(n):
        fetch(n).wait()
        return wbuf[n % 2]

    def used(n):
        if n + 2 < len(blocks):
            fetch(n + 2).start()

    fetch(0).start()
    fetch(1).start()
    gate_l = loads.start(gate_i, ggate)
    up_l = loads.start(up_i, gup)
    mlp_l, mid_l, attn_l = loads.start(mlp_i, mlp), loads.start(mid_i, mid), loads.start(attn_i, attn)
    head_l = [loads.start(a, b) for a, b in ((q_i, q), (k_i, k), (v_i, v), (qraw_i, qraw), (kraw_i, kraw))]
    ain_l = loads.start(ain_i, ain)

    todo = []

    def put(val, spot, subs, shards_from):
        size = bufs[0].shape[4]
        for f in range(val.shape[0] // (size * subs)):
            for s in range(subs):
                owner = shards_from + f
                lo = (f * subs + s) * size
                bufs[0][(spot + s) % bufs[0].shape[0], owner // 4, owner // 2 % 2, owner % 2] = val[lo:lo + size, :].astype(bf16)

    def make_down(j):
        def run(spot):
            loads.wait(hidden_l)
            wide = hidden.shape[1] // 4
            for b in range(4):
                put(dot_tn(hidden[:, b * wide:(b + 1) * wide], cot[:, j * cols:(j + 1) * cols]), spot, wide // 256, b * 4)
        return run

    def make_out(j):
        def run(spot):
            loads.wait(attn_l)
            tall = attn.shape[0] // 4
            for b in range(4):
                put(dot_nn(attn[b * tall:(b + 1) * tall, :], gproj[:, j * cols:(j + 1) * cols]), spot, tall // 256, b * 4)
        return run

    def make(lhs, rhs, j):
        def run(spot):
            put(dot_tn(lhs(), rhs[:, j * cols:(j + 1) * cols]), spot, 1, 0)
        return run

    def mlp_all():
        loads.wait(mlp_l)
        return mlp[...]

    def ain_own():
        loads.wait(ain_l)
        return ain[second, :]

    def ain_all():
        loads.wait(ain_l)
        return ain[...]

    def add_weight(w, subs, maker, count):
        for j in range(count):
            for s in range(subs):
                out = grads[w].at[pl.ds(s * 64, 64), pl.ds(j * cols, cols)]
                todo.append((maker(j) if s == 0 else None, out))

    add_weight(6, hidden.shape[1] // (64 * 16), make_down, width // cols)
    add_weight(4, 1, lambda j: make(mlp_all, ggate, j), ff // cols)
    add_weight(5, 1, lambda j: make(mlp_all, gup, j), ff // cols)
    add_weight(3, attn.shape[0] // (64 * 16), make_out, width // cols)
    add_weight(0, 1, lambda j: make(ain_own, q, j), qh * hd // cols)
    add_weight(1, 1, lambda j: make(ain_all, k, j), kv * hd // cols)
    add_weight(2, 1, lambda j: make(ain_all, v, j), kv * hd // cols)
    chunks = [Chunk(i, bufs, sems, at, out) for i, (_, out) in enumerate(todo)]
    total = len(chunks)

    def slot(t):
        def has(d):
            return 0 <= t - d < total

        if has(0):
            if todo[t][0] is not None:
                todo[t][0](t)
            chunks[t].go()
        if has(1):
            chunks[t - 1].over_c()
        if has(2):
            chunks[t - 2].over_x()
        if has(3):
            chunks[t - 3].over_y()
            chunks[t - 3].over_z(0)
        for d in (4, 5, 6):
            if has(d):
                chunks[t - d].over_z(d - 3)
        if has(6):
            chunks[t - 6].hand()
        if has(7):
            chunks[t - 7].finish(chunks[t - 9] if t >= 9 else None)

    nb = ff // span

    def piece_down(j):
        acc[...] = dot_nt(cot[...], weight(j))
        used(j)
        loads.wait(gate_l)
        loads.wait(up_l)
        cc = slice(j * span, (j + 1) * span)

        def act(r, n):
            rr = pl.ds(r, n)
            gate, up, grad = ggate[rr, cc].astype(f32), gup[rr, cc].astype(f32), acc[rr, :]
            sig = jax.nn.sigmoid(gate)
            ggate[rr, cc] = (grad * up * sig * (1.0 + gate * (1.0 - sig))).astype(bf16)
            gup[rr, cc] = (grad * (gate * sig)).astype(bf16)

        rows_loop(rows, 64, act)

    def piece_mlp(j):
        n = nb + 2 * j
        cc = slice(j * span, (j + 1) * span)
        one = dot_nt(ggate[:, cc], weight(n))
        used(n)
        acc[...] = one if j == 0 else acc[...] + one
        acc[...] += dot_nt(gup[:, cc], weight(n + 1))
        used(n + 1)

    def fold(into, terms):
        into[...] += jnp.sum(terms.reshape(terms.shape[0] // 8, 8, terms.shape[1]), axis=0)

    def norm_back(grad, unit, inverse, gain):
        scaled = grad * gain
        return inverse * (scaled - unit * jnp.mean(scaled * unit, axis=-1, keepdims=True))

    def piece_mid():
        loads.wait(mid_l)
        sum_two[...] = jnp.zeros_like(sum_two)

        def body(r, n):
            rr = pl.ds(r, n)
            unit, inverse = unit_rows(mid[rr, :])
            grad = acc[rr, :]
            fold(sum_two, grad * unit)
            out = cot[rr, :].astype(f32) + norm_back(grad, unit, inverse, mlp_gain[...])
            mid[rr, :] = out
            gproj[rr, :] = out.astype(bf16)

        rows_loop(rows, 64, body)

    at_out = 3 * nb
    n_out = qh * hd // span

    def piece_attn_grad():
        for j in range(n_out):
            hidden[:, j * span:(j + 1) * span] = dot_nt(gproj[...], weight(at_out + j)).astype(bf16)
            used(at_out + j)
        mask_bias(bias, start, rows)
        sum_q[...] = jnp.zeros_like(sum_q)
        sum_k[...] = jnp.zeros_like(sum_k)
        loads.wait(attn_l)
        for n in head_l:
            loads.wait(n)

    c2 = scale * log2e
    tile = rows // 2

    def piece_head(h):
        cc = slice(h * hd, (h + 1) * hd)
        kt[...] = k[:, cc].T
        dk[...] = jnp.zeros_like(dk)
        dv[...] = jnp.zeros_like(dv)

        @pl.loop(0, group)
        def _(g):
            n = h * group + g
            qc = pl.ds(pl.multiple_of(n * hd, hd), hd)
            delta = jnp.sum(attn[qc, :].astype(f32) * hidden[:, qc].T.astype(f32), axis=0, keepdims=True)
            shift = lse[pl.ds(n, 1), :]
            for i in range(2):
                rs = slice(i * tile, (i + 1) * tile)
                kk = rows + (i + 1) * tile
                query, grad = q[rs, qc], hidden[rs, qc]
                p = jnp.exp2(dot_nt(k[:kk, cc], query) * c2 + (bias[:kk, rs] - shift[:, rs]))
                gp = dot_nt(v[:kk, cc], grad)
                ds = (p * (gp - delta[:, rs])).astype(bf16)
                dv[:kk, :] += dot_nn(p.astype(bf16), grad)
                dk[:kk, :] += dot_nn(ds, query)
                dq = dot_nn(kt[:, :kk], ds).T * scale
                unit, inverse = unit_rows(qraw[rs, qc].astype(f32))
                t = slice(rows + i * tile, rows + (i + 1) * tile)
                back = turn_back(dq, cos[t, :], sin[t, :])
                fold(sum_q, back * unit)
                q[rs, qc] = norm_back(back, unit, inverse, query_gain[...]).astype(bf16)

        for r in range(0, 2 * rows, tile):
            rr = slice(r, r + tile)
            unit, inverse = unit_rows(kraw[rr, cc].astype(f32))
            back = turn_back(dk[rr, :] * scale, cos[rr, :], sin[rr, :])
            fold(sum_k, back * unit)
            k[rr, cc] = norm_back(back, unit, inverse, key_gain[...]).astype(bf16)
            v[rr, cc] = dv[rr, :].astype(bf16)

    at_kv = at_out + n_out
    handed = pltpu.make_async_remote_copy(
        src_ref=gproj, dst_ref=earlier, send_sem=early_sem.at[0], recv_sem=early_sem.at[1],
        device_id=(z * 4 + y * 2 + c, 1 - x), device_id_type=MESH)

    def piece_queries(j):
        acc[...] += dot_nt(q[:, j * span:(j + 1) * span], weight(at_kv + 2 + j))
        used(at_kv + 2 + j)

    x_in, x_out = mlp, ggate.at[:, pl.ds(0, span)]
    late = []

    def piece_last():
        @pl.when(x == 0)
        def _():
            handed.wait_recv()

            def more(r, n):
                rr = pl.ds(r, n)
                acc[rr, :] += earlier[rr, :].astype(f32)

            rows_loop(rows, 64, more)

        loads.wait(late[0])
        sum_one[...] = jnp.zeros_like(sum_one)

        def body(r, n):
            rr = pl.ds(r, n)
            unit, inverse = unit_rows(x_in[rr, :].astype(f32))
            grad = acc[rr, :]
            fold(sum_one, grad * unit)
            x_out[rr, :] = (mid[rr, :] + norm_back(grad, unit, inverse, norm_gain[...])).astype(bf16)

        rows_loop(rows, 64, body)
        late.append(loads.start(x_out, gin_o))
        gain_mine[0] = jnp.zeros_like(gain_mine[0])
        gain_mine[0, 0:1, :] = jnp.sum(sum_one[...], axis=0, keepdims=True)
        gain_mine[0, 1:2, :] = jnp.sum(sum_two[...], axis=0, keepdims=True)
        gain_mine[0, 2:3, 0:hd] = jnp.sum(sum_q[...], axis=0, keepdims=True)
        gain_mine[0, 3:4, 0:hd] = jnp.sum(sum_k[...], axis=0, keepdims=True)

    totals = Totals(gain_mine, gain_got, gain_sem, at)
    plan = {}

    def place_at(t, f, *args):
        plan.setdefault(t, []).append((f, args))

    for j in range(nb):
        place_at(j, piece_down, j)
        place_at(nb + j, piece_mlp, j)
    t = 2 * nb
    place_at(t, piece_mid)
    place_at(t + 1, piece_attn_grad)
    t += 2
    for h in range(kv):
        place_at(t + h, piece_head, h)
    t += kv

    def piece_both():
        w_k, w_v = weight(at_kv), weight(at_kv + 1)
        acc[...] = dot_nt(k[second, :], w_k) + dot_nt(v[second, :], w_v)

        @pl.when(x == 1)
        def _():
            gproj[...] = (dot_nt(k[first, :], w_k) + dot_nt(v[first, :], w_v)).astype(bf16)
            handed.start()

        used(at_kv)
        used(at_kv + 1)

    t = max(t, 21)
    place_at(t, piece_both)
    for j in range(n_out):
        place_at(t + 1 + j, piece_queries, j)
    t += 1 + n_out
    place_at(t, piece_last)
    for s in range(6):
        place_at(t + 1 + s, totals.step, s)
    for t in range(total + 8):
        slot(t)
        if t == 18:
            late.append(loads.start(hid_i, x_in))
        for f, args in plan.get(t, []):
            f(*args)
    for ch in chunks[-2:]:
        ch.o_copy().wait()

    @pl.when(x == 1)
    def _():
        handed.wait_send()

    loads.wait_all()
    norm_o[...] = gain_mine[5, 0:1, :]
    mlp_o[...] = gain_mine[5, 1:2, :]
    query_o[...] = gain_mine[5, 2:3, 0:hd]
    key_o[...] = gain_mine[5, 3:4, 0:hd]


def backward(hid, cot, cos, sin, start, gains, saved, shards):
    rows, width = hid.shape
    hd = cos.shape[1]
    full = saved[:7]
    q, k, v, qraw, kraw, ain, attn, lse, mid, mlp, gate, up, hidden = saved[8:]
    shape, vm, dma = jax.ShapeDtypeStruct, pltpu.VMEM, pltpu.SemaphoreType.DMA
    heads, keys, ff = q.shape[1], k.shape[1], gate.shape[1]
    span = keys
    outs = [shape(s.shape, f32) for s in shards] + [
        shape((rows, width), bf16), shape((1, width), f32), shape((1, hd), f32), shape((1, hd), f32), shape((1, width), f32)]
    n = sum(s.shape[0] // 64 * (s.shape[1] // 512) for s in shards)
    return pl.pallas_call(
        backward_kernel,
        out_shape=outs,
        in_specs=[VMEM] * 9 + [HBM] * 20,
        out_specs=[HBM] * 8 + [VMEM] * 4,
        scratch_shapes=[
            vm((rows, ff), bf16), vm((rows, width), bf16), vm((rows, ff), bf16), vm((rows, ff), bf16), vm((rows, width), f32), vm((rows, width), f32),
            vm((rows, width), bf16), vm((heads, rows), bf16), vm((rows, heads), bf16), vm((2 * rows, keys), bf16), vm((2 * rows, keys), bf16),
            vm((rows, heads), bf16), vm((2 * rows, keys), bf16), vm((2 * rows, width), bf16), vm((2 * rows, hd), f32), vm((2 * rows, hd), f32),
            vm((hd, 2 * rows), bf16), vm((2 * rows, rows), f32), vm((2, span, span), bf16), vm((rows, width), bf16),
            vm((8, width), f32), vm((8, width), f32), vm((8, hd), f32), vm((8, hd), f32), vm((6, 8, width), f32), vm((5, 8, width), f32),
            dma((5, 2)), dma((24,)), dma((2,)), dma((2,))] + chunk_bufs(64, 512) + chunk_sems(n),
        compiler_params=pltpu.CompilerParams(collective_id=2, has_side_effects=True, vmem_limit_bytes=62 * 2**20),
        name="backward_reduce",
    )(cot, cos, sin, start, *gains, lse, *full, hid, q, k, v, qraw, kraw, ain, attn, mid, mlp, gate, up, hidden)


def as_sent(shard):

    def short(part):
        return part.astype(jnp.bfloat16) if part.dtype == jnp.float32 else part

    return jax.tree.map(short, shard)


def norm_rows(values, gain_vec):
    inverse = lax.rsqrt(jnp.mean(values * values, axis=-1, keepdims=True) + epsilon)
    normed = values * inverse
    return (normed * gain_vec, normed, inverse)


def norm_back(grad_out, gain_vec, normed, inverse):
    scaled = grad_out * gain_vec
    grad_in = inverse * (scaled - normed * jnp.mean(scaled * normed, axis=-1, keepdims=True))
    return (grad_in, grad_out * normed)


def rope_tables(positions, head_dim):
    frequency = theta_base ** (-jnp.arange(0, head_dim, 2).astype(jnp.float32) / head_dim)
    angles = positions.astype(jnp.float32)[:, None] * frequency[None, :]
    angles = jnp.concatenate([angles, angles], axis=-1)
    return (jnp.cos(angles), jnp.sin(angles))


def rotate(values, cosine, sine_tab):
    half_dim = values.shape[-1] // 2
    turned = jnp.concatenate([-values[..., half_dim:], values[..., :half_dim]], axis=-1)
    return values * cosine[:, None, :] + turned * sine_tab[:, None, :]


def rotate_back(grad_out, cosine, sine_tab):
    half_dim = grad_out.shape[-1] // 2
    weighted = grad_out * sine_tab[:, None, :]
    turned = jnp.concatenate([weighted[..., half_dim:], -weighted[..., :half_dim]], axis=-1)
    return grad_out * cosine[:, None, :] + turned


def back_dot(grad_rows, weight):
    return lax.dot_general(
        grad_rows, weight, (((1,), (1,)), ((), ())), preferred_element_type=jnp.float32
    )


def weight_term(acts_in, grad_out):
    return lax.dot_general(
        acts_in, grad_out, (((0,), (0,)), ((), ())), preferred_element_type=jnp.float32
    )


def per_device(
    hidden_in,
    positions,
    cotangent,
    norm_gain,
    w_query,
    w_key,
    w_value,
    query_gain,
    key_gain,
    w_out,
    mlp_gain,
    w_gate,
    w_up,
    w_down,
):
    seqs_here, block_len, model_width = hidden_in.shape
    head_dim = query_gain.shape[0]
    kv_heads = w_key.shape[1] // head_dim
    q_heads = w_query.shape[1] // head_dim
    groups = q_heads // kv_heads
    ctx_count = lax.axis_size("ctx")
    ctx_rank = lax.axis_index("ctx")
    seq_total = block_len * ctx_count
    row_count = seqs_here * block_len
    scale_val = head_dim ** (-0.5)
    shards = (w_query, w_key, w_value, w_out, w_gate, w_up, w_down)
    full_weights = (
        lax.all_gather(shards[0], "fsdp", axis=0, tiled=True),
        lax.all_gather(shards[1], "fsdp", axis=0, tiled=True),
        lax.all_gather(shards[2], "fsdp", axis=0, tiled=True),
        lax.all_gather(shards[3], "fsdp", axis=0, tiled=True),
        lax.all_gather(shards[4], "fsdp", axis=0, tiled=True),
        lax.all_gather(shards[5], "fsdp", axis=0, tiled=True),
        lax.all_gather(shards[6], "fsdp", axis=0, tiled=True),
    )
    full_query, full_key, full_value, full_out, full_gate, full_up, full_down = full_weights
    residual = hidden_in.astype(jnp.float32).reshape(row_count, model_width)
    scaled_one, normed_one, inverse_one = norm_rows(residual, norm_gain)
    attn_in = scaled_one.astype(jnp.bfloat16)
    query_raw = jnp.dot(attn_in, full_query, preferred_element_type=jnp.float32).reshape(
        row_count, q_heads, head_dim
    )
    key_raw = jnp.dot(attn_in, full_key, preferred_element_type=jnp.float32).reshape(
        row_count, kv_heads, head_dim
    )
    value_bf = jnp.dot(attn_in, full_value, preferred_element_type=jnp.float32).astype(jnp.bfloat16)
    flat_pos = positions.reshape(row_count)
    cosine, sine_tab = rope_tables(flat_pos, head_dim)
    query_scaled, query_normed, query_inverse = norm_rows(query_raw, query_gain)
    query_bf = rotate(query_scaled, cosine, sine_tab).astype(jnp.bfloat16)
    key_scaled, key_normed, key_inverse = norm_rows(key_raw, key_gain)
    key_bf = rotate(key_scaled, cosine, sine_tab).astype(jnp.bfloat16)
    key_flat = key_bf.reshape(seqs_here, block_len, kv_heads * head_dim)
    value_flat = value_bf.reshape(seqs_here, block_len, kv_heads * head_dim)
    keys_all, values_all = (
        lax.all_gather(key_flat, "ctx", axis=1, tiled=True),
        lax.all_gather(value_flat, "ctx", axis=1, tiled=True),
    )
    query_five = query_bf.reshape(seqs_here, block_len, kv_heads, groups, head_dim)
    query_index = ctx_rank * block_len + jnp.arange(block_len, dtype=jnp.int32)
    doc_start = query_index[None, :] - positions

    def block_scores(key_source, block_idx):
        key_block = lax.dynamic_slice_in_dim(key_source, block_idx * block_len, block_len, 1)
        scores = (
            jnp.einsum(
                "sqkgd,spkd->skgqp", query_five, key_block, preferred_element_type=jnp.float32
            )
            * scale_val
        )
        key_index = block_idx * block_len + jnp.arange(block_len, dtype=jnp.int32)
        allowed = (key_index[None, None, :] <= query_index[None, :, None]) & (
            key_index[None, None, :] >= doc_start[:, :, None]
        )
        return (jnp.where(allowed[:, None, None, :, :], scores, -1e30), key_block)

    keys_four = keys_all.reshape(seqs_here, seq_total, kv_heads, head_dim)
    values_four = values_all.reshape(seqs_here, seq_total, kv_heads, head_dim)

    def stats_step(block_idx, carry_stats):
        running_max, running_sum = carry_stats
        scores, key_block = block_scores(keys_four, block_idx)
        new_max = jnp.maximum(running_max, jnp.max(scores, axis=-1))
        running_sum = running_sum * jnp.exp(running_max - new_max) + jnp.sum(
            jnp.exp(scores - new_max[..., None]), axis=-1
        )
        return (new_max, running_sum)

    stat_shape = (seqs_here, kv_heads, groups, block_len)
    row_max, row_sum = lax.fori_loop(
        0,
        ctx_rank + 1,
        stats_step,
        (jnp.full(stat_shape, -1e30, jnp.float32), jnp.zeros(stat_shape, jnp.float32)),
    )

    def output_step(block_idx, accum):
        scores, key_block = block_scores(keys_four, block_idx)
        probs_bf = (jnp.exp(scores - row_max[..., None]) / row_sum[..., None]).astype(jnp.bfloat16)
        value_block = lax.dynamic_slice_in_dim(values_four, block_idx * block_len, block_len, 1)
        return accum + jnp.einsum(
            "skgqp,spkd->sqkgd", probs_bf, value_block, preferred_element_type=jnp.float32
        )

    attn_f32 = lax.fori_loop(
        0,
        ctx_rank + 1,
        output_step,
        jnp.zeros((seqs_here, block_len, kv_heads, groups, head_dim), jnp.float32),
    )
    attn_bf = attn_f32.reshape(row_count, q_heads * head_dim).astype(jnp.bfloat16)
    middle = residual + jnp.dot(attn_bf, full_out, preferred_element_type=jnp.float32)
    scaled_two, normed_two, inverse_two = norm_rows(middle, mlp_gain)
    mlp_in = scaled_two.astype(jnp.bfloat16)
    gate_pre = jnp.dot(mlp_in, full_gate, preferred_element_type=jnp.float32)
    up_pre = jnp.dot(mlp_in, full_up, preferred_element_type=jnp.float32)
    sigmoid_gate = jax.nn.sigmoid(gate_pre)
    silu_gate = gate_pre * sigmoid_gate
    hidden_bf = (silu_gate * up_pre).astype(jnp.bfloat16)
    layer_out = middle + jnp.dot(hidden_bf, full_down, preferred_element_type=jnp.float32)
    output = layer_out.astype(jnp.bfloat16).reshape(seqs_here, block_len, model_width)
    back_weights = full_weights
    keys_back, values_back = (
        lax.all_gather(key_flat, "ctx", axis=1, tiled=True),
        lax.all_gather(value_flat, "ctx", axis=1, tiled=True),
    )
    back_query, back_key, back_value, back_out, back_gate, back_up, back_down = back_weights
    keys_again = keys_back.reshape(seqs_here, seq_total, kv_heads, head_dim)
    values_again = values_back.reshape(seqs_here, seq_total, kv_heads, head_dim)
    grad_rows = cotangent.reshape(row_count, model_width)
    down_grad = back_dot(grad_rows, back_down)
    grad_gate = (
        down_grad * up_pre * sigmoid_gate * (1.0 + gate_pre * (1.0 - sigmoid_gate))
    ).astype(jnp.bfloat16)
    grad_up = (down_grad * silu_gate).astype(jnp.bfloat16)
    grad_mlp_in = back_dot(grad_gate, back_gate) + back_dot(grad_up, back_up)
    grad_norm_two, mlp_gain_terms = norm_back(grad_mlp_in, mlp_gain, normed_two, inverse_two)
    grad_mid = grad_rows.astype(jnp.float32) + grad_norm_two
    grad_proj = grad_mid.astype(jnp.bfloat16)
    grad_attn = back_dot(grad_proj, back_out).astype(jnp.bfloat16)
    grad_five = grad_attn.reshape(seqs_here, block_len, kv_heads, groups, head_dim)
    delta = jnp.einsum("sqkgd,sqkgd->skgq", grad_five.astype(jnp.float32), attn_f32)

    def grad_step(block_idx, carry_grads):
        grad_query, grad_keys, grad_values = carry_grads
        scores, key_block = block_scores(keys_again, block_idx)
        probs = jnp.exp(scores - row_max[..., None]) / row_sum[..., None]
        value_block = lax.dynamic_slice_in_dim(values_again, block_idx * block_len, block_len, 1)
        grad_probs = jnp.einsum(
            "sqkgd,spkd->skgqp", grad_five, value_block, preferred_element_type=jnp.float32
        )
        grad_scores = (probs * (grad_probs - delta[..., None])).astype(jnp.bfloat16)
        grad_query = (
            grad_query
            + jnp.einsum(
                "skgqp,spkd->sqkgd", grad_scores, key_block, preferred_element_type=jnp.float32
            )
            * scale_val
        )
        key_part = (
            jnp.einsum(
                "skgqp,sqkgd->spkd", grad_scores, query_five, preferred_element_type=jnp.float32
            )
            * scale_val
        )
        value_part = jnp.einsum(
            "skgqp,sqkgd->spkd",
            probs.astype(jnp.bfloat16),
            grad_five,
            preferred_element_type=jnp.float32,
        )
        grad_keys = lax.dynamic_update_slice_in_dim(grad_keys, key_part, block_idx * block_len, 1)
        grad_values = lax.dynamic_update_slice_in_dim(
            grad_values, value_part, block_idx * block_len, 1
        )
        return (grad_query, grad_keys, grad_values)

    whole_shape = (seqs_here, seq_total, kv_heads, head_dim)
    grad_query, grad_keys, grad_values = lax.fori_loop(
        0,
        ctx_rank + 1,
        grad_step,
        (
            jnp.zeros((seqs_here, block_len, kv_heads, groups, head_dim), jnp.float32),
            jnp.zeros(whole_shape, jnp.float32),
            jnp.zeros(whole_shape, jnp.float32),
        ),
    )
    key_grad_own, value_grad_own = (
        lax.psum_scatter(
            grad_keys.reshape(seqs_here, seq_total, kv_heads * head_dim).astype(jnp.bfloat16),
            "ctx",
            scatter_dimension=1,
            tiled=True,
        ).astype(jnp.float32),
        lax.psum_scatter(
            grad_values.reshape(seqs_here, seq_total, kv_heads * head_dim).astype(jnp.bfloat16),
            "ctx",
            scatter_dimension=1,
            tiled=True,
        ).astype(jnp.float32),
    )
    key_unrot = rotate_back(key_grad_own.reshape(row_count, kv_heads, head_dim), cosine, sine_tab)
    key_raw_grad, key_gain_terms = norm_back(key_unrot, key_gain, key_normed, key_inverse)
    key_raw_bf = key_raw_grad.reshape(row_count, kv_heads * head_dim).astype(jnp.bfloat16)
    query_unrot = rotate_back(grad_query.reshape(row_count, q_heads, head_dim), cosine, sine_tab)
    query_raw_grad, query_gain_terms = norm_back(
        query_unrot, query_gain, query_normed, query_inverse
    )
    query_raw_bf = query_raw_grad.reshape(row_count, q_heads * head_dim).astype(jnp.bfloat16)
    value_raw_bf = value_grad_own.reshape(row_count, kv_heads * head_dim).astype(jnp.bfloat16)
    grad_attn_in = (
        back_dot(query_raw_bf, back_query)
        + back_dot(key_raw_bf, back_key)
        + back_dot(value_raw_bf, back_value)
    )
    grad_norm_one, norm_gain_terms = norm_back(grad_attn_in, norm_gain, normed_one, inverse_one)
    grad_input = (
        (grad_mid + grad_norm_one).astype(jnp.bfloat16).reshape(seqs_here, block_len, model_width)
    )
    gain_one, gain_query, gain_key, gain_two = lax.psum(
        (
            jnp.sum(norm_gain_terms, axis=0),
            jnp.sum(query_gain_terms, axis=(0, 1)),
            jnp.sum(key_gain_terms, axis=(0, 1)),
            jnp.sum(mlp_gain_terms, axis=0),
        ),
        ("fsdp", "ctx"),
    )
    weight_pairs = (
        (attn_in, query_raw_bf),
        (attn_in, key_raw_bf),
        (attn_in, value_raw_bf),
        (attn_bf, grad_proj),
        (mlp_in, grad_gate),
        (mlp_in, grad_up),
        (hidden_bf, grad_rows),
    )
    pieces = tuple(
        (
            lax.psum_scatter(
                weight_term(acts_in, grad_out).astype(jnp.bfloat16),
                "fsdp",
                scatter_dimension=0,
                tiled=True,
            ).astype(jnp.float32)
            for acts_in, grad_out in weight_pairs
        )
    )
    weight_grads = jax.tree.map(
        lambda part: part.astype(jnp.float32), lax.psum(as_sent(pieces), "ctx")
    )
    grad_wq, grad_wk, grad_wv, grad_wo, grad_wg, grad_wu, grad_wd = weight_grads
    return (
        output,
        grad_input,
        gain_one,
        grad_wq,
        grad_wk,
        grad_wv,
        gain_query,
        gain_key,
        grad_wo,
        gain_two,
        grad_wg,
        grad_wu,
        grad_wd,
    )


def tables(positions, rows, hd):
    own = positions.reshape(rows)
    index = jnp.arange(rows, dtype=jnp.int32)
    place_in = jnp.concatenate([index - rows + own[0], own])
    frequency = theta_base ** (-jnp.arange(0, hd, 2).astype(jnp.float32) / hd)
    angles = place_in.astype(jnp.float32)[:, None] * frequency[None, :]
    cosine, sine = jnp.cos(angles), jnp.sin(angles)
    start = index + rows - own
    start = jnp.where(lax.axis_index("ctx") == 0, jnp.maximum(start, rows), start)
    return jnp.concatenate([cosine, cosine], axis=1), jnp.concatenate([-sine, sine], axis=1), start[None, :]


def grid_device(hidden_in, positions, cotangent, norm_gain, w_query, w_key, w_value, query_gain, key_gain, w_out, mlp_gain, w_gate, w_up, w_down):
    rows, width = hidden_in.shape[1:]
    head_dim = query_gain.shape[0]
    hid, cot = hidden_in.reshape(rows, width), cotangent.reshape(rows, width)
    cos, sin, start = tables(positions, rows, head_dim)
    gains = [g[None, :] for g in (norm_gain, query_gain, key_gain, mlp_gain)]
    shards = (w_query, w_key, w_value, w_out, w_gate, w_up, w_down)
    saved = forward(hid, cos, sin, start, gains, shards)
    done = backward(hid, cot, cos, sin, start, gains, saved, shards)
    gq, gk, gv, go, gg, gu, gd, grad_in, norm, query, key, mlp = done
    return (saved[7][None], grad_in[None], norm[0], gq, gk, gv, query[0], key[0], go, mlp[0], gg, gu, gd)


def is_grid(mesh):
    if dict(mesh.shape) != {"fsdp": 16, "ctx": 2}:
        return False
    for f in range(16):
        for x in range(2):
            device = mesh.devices[f, x]
            if tuple(device.coords) != (x, (f // 2) % 2, f // 4) or device.core_on_chip != f % 2:
                return False
    return True


def solution(mesh):
    in_specs = (
        P("fsdp", "ctx", None),
        P("fsdp", "ctx"),
        P("fsdp", "ctx", None),
        P(),
        P("fsdp", None),
        P("fsdp", None),
        P("fsdp", None),
        P(),
        P(),
        P("fsdp", None),
        P(),
        P("fsdp", None),
        P("fsdp", None),
        P("fsdp", None),
    )
    out_specs = (
        P("fsdp", "ctx", None),
        P("fsdp", "ctx", None),
        P(),
        P("fsdp", None),
        P("fsdp", None),
        P("fsdp", None),
        P(),
        P(),
        P("fsdp", None),
        P(),
        P("fsdp", None),
        P("fsdp", None),
        P("fsdp", None),
    )
    return jax.shard_map(
        grid_device if is_grid(mesh) else per_device, mesh=mesh, in_specs=in_specs, out_specs=out_specs, check_vma=False
    )
```

```python
import functools

import jax
import jax.numpy as jnp
import numpy as np
from jax import lax
from jax.experimental import pallas as pl
from jax.experimental.pallas import tpu as pltpu
from jax.sharding import PartitionSpec as P

MESH = pl.DeviceIdType.MESH

epsilon = 1e-06
theta_base = 1000000.0
log2e = 1.4426950408889634
bf16, f32 = jnp.bfloat16, jnp.float32
HBM = pl.BlockSpec(memory_space=pl.ANY)
VMEM = pl.BlockSpec(memory_space=pltpu.VMEM)

FORWARD_PLAN = (
    ((1, 16, 3, 6), (1, 8, 3, 3), (1, 8, 2, 2), (1, 8, 3, 3), (1, 24, 7, 8), (1, 24, 9, 9), (0, 12, 4, 3)),
    (0, 2, 9, 10, 17, 13, 24),
    (0, 2, 4, 6, 5, 7, 9, 9, 11, 11, 12, 12, 12),
    (1, 0, 13, 0, 0, 7, 6, 2, 3, 0, 1, 1, 0, 1, 7, 1, 0, 3, 0, 3, 0, 2, 0, 1, 0, 1, 0, 0, 2, 2, 0, 36, 25, 3, 8, 20),
    2,
    4,
)

BACKWARD_PLAN = (
    ((1, 1), (1, 1), (1, 1), (1, 1), (1, 1), (1, 1), (1, 1), (1, 1), (1, 1), (1, 1), (1, 1), (1, 1), (1, 1), (1, 1), (1, 1), (1, 1), (1, 1), (1, 1), (1, 1), (1, 1), (1, 1), (1, 1), (1, 1), (1, 1), (1, 1), (1, 1), (0, 0), (0, 0), (0, 0), (0, 0)),
    (
        (0, 0, 0), (1, 0, 0), (0, 1, 0), (1, 1, 0), (0, 0, 1), (1, 2, 0), (0, 1, 1), (0, 2, 0), (0, 3, 0), (0, 2, 1),
        (0, 0, 2), (1, 3, 0), (0, 4, 0), (0, 1, 2), (1, 4, 0), (1, 5, 0), (0, 2, 2), (0, 3, 1), (0, 4, 1), (1, 6, 0),
        (0, 5, 0), (1, 7, 0), (0, 0, 3), (1, 8, 0), (0, 5, 1), (0, 1, 3), (0, 6, 0), (0, 3, 2), (1, 9, 0), (0, 0, 4),
        (0, 7, 0), (1, 10, 0), (0, 2, 3), (0, 6, 1), (0, 4, 2), (0, 1, 4), (0, 8, 0), (0, 7, 1), (0, 0, 5), (1, 11, 0),
        (1, 12, 0), (1, 13, 0), (0, 3, 3), (0, 5, 2), (0, 0, 6), (0, 4, 3), (0, 2, 4), (1, 14, 0), (0, 8, 1), (0, 6, 2),
        (1, 15, 0), (1, 16, 0), (0, 9, 0), (0, 0, 8), (0, 2, 5), (0, 3, 4), (0, 7, 2), (1, 17, 0), (0, 1, 5), (1, 18, 0),
        (0, 8, 2), (0, 4, 4), (0, 1, 6), (0, 5, 3), (0, 3, 5), (0, 10, 0), (0, 2, 6), (0, 9, 1), (1, 19, 0), (0, 1, 8),
        (1, 20, 0), (0, 3, 6), (0, 6, 3), (0, 2, 8), (0, 10, 1), (1, 21, 0), (1, 22, 0), (1, 23, 0), (0, 4, 5), (0, 5, 4),
        (0, 9, 2), (0, 11, 0), (0, 7, 3), (1, 24, 0), (0, 4, 6), (0, 12, 0), (0, 10, 2), (0, 8, 3), (1, 25, 0), (0, 11, 1),
        (1, 26, 0), (1, 27, 0), (0, 4, 8), (1, 28, 0), (0, 9, 3), (0, 5, 5), (0, 12, 1), (0, 6, 4), (1, 29, 0), (1, 30, 0),
        (0, 3, 8), (0, 11, 2), (0, 13, 0), (0, 8, 4), (0, 6, 5), (0, 7, 4), (0, 5, 6), (0, 10, 3), (0, 14, 0), (0, 8, 5),
        (0, 9, 4), (0, 12, 2), (0, 6, 6), (0, 13, 1), (1, 31, 0), (1, 32, 0), (0, 7, 5), (0, 14, 1), (0, 5, 8), (0, 15, 0),
        (0, 6, 8), (1, 33, 0), (0, 13, 2), (0, 8, 6), (0, 16, 0), (1, 34, 0), (0, 9, 5), (0, 10, 4), (0, 7, 6), (0, 11, 3),
        (0, 15, 1), (1, 35, 0), (1, 36, 0), (1, 37, 0), (0, 14, 2), (0, 10, 5), (0, 7, 8), (0, 12, 3), (0, 11, 4), (1, 38, 0),
        (0, 16, 1), (1, 39, 0), (0, 12, 4), (1, 40, 0), (0, 9, 6), (0, 17, 0), (0, 15, 2), (1, 41, 0), (0, 8, 8), (1, 42, 0),
        (0, 11, 5), (0, 16, 2), (0, 13, 3), (0, 14, 3), (1, 43, 0), (0, 9, 8), (0, 12, 5), (0, 17, 1), (0, 18, 0), (0, 13, 4),
        (1, 44, 0), (0, 10, 6), (0, 11, 6), (1, 45, 0), (0, 17, 2), (0, 19, 0), (1, 46, 0), (0, 10, 8), (0, 18, 1), (0, 15, 3),
        (1, 47, 0), (0, 12, 6), (0, 14, 4), (0, 11, 8), (0, 19, 1), (0, 13, 5), (0, 20, 0), (0, 16, 3), (1, 48, 0), (0, 15, 4),
        (0, 18, 2), (0, 21, 0), (0, 17, 3), (1, 49, 0), (0, 16, 4), (0, 20, 1), (0, 14, 5), (1, 50, 0), (1, 51, 0), (0, 15, 5),
        (1, 52, 0), (0, 13, 6), (0, 19, 2), (0, 17, 4), (1, 53, 0), (0, 14, 6), (0, 16, 5), (1, 54, 0), (1, 55, 0), (0, 13, 8),
        (0, 12, 8), (0, 21, 1), (0, 18, 3), (0, 20, 2), (0, 17, 5), (0, 22, 0), (0, 23, 0), (0, 18, 4), (0, 15, 6), (1, 56, 0),
        (1, 57, 0), (1, 58, 0), (0, 21, 2), (0, 15, 8), (0, 23, 1), (0, 14, 8), (1, 59, 0), (0, 16, 6), (0, 18, 5), (0, 20, 3),
        (0, 22, 1), (0, 24, 0), (0, 17, 6), (1, 60, 0), (0, 19, 3), (0, 20, 4), (0, 23, 2), (0, 21, 3), (0, 16, 8), (0, 24, 1),
        (0, 25, 0), (0, 26, 0), (0, 22, 2), (0, 19, 4), (0, 25, 1), (0, 18, 6), (0, 20, 5), (0, 23, 3), (0, 19, 5), (0, 24, 2),
        (0, 23, 4), (1, 61, 0), (0, 26, 1), (2, 0, 0), (0, 22, 3), (0, 25, 2), (1, 62, 0), (0, 18, 8), (1, 63, 0), (0, 17, 8),
        (0, 19, 6), (0, 21, 4), (0, 27, 0), (1, 64, 0), (0, 20, 6), (0, 22, 4), (0, 28, 0), (0, 19, 8), (0, 24, 3), (0, 21, 5),
        (2, 1, 0), (0, 24, 4), (0, 27, 1), (0, 26, 3), (0, 22, 5), (2, 2, 0), (0, 21, 6), (1, 65, 0), (2, 3, 0), (0, 29, 0),
        (0, 26, 4), (0, 25, 3), (2, 4, 0), (0, 29, 1), (0, 23, 5), (0, 24, 5), (1, 66, 0), (0, 24, 6), (0, 20, 8), (2, 5, 0),
        (1, 67, 0), (0, 22, 6), (0, 27, 3), (0, 27, 4), (0, 26, 5), (0, 28, 1), (0, 29, 3), (2, 6, 0), (2, 7, 0), (0, 26, 6),
        (0, 25, 4), (0, 22, 8), (0, 21, 8), (0, 27, 5), (1, 68, 0), (0, 29, 4), (0, 23, 6), (0, 25, 5), (0, 28, 3), (0, 25, 6),
        (0, 27, 6), (0, 28, 4), (0, 28, 5), (0, 24, 8), (0, 28, 6), (0, 23, 8), (0, 29, 5), (0, 26, 8), (0, 25, 8), (1, 69, 0),
        (0, 29, 6), (1, 71, 0), (0, 27, 8), (1, 70, 0), (0, 29, 8), (0, 28, 8),
    ),
)


def place():
    f = lax.axis_index("fsdp")
    return f // 4, (f // 2) % 2, f % 2, lax.axis_index("ctx")


def enter(z, y, c, x, ends=False):
    bar = pltpu.get_barrier_semaphore()

    def hail(z2, y2, c2, x2):
        pl.semaphore_signal(bar, inc=1, device_id=(z2 * 4 + y2 * 2 + c2, x2), device_id_type=MESH)

    hail(z, y, c, 1 - x)
    hail(z, 1 - y, c, x)
    hail(z, y, 1 - c, x)

    @pl.when(z > 0)
    def _():
        hail(z - 1, y, c, x)

    @pl.when(z < 3)
    def _():
        hail(z + 1, y, c, x)

    if ends:
        @pl.when(z % 3 == 0)
        def _():
            hail(3 - z, y, c, x)

    pl.semaphore_wait(bar, 5 if ends else 4 + (z * (3 - z)) // 2)


class Gather:
    def __init__(self, index, own, full, sems, at, cut):
        self.g, self.own, self.full = index, own, full
        self.zr, self.yr, self.xr, self.cr, self.zs, self.ys, self.xs, self.cs, self.ls = sems
        self.z, self.y, self.c, self.x = at
        self.rows, self.cols = own.shape
        self.dim, units, ones, twos = cut
        step = own.shape[self.dim] // units
        low, middle, high = (0, ones * step), (ones * step, (units - twos - ones) * step), ((units - twos) * step, twos * step)
        self.plans = ((0, low[1] + middle[1]), low, high), ((low[1], middle[1] + high[1]), high, low)
        self.all = None

    def step(self, name, *args):
        for x in (0, 1):
            @pl.when(self.x == x)
            def _():
                self.ywin, self.xwin, self.xgot = self.plans[x]
                getattr(self, name)(*args)

    def window(self, ref, row, win):
        if win is None:
            return ref.at[pl.ds(row, self.rows), :]
        if self.dim == 0:
            return ref.at[pl.ds(row + win[0], win[1]), :]
        return ref.at[pl.ds(row, self.rows), pl.ds(*win)]

    def part(self, z2, y2, c2, win):
        f2 = z2 * 4 + y2 * 2 + c2
        return self.window(self.full, pl.multiple_of(f2 * self.rows, 16), win)

    def mine(self):
        return self.window(self.own, 0, self.ywin)

    def send(self, src, dst, ssem, rsem, to):
        z2, y2, c2, x2 = to
        return pltpu.make_async_remote_copy(
            src_ref=src, dst_ref=dst, send_sem=ssem, recv_sem=rsem,
            device_id=(z2 * 4 + y2 * 2 + c2, x2), device_id_type=MESH)

    def z_copy(self, zs, up, first):
        dst = self.part(zs, self.y, self.c, self.ywin)
        src = self.mine() if first else dst
        z2 = self.z + 1 if up else self.z - 1
        return self.send(src, dst, self.zs.at[self.g, zs, 1 if up else 0], self.zr.at[self.g, zs], (z2, self.y, self.c, self.x))

    def y_copy(self, zs, first):
        dst = self.part(zs, self.y, self.c, self.ywin)
        src = self.mine() if first else dst
        return self.send(src, dst, self.ys.at[self.g, zs], self.yr.at[self.g, zs], (self.z, 1 - self.y, self.c, self.x))

    def x_copy(self, zs, y2):
        dst = self.part(zs, y2, self.c, self.xwin)
        s = zs * 2 + y2
        return self.send(dst, dst, self.xs.at[self.g, s], self.xr.at[self.g, s], (self.z, self.y, self.c, 1 - self.x))

    def c_copy(self, zs, y2, win, piece, first=False):
        dst = self.part(zs, y2, self.c, win)
        src = self.own if first else dst
        s = (zs * 2 + y2) * 2 + piece
        return self.send(src, dst, self.cs.at[self.g, s], self.cr.at[self.g, s], (self.z, self.y, 1 - self.c, self.x))

    def await_(self, dst, sem):
        pltpu.make_async_copy(dst, dst, sem).wait()

    def local(self):
        return pltpu.make_async_copy(self.own, self.part(self.z, self.y, self.c, self.all), self.ls.at[self.g])

    def begin(self):
        z = self.z

        @pl.when(z < 3)
        def _():
            self.z_copy(z, True, True).start()

        @pl.when(z > 0)
        def _():
            self.z_copy(z, False, True).start()

        self.y_copy(z, True).start()
        self.c_copy(z, self.y, self.all, 0, True).start()
        self.local().start()

    def spread(self, zs, up):
        self.await_(self.part(zs, self.y, self.c, self.ywin), self.zr.at[self.g, zs])

        @pl.when(self.z < 3 if up else self.z > 0)
        def _():
            self.z_copy(zs, up, False).start()

        self.y_copy(zs, False).start()
        self.x_copy(zs, self.y).start()
        self.c_copy(zs, self.y, self.ywin, 0).start()

    def along_z(self, k):
        @pl.when(self.z >= k)
        def _():
            self.spread(self.z - k, True)

        @pl.when(self.z + k <= 3)
        def _():
            self.spread(self.z + k, False)

    def over_y(self, zs):
        self.await_(self.part(zs, 1 - self.y, self.c, self.ywin), self.yr.at[self.g, zs])
        self.x_copy(zs, 1 - self.y).start()
        self.c_copy(zs, 1 - self.y, self.ywin, 0).start()

    def along_y(self, k):
        if k == 0:
            self.over_y(self.z)
            return

        @pl.when(self.z >= k)
        def _():
            self.over_y(self.z - k)

        @pl.when(self.z + k <= 3)
        def _():
            self.over_y(self.z + k)

    def over_x(self, zs, y2):
        self.await_(self.part(zs, y2, self.c, self.xgot), self.xr.at[self.g, zs * 2 + y2])
        self.c_copy(zs, y2, self.xgot, 1).start()

    def along_x(self, k):
        if k == 0:
            self.over_x(self.z, 1 - self.y)
            return

        for y2 in (self.y, 1 - self.y):
            @pl.when(self.z >= k)
            def _():
                self.over_x(self.z - k, y2)

            @pl.when(self.z + k <= 3)
            def _():
                self.over_x(self.z + k, y2)

    def finish(self):
        z, y = self.z, self.y
        self.local().wait()
        c = 1 - self.c
        self.await_(self.part(z, y, c, self.all), self.cr.at[self.g, (z * 2 + y) * 2])
        for k in range(0, 4):
            for y2 in ((y, 1 - y) if k else (1 - y,)):
                for zs, ok in ((z - k, z >= k), (z + k, z + k <= 3))[: 2 if k else 1]:
                    @pl.when(ok)
                    def _():
                        s = (zs * 2 + y2) * 2
                        self.await_(self.part(zs, y2, c, self.ywin), self.cr.at[self.g, s])
                        self.await_(self.part(zs, y2, c, self.xgot), self.cr.at[self.g, s + 1])

    def drain(self):
        z, y = self.z, self.y

        @pl.when(z < 3)
        def _():
            self.z_copy(z, True, True).wait_send()

        @pl.when(z > 0)
        def _():
            self.z_copy(z, False, True).wait_send()

        self.y_copy(z, True).wait_send()
        self.c_copy(z, y, self.all, 0, True).wait_send()
        self.x_copy(z, 1 - y).wait_send()
        self.c_copy(z, 1 - y, self.ywin, 0).wait_send()
        self.c_copy(z, 1 - y, self.xgot, 1).wait_send()
        for k in range(1, 4):
            for zs, ok, more, up in ((z - k, z >= k, z < 3, True), (z + k, z + k <= 3, z > 0, False)):
                @pl.when(ok)
                def _():
                    @pl.when(more)
                    def _():
                        self.z_copy(zs, up, False).wait_send()

                    self.y_copy(zs, False).wait_send()
                    for y2 in (y, 1 - y):
                        self.x_copy(zs, y2).wait_send()
                        self.c_copy(zs, y2, self.ywin, 0).wait_send()
                        self.c_copy(zs, y2, self.xgot, 1).wait_send()


def gather_sems(n):
    return [pltpu.SemaphoreType.DMA(s) for s in ((n, 4), (n, 4), (n, 8), (n, 16), (n, 4, 2), (n, 4), (n, 8), (n, 16), (n,))]


def dot_nn(a, b):
    return lax.dot_general(a, b, (((1,), (0,)), ((), ())), preferred_element_type=f32)


def dot_nt(a, b):
    return lax.dot_general(a, b, (((1,), (1,)), ((), ())), preferred_element_type=f32)


def dot_tn(a, b):
    return lax.dot_general(a, b, (((0,), (0,)), ((), ())), preferred_element_type=f32)


def rows_loop(count, step, body):
    @pl.loop(0, count // step)
    def _(i):
        body(pl.multiple_of(i * step, step), step)


class Writes:
    def __init__(self, sem):
        self.sem, self.all, self.open = sem, [], set()

    def start(self, src, dst):
        copy = pltpu.make_async_copy(src, dst, self.sem.at[len(self.all)])
        copy.start()
        self.open.add(len(self.all))
        self.all.append(copy)
        return len(self.all) - 1

    def wait(self, i):
        if i in self.open:
            self.all[i].wait()
            self.open.remove(i)

    def wait_all(self):
        for i in sorted(self.open):
            self.wait(i)


def unit_heads(values):
    size = values.shape[-1]
    mean = dot_nn((values * values).astype(bf16), jnp.full((size, size), 1.0 / size, bf16))
    inverse = lax.rsqrt(mean + epsilon)
    return values * inverse, inverse


def unit_rows(values):
    inverse = lax.rsqrt(jnp.mean(values * values, axis=-1, keepdims=True) + epsilon)
    return values * inverse, inverse


def turn(u, cos, sin):
    return u * cos + pltpu.roll(u, u.shape[-1] // 2, 1) * sin


def turn_back(u, cos, sin):
    return u * cos - pltpu.roll(u, u.shape[-1] // 2, 1) * sin


def mask_bias(bias, start_ref, rows):
    block = 128

    @pl.loop(0, bias.shape[0] // block)
    def _(i):
        rr = pl.ds(pl.multiple_of(i * block, block), block)
        key = lax.broadcasted_iota(jnp.int32, (block, rows), 0) + i * block
        query = lax.broadcasted_iota(jnp.int32, (block, rows), 1) + rows
        ok = (key >= start_ref[...]) & (key <= query)
        bias[rr, :] = jnp.where(ok, 0.0, -1e30)


class Schedule:
    def __init__(self, gathers, starts, after):
        steps = [("begin",)] + [("along_z", k) for k in (1, 2, 3)] + [("along_y", k) for k in range(4)] + [("along_x", k) for k in range(4)] + [("finish",)]
        slots = {}
        for i, g in reversed(list(enumerate(gathers))):
            for j, s in zip(after, steps):
                slots.setdefault(starts[i] + j, []).append((i, g, s))
        self.steps = [step for t in sorted(slots) for step in slots[t]]

    def run(self, count):
        for i, g, s in self.steps[:count]:
            g.step(*s)
        self.steps = self.steps[count:]

    def until(self, weight):
        ends = [n for n, (i, g, s) in enumerate(self.steps) if i == weight and s[0] == "finish"]
        if ends:
            self.run(ends[0] + 1)


def forward_kernel(plan, hid, pos, freq, norm_gain, query_gain, key_gain, mlp_gain, *refs):
    owns, refs = refs[:7], refs[7:]
    outs, refs = refs[:7], refs[7:]
    (q_o, k_o, v_o, qraw_o, kraw_o, ain_o, attn_o, lse_o, mid_o, mlp_o, gate_o, up_o, hidden_o, cos_o, sin_o, start), refs = refs[:16], refs[16:]
    fulls, refs = refs[:6] + (outs[6],), refs[6:]
    (ain, q, k, vt, attn, bias, tmp, mid, stage, cos, sin, ain_sem, out_sem), sems = refs[:13], refs[13:]
    w_q, w_k, w_v, w_o, w_g, w_u = fulls[:6]
    cuts, starts, after, runs, early, _ = plan
    runs = list(runs)
    at = place()
    z, y, c, x = at
    rows, width = hid.shape
    hd = freq.shape[1]
    kv = w_k.shape[1] // hd
    qh = w_q.shape[1] // hd
    group = qh // kv
    span = tmp.shape[1]
    first, second = pl.ds(0, rows), pl.ds(rows, rows)
    enter(*at)
    gs = [Gather(i, owns[i], fulls[i], sems, at, cuts[i]) for i in range(7)]
    sched = Schedule(gs, starts, after)
    writes = Writes(out_sem)
    sched.run(1)

    def norm_one(r, n):
        unit, _ = unit_rows(hid[pl.ds(r, n), :].astype(f32))
        ain[pl.ds(pl.multiple_of(r + rows, n), n), :] = (unit * norm_gain[...]).astype(bf16)

    rows_loop(rows, 64, norm_one)
    count = ain_sem.shape[1]
    size = rows // count

    def handed(n):
        return pltpu.make_async_remote_copy(
            src_ref=ain.at[pl.ds(rows + n * size, size), :], dst_ref=ain.at[pl.ds(n * size, size), :],
            send_sem=ain_sem.at[0, n], recv_sem=ain_sem.at[1, n],
            device_id=(z * 4 + y * 2 + c, 1 - x), device_id_type=MESH)

    left = list(range(count))

    def hand():
        if left:
            n = left.pop(0)

            @pl.when(x == 0)
            def _():
                handed(n).start()

    def pump():
        sched.run(runs.pop(0))
        hand()

    hand()

    @pl.when(x == 0)
    def _():
        ain[first, :] = jnp.zeros((rows, width), bf16)

    index = lax.broadcasted_iota(jnp.int32, (1, rows), 1)
    head = jnp.sum(jnp.where(index == 0, pos[...], 0), axis=1, keepdims=True)
    own_start = index + rows - pos[...]
    start[...] = jnp.where(x == 0, jnp.maximum(own_start, rows), own_start)
    sign = jnp.where(lax.broadcasted_iota(jnp.int32, (rows, hd), 1) < hd // 2, -1.0, 1.0)
    for rr, row in ((second, pos[...]), (first, index - rows + head)):
        angle = jnp.broadcast_to(row.astype(f32), (hd, rows)).T * freq[...]
        cos[rr, :] = jnp.cos(angle)
        sin[rr, :] = jnp.sin(angle) * sign
    writes.start(cos, cos_o)
    writes.start(sin, sin_o)
    mask_bias(bias, start, rows)
    for _ in range(early):
        sched.run(2)
        hand()
    sched.until(0)

    def heads(lhs, weight, base, count, gain, into, col):
        for r in range(0, count, rows):
            tmp[r:r + rows, :] = dot_nn(lhs[pl.ds(r, rows), :], weight)
            pump()
        for part in range(0, span // hd, 4):
            @pl.loop(part, part + 4)
            def _(h):
                cc = pl.ds(pl.multiple_of(h * hd, hd), hd)
                to = pl.ds(pl.multiple_of(col + h * hd, hd), hd)
                for r in range(0, count, 256):
                    raw = tmp[r:r + 256, cc]
                    stage[r:r + 256, cc] = raw.astype(bf16)
                    unit, _ = unit_heads(raw)
                    t = slice(base + r, base + r + 256)
                    into[r:r + 256, to] = turn(unit * gain[...], cos[t, :], sin[t, :]).astype(bf16)

            pump()

    last = None
    for b in range(w_q.shape[1] // span):
        if last is not None:
            writes.wait(last)
        heads(ain.at[second, :], w_q[:, b * span:(b + 1) * span], rows, rows, query_gain, q, b * span)
        last = writes.start(stage.at[first, :], qraw_o.at[:, pl.ds(b * span, span)])
    while left:
        hand()
    sched.until(1)

    @pl.when(x == 1)
    def _():
        for n in range(count):
            handed(n).wait_recv()

    writes.wait(last)
    heads(ain, w_k[...], 0, 2 * rows, key_gain, k, 0)
    last = writes.start(stage, kraw_o)
    writes.start(ain, ain_o)
    writes.start(q, q_o)
    writes.start(k, k_o)
    sched.until(2)
    for r in (first, second):
        tmp[r, :] = dot_nn(ain[r, :], w_v[...])
        pump()
    writes.wait(last)
    stage[...] = tmp[...].astype(bf16)
    last = writes.start(stage, v_o)

    @pl.loop(0, kv)
    def _(h):
        cc = pl.ds(pl.multiple_of(h * hd, hd), hd)
        vt[cc, :] = tmp[:, cc].astype(bf16).T

    pump()

    c2 = hd ** (-0.5) * log2e
    for part in range(kv):
        @pl.loop(part, part + 1)
        def _(h):
            cc = pl.ds(pl.multiple_of(h * hd, hd), hd)
            for g in range(group):
                n = h * group + g
                qc = pl.ds(pl.multiple_of(n * hd, hd), hd)
                p = jnp.exp2(dot_nt(k[:, cc], q[:, qc]) * c2 + bias[...])
                total = jnp.sum(p, axis=0, keepdims=True)
                o = dot_nn(vt[cc, :], p.astype(bf16))
                attn[qc, :] = (o * (1.0 / total)).astype(bf16)
                lse_o[pl.ds(n, 1), :] = jnp.log2(total)

        pump()
    writes.start(attn, attn_o)
    sched.until(3)
    for i in range(3):
        gs[i].step("drain")
    leaving = [writes.start(fulls[i], outs[i]) for i in range(3)]
    mid[...] = hid[...].astype(f32) + dot_tn(attn[...], w_o[...])
    pump()

    for n in leaving:
        writes.wait(n)
    writes.wait(last)
    blocks = w_g.shape[1] // span
    hidden = [w_q.at[first, pl.ds(0, span)], w_q.at[second, pl.ds(0, span)], w_q.at[first, pl.ds(span, span)]]
    mlp_in = w_q.at[second, pl.ds(span, span)]
    gates = [w_k.at[first, :], w_v.at[first, :], stage.at[first, :]]
    ups = [w_k.at[second, :], w_v.at[second, :], stage.at[second, :]]

    def norm_two(r, n):
        unit, _ = unit_rows(mid[pl.ds(r, n), :])
        mlp_in[pl.ds(r, n), :] = (unit * mlp_gain[...]).astype(bf16)

    rows_loop(rows, 64, norm_two)
    writes.start(mid, mid_o)
    writes.start(mlp_in, mlp_o)
    sched.until(4)
    sched.until(5)
    for j in range(blocks):
        cols = pl.ds(j * span, span)
        tmp[first, :] = dot_nn(mlp_in[...], w_g[:, cols])
        pump()
        tmp[second, :] = dot_nn(mlp_in[...], w_u[:, cols])
        pump()

        def act(r, n):
            rr = pl.ds(r, n)
            gate, up = tmp[rr, :], tmp[pl.ds(pl.multiple_of(r + rows, n), n), :]
            hidden[j][rr, :] = (gate * jax.nn.sigmoid(gate) * up).astype(bf16)
            gates[j][rr, :] = gate.astype(bf16)
            ups[j][rr, :] = up.astype(bf16)

        rows_loop(rows, 64, act)
        writes.start(gates[j], gate_o.at[:, cols])
        writes.start(ups[j], up_o.at[:, cols])
        writes.start(hidden[j], hidden_o.at[:, cols])
        pump()
    for i in (3, 4, 5):
        writes.start(fulls[i], outs[i])
    sched.until(6)
    sched.run(len(sched.steps))
    for g in gs[3:]:
        g.step("drain")

    @pl.when(x == 0)
    def _():
        for n in range(count):
            handed(n).wait_send()

    writes.wait_all()


def forward(hid, pos, freq, gains, shards):
    rows, width = hid.shape
    hd = freq.shape[1]
    fulls = [(s.shape[0] * 16, s.shape[1]) for s in shards]
    heads, keys, ff = shards[0].shape[1], shards[1].shape[1], shards[4].shape[1]
    shape = jax.ShapeDtypeStruct
    vm = pltpu.VMEM
    outs = [shape(s, bf16) for s in fulls] + [
        shape((rows, heads), bf16), shape((2 * rows, keys), bf16), shape((2 * rows, keys), bf16),
        shape((rows, heads), bf16), shape((2 * rows, keys), bf16), shape((2 * rows, width), bf16), shape((heads, rows), bf16),
        shape((heads // hd, rows), f32), shape((rows, width), f32), shape((rows, width), bf16),
        shape((rows, ff), bf16), shape((rows, ff), bf16), shape((rows, ff), bf16),
        shape((2 * rows, hd), f32), shape((2 * rows, hd), f32), shape((1, rows), jnp.int32)]
    specs = [HBM] * 7 + [VMEM if i in (7, 15) else HBM for i in range(16)]
    return pl.pallas_call(
        functools.partial(forward_kernel, FORWARD_PLAN),
        out_shape=outs,
        in_specs=[VMEM] * 7 + [HBM] * 7,
        out_specs=specs,
        scratch_shapes=[vm(s, bf16) for s in fulls[:6]] + [
            vm((2 * rows, width), bf16), vm((rows, heads), bf16), vm((2 * rows, keys), bf16), vm((keys, 2 * rows), bf16),
            vm((heads, rows), bf16), vm((2 * rows, rows), f32), vm((2 * rows, keys), f32), vm((rows, width), f32),
            vm((2 * rows, keys), bf16), vm((2 * rows, hd), f32), vm((2 * rows, hd), f32), pltpu.SemaphoreType.DMA((2, FORWARD_PLAN[5])), pltpu.SemaphoreType.DMA((32,))] + gather_sems(7),
        compiler_params=pltpu.CompilerParams(collective_id=1, has_side_effects=True, vmem_limit_bytes=62 * 2**20),
        name="forward_gather",
    )(hid, pos, freq, *gains, *shards)


class Chunk:
    def __init__(self, index, bufs, sems, at, out, ones, twos):
        self.i, self.out, self.ones, self.twos = index, out, ones, twos
        ring = [index % b.shape[0] for b in bufs]
        self.g, self.cb, self.xb, self.yb, self.zb, self.fb, self.st = [b.at[r] for b, r in zip(bufs, ring)]
        self.sc, self.sx, self.sy, self.zs, self.zr, self.sf, self.so = [s.at[index] for s in sems]
        self.z, self.y, self.c, self.x = at
        self.unit = self.g.shape[3] // 4

    def step(self, name, *args):
        u = self.unit
        if self.ones == self.twos and name != "finish":
            t = self.ones
            self.first = self.x * t
            self.keep, self.send_x, self.got_x, self.theirs = 4 - t, t, t, 4 - t
            self.ywin = pl.ds(pl.multiple_of(self.first * u, 16), self.keep * u)
            self.xsend = pl.ds(pl.multiple_of((1 - self.x) * (4 - t) * u, 16), t * u)
            self.xgot = pl.ds(pl.multiple_of(self.x * (4 - t) * u, 16), t * u)
            getattr(self, name)(*args)
            return
        for x in (0, 1):
            @pl.when(self.x == x)
            def _():
                spans = ((0, 4 - self.twos), (self.ones, 4))
                lows, highs = (0, self.ones), (4 - self.twos, 4)
                self.span, self.other = spans[x], spans[1 - x]
                self.keep, self.theirs = self.span[1] - self.span[0], self.other[1] - self.other[0]
                out, into = (highs, lows) if x == 0 else (lows, highs)
                self.send_x, self.got_x = out[1] - out[0], into[1] - into[0]
                self.ywin = pl.ds(self.span[0] * u, self.keep * u)
                self.xsend, self.xgot = pl.ds(out[0] * u, self.send_x * u), pl.ds(into[0] * u, self.got_x * u)
                getattr(self, name)(*args)

    def send(self, src, dst, ssem, rsem, z2, y2, c2, x2):
        return pltpu.make_async_remote_copy(
            src_ref=src, dst_ref=dst, send_sem=ssem, recv_sem=rsem,
            device_id=(z2 * 4 + y2 * 2 + c2, x2), device_id_type=MESH)

    def c_copy(self):
        return self.send(self.g.at[:, :, 1 - self.c], self.cb, self.sc.at[0], self.sc.at[1], self.z, self.y, 1 - self.c, self.x)

    def x_copy(self):
        return self.send(
            self.g.at[:, :, self.c, self.xsend], self.xb.at[:, :, pl.ds(0, self.send_x * self.unit)], self.sx.at[0], self.sx.at[1],
            self.z, self.y, self.c, 1 - self.x)

    def y_copy(self):
        return self.send(
            self.g.at[:, 1 - self.y, self.c, self.ywin], self.yb.at[:, pl.ds(0, self.keep * self.unit)], self.sy.at[0], self.sy.at[1],
            self.z, 1 - self.y, self.c, self.x)

    def z_slot(self, slot):
        return self.zb.at[slot, pl.ds(0, self.keep * self.unit)]

    def z_copy(self, here, to, up):
        there = here + 1 if up else here - 1
        slot = 4 if to == there and not up else to
        return self.send(
            self.g.at[to, self.y, self.c, self.ywin], self.z_slot(slot), self.zs.at[to], self.zr.at[slot], there, self.y, self.c, self.x)

    def f_copy(self):
        return self.send(
            self.g.at[self.z, self.y, self.c, self.ywin], self.fb.at[pl.ds(0, self.keep * self.unit)], self.sf.at[0], self.sf.at[1],
            self.z, self.y, self.c, 1 - self.x)

    def o_copy(self):
        return pltpu.make_async_copy(self.st, self.out, self.so)

    def arrived(self, dst, sem):
        pltpu.make_async_copy(dst, dst, sem).wait()

    def add(self, zz, yy, win, src):
        dst = self.g.at[zz, yy, self.c, win]
        dst[...] = dst[...] + src[...]

    def go(self):
        self.c_copy().start()

    def over_c(self):
        self.c_copy().wait_recv()

        @pl.loop(0, 4)
        def _(zz):
            for yy in (0, 1):
                self.add(zz, yy, slice(None), self.cb.at[zz, yy])

        if self.send_x:
            self.x_copy().start()
        if not self.ones and not self.twos:
            self.y_copy().start()

    def over_x(self):
        if self.got_x:
            got = self.xb.at[:, :, pl.ds(0, self.got_x * self.unit)]
            self.arrived(got, self.sx.at[1])

            @pl.loop(0, 4)
            def _(zz):
                for yy in (0, 1):
                    self.add(zz, yy, self.xgot, got.at[zz, yy])

        self.y_copy().start()

    def over_y(self):
        self.y_copy().wait_recv()

        @pl.loop(0, 4)
        def _(zz):
            self.add(zz, self.y, self.ywin, self.yb.at[zz, pl.ds(0, self.keep * self.unit)])

    def take(self, zz, slot):
        self.arrived(self.z_slot(slot), self.zr.at[slot])
        self.add(zz, self.y, self.ywin, self.z_slot(slot))

    def over_z(self, k):
        for up in (True, False):
            here = k if up else 3 - k

            @pl.when(self.z == here)
            def _():
                for to in (range(3, here, -1) if up else range(here)):
                    if k:
                        self.take(to, to)
                    self.z_copy(here, to, up).start()
                if k:
                    self.take(here, here if up else 4)

    def hand(self):
        self.f_copy().start()

    def finish(self, before):
        u = self.unit
        self.arrived(self.fb.at[pl.ds(0, self.theirs * u)], self.sf.at[1])
        if before is not None:
            before.o_copy().wait()
        own = self.g.at[self.z, self.y, self.c]
        (a, b), (c, d) = self.span, self.other
        for lo, hi in ((0, max(a, c)), (max(a, c), min(b, d)), (min(b, d), 4)):
            if lo < hi:
                mine, theirs = own[lo * u:hi * u, :].astype(f32), None
                if c <= lo and hi <= d:
                    theirs = self.fb[(lo - c) * u:(hi - c) * u, :].astype(f32)
                held = a <= lo and hi <= b
                self.st[lo * u:hi * u, :] = theirs if not held else mine if theirs is None else mine + theirs
        self.o_copy().start()
        self.c_copy().wait_send()
        if self.send_x:
            self.x_copy().wait_send()
        self.y_copy().wait_send()
        self.f_copy().wait_send()
        for here in range(4):
            @pl.when(self.z == here)
            def _():
                for to in range(4):
                    if to != here:
                        self.z_copy(here, to, to > here).wait_send()


def chunk_bufs(rows, cols):
    part = rows // 4
    sizes = ((10, 4, 2, 2, rows, cols), (4, 4, 2, rows, cols), (6, 4, 2, part, cols), (6, 4, rows, cols), (6, 5, rows, cols), (8, rows, cols))
    return [pltpu.VMEM(s, bf16) for s in sizes] + [pltpu.VMEM((2, rows, cols), f32)]


def chunk_sems(n):
    return [pltpu.SemaphoreType.DMA(s) for s in ((n, 2), (n, 2), (n, 2), (n, 4), (n, 5), (n, 2), (n,))]


class Totals:
    def __init__(self, mine, got, sem, at):
        self.mine, self.got, self.sem = mine, got, sem
        z, y, c, x = at
        self.to = [(z, y, 1 - c, x), (z, y, c, 1 - x), (z, 1 - y, c, x), (z + 1 - 2 * (z % 2), y, c, x), (3 - z, y, c, x)]

    def copy(self, s):
        z, y, c, x = self.to[s]
        return pltpu.make_async_remote_copy(
            src_ref=self.mine.at[s], dst_ref=self.got.at[s], send_sem=self.sem.at[s, 0], recv_sem=self.sem.at[s, 1],
            device_id=(z * 4 + y * 2 + c, x), device_id_type=MESH)

    def step(self, s):
        if s > 0:
            self.copy(s - 1).wait()
            self.mine[s] = self.mine[s - 1] + self.got[s - 1]
        if s < 5:
            self.copy(s).start()


def backward_kernel(plan, cot, cos, sin, start, norm_gain, query_gain, key_gain, mlp_gain, lse, *refs):
    full, refs = refs[:7], refs[7:]
    (hid_i, q_i, k_i, v_i, qraw_i, kraw_i, ain_i, attn_i, mid_i, mlp_i, gate_i, up_i, hidden_i), refs = refs[:13], refs[13:]
    grads, refs = refs[:7], refs[7:]
    (out_o, gin_o, norm_o, query_o, key_o, mlp_o), refs = refs[:6], refs[6:]
    (hidden, mlp, ggate, gup, mid, acc, gproj, attn, q, k, v, qraw, kraw, ain, dk, dv, kt, bias, wbuf, earlier, sum_one, sum_two, sum_q, sum_k,
     gain_mine, gain_got, gain_sem, load_sem, w_sem, early_sem), refs = refs[:30], refs[30:]
    bufs, sems = refs[:7], refs[7:]
    at = place()
    z, y, c, x = at
    rows, width = cot.shape
    hd = cos.shape[1]
    kv, qh = k.shape[1] // hd, q.shape[1] // hd
    group = qh // kv
    span = wbuf.shape[1]
    ff = ggate.shape[1]
    cols = bufs[0].shape[-1]
    first, second = pl.ds(0, rows), pl.ds(rows, rows)
    scale = hd ** (-0.5)
    enter(*at, True)

    loads = Writes(load_sem)
    hidden_l = loads.start(hidden_i, hidden)
    blocks = [full[6].at[pl.ds(j * span, span), :] for j in range(ff // span)]
    for j in range(ff // span):
        blocks += [full[4].at[:, pl.ds(j * span, span)], full[5].at[:, pl.ds(j * span, span)]]
    blocks += [full[3].at[pl.ds(j * span, span), :] for j in range(qh * hd // span)]
    blocks += [full[1], full[2]] + [full[0].at[:, pl.ds(j * span, span)] for j in range(qh * hd // span)]

    def fetch(n):
        return pltpu.make_async_copy(blocks[n], wbuf.at[n % 2], w_sem.at[n % 2])

    def weight(n):
        fetch(n).wait()
        return wbuf[n % 2]

    def used(n):
        if n + 2 < len(blocks):
            fetch(n + 2).start()

    fetch(0).start()
    fetch(1).start()
    gate_l = loads.start(gate_i, ggate)
    up_l = loads.start(up_i, gup)
    mlp_l, mid_l, attn_l = loads.start(mlp_i, mlp), loads.start(mid_i, mid), loads.start(attn_i, attn)
    later = []

    todo = []

    def put(val, spot, subs, shards_from):
        size = bufs[0].shape[4]
        for f in range(val.shape[0] // (size * subs)):
            for s in range(subs):
                owner = shards_from + f
                lo = (f * subs + s) * size
                bufs[0][(spot + s) % bufs[0].shape[0], owner // 4, owner // 2 % 2, owner % 2] = val[lo:lo + size, :].astype(bf16)

    def make_down(j):
        def run(spot):
            loads.wait(hidden_l)
            wide = hidden.shape[1] // 4
            for b in range(4):
                put(dot_tn(hidden[:, b * wide:(b + 1) * wide], cot[:, j * cols:(j + 1) * cols]), spot, wide // 256, b * 4)
        return run

    def make_out(j):
        def run(spot):
            loads.wait(attn_l)
            tall = attn.shape[0] // 4
            for b in range(4):
                put(dot_nn(attn[b * tall:(b + 1) * tall, :], gproj[:, j * cols:(j + 1) * cols]), spot, tall // 256, b * 4)
        return run

    def make(lhs, rhs, j):
        def run(spot):
            put(dot_tn(lhs(), rhs[:, j * cols:(j + 1) * cols]), spot, 1, 0)
        return run

    def mlp_all():
        loads.wait(mlp_l)
        return mlp[...]

    def ain_own():
        return ain[second, :]

    def ain_all():
        return ain[...]

    def add_weight(w, subs, maker, count):
        for j in range(count):
            for s in range(subs):
                out = grads[w].at[pl.ds(s * 64, 64), pl.ds(j * cols, cols)]
                todo.append((maker(j) if s == 0 else None, out))

    add_weight(6, hidden.shape[1] // (64 * 16), make_down, width // cols)
    add_weight(4, 1, lambda j: make(mlp_all, ggate, j), ff // cols)
    add_weight(5, 1, lambda j: make(mlp_all, gup, j), ff // cols)
    add_weight(3, attn.shape[0] // (64 * 16), make_out, width // cols)
    add_weight(0, 1, lambda j: make(ain_own, q, j), qh * hd // cols)
    add_weight(1, 1, lambda j: make(ain_all, k, j), kv * hd // cols)
    add_weight(2, 1, lambda j: make(ain_all, v, j), kv * hd // cols)
    kinds, order = plan
    chunks = [Chunk(i, bufs, sems, at, out, *kinds[i]) for i, (_, out) in enumerate(todo)]

    nb = ff // span

    def piece_down(j):
        block = weight(j)
        acc[...] = dot_nt(cot[...], block)
        cc = slice(j * span, (j + 1) * span)
        for part in range(2):
            more = dot_nn(hidden[:, cc], wbuf[j % 2, :, part * rows:(part + 1) * rows])
            rr = pl.ds(part * rows, rows)
            bias[rr, :] = more if j == 0 else bias[rr, :] + more
        used(j)

    def piece_act(j, part):
        cc = slice(j * span, (j + 1) * span)
        loads.wait(gate_l)
        loads.wait(up_l)

        def act(r, n):
            rr = pl.ds(pl.multiple_of(r + part * (rows // 2), n), n)
            gate, up, grad = ggate[rr, cc].astype(f32), gup[rr, cc].astype(f32), acc[rr, :]
            sig = jax.nn.sigmoid(gate)
            ggate[rr, cc] = (grad * up * sig * (1.0 + gate * (1.0 - sig))).astype(bf16)
            gup[rr, cc] = (grad * (gate * sig)).astype(bf16)

        rows_loop(rows // 2, 64, act)

    def piece_output():
        loads.wait(mid_l)
        for part in range(2):
            cc = slice(part * rows, (part + 1) * rows)
            gproj[:, cc] = (mid[:, cc] + bias[part * rows:(part + 1) * rows, :]).astype(bf16)
        later.append(loads.start(gproj, out_o))

    def piece_mlp(j, part):
        n = nb + 2 * j + part
        cc = slice(j * span, (j + 1) * span)
        one = dot_nt((gup if part else ggate)[:, cc], weight(n))
        acc[...] = one if n == nb else acc[...] + one
        used(n)

    def fold(into, terms):
        into[...] += jnp.sum(terms.reshape(terms.shape[0] // 8, 8, terms.shape[1]), axis=0)

    def norm_back(grad, unit, inverse, gain):
        scaled = grad * gain
        return inverse * (scaled - unit * jnp.mean(scaled * unit, axis=-1, keepdims=True))

    def piece_mid(part):
        if part == 0:
            loads.wait(later[0])
            sum_two[...] = jnp.zeros_like(sum_two)

        def body(r, n):
            rr = pl.ds(pl.multiple_of(r + part * (rows // 2), n), n)
            unit, inverse = unit_rows(mid[rr, :])
            grad = acc[rr, :]
            fold(sum_two, grad * unit)
            out = cot[rr, :].astype(f32) + norm_back(grad, unit, inverse, mlp_gain[...])
            mid[rr, :] = out
            gproj[rr, :] = out.astype(bf16)

        rows_loop(rows // 2, 64, body)

    at_out = 3 * nb
    n_out = qh * hd // span

    def piece_attn_grad(j):
        hidden[:, j * span:(j + 1) * span] = dot_nt(gproj[...], weight(at_out + j)).astype(bf16)
        used(at_out + j)

    def piece_ready():
        mask_bias(bias, start, rows)
        sum_q[...] = jnp.zeros_like(sum_q)
        sum_k[...] = jnp.zeros_like(sum_k)
        loads.wait(attn_l)
        for n in head_l:
            loads.wait(n)
        loads.wait(ain_l)

    c2 = scale * log2e
    tile = rows // 2

    def norm_back_heads(grad, unit, inverse, gain):
        scaled = grad * gain
        mean = dot_nn((scaled * unit).astype(bf16), jnp.full((hd, hd), 1.0 / hd, bf16))
        return inverse * (scaled - unit * mean)

    def piece_head(h, g, i):
        cc = slice(h * hd, (h + 1) * hd)
        n = h * group + g
        qc = slice(n * hd, (n + 1) * hd)
        if g == 0 and i == 0:
            kt[...] = k[:, cc].T
            dk[...] = jnp.zeros_like(dk)
            dv[...] = jnp.zeros_like(dv)
        rs = slice(i * tile, (i + 1) * tile)
        kk = rows + (i + 1) * tile
        query, grad = q[rs, qc], hidden[rs, qc]
        delta = jnp.sum(attn[qc, rs].astype(f32) * grad.T.astype(f32), axis=0, keepdims=True)
        p = jnp.exp2(dot_nt(k[:kk, cc], query) * c2 + (bias[:kk, rs] - lse[n:n + 1, rs]))
        gp = dot_nt(v[:kk, cc], grad)
        ds = (p * (gp - delta)).astype(bf16)
        dv[:kk, :] += dot_nn(p.astype(bf16), grad)
        dk[:kk, :] += dot_nn(ds, query)
        dq = dot_nn(kt[:, :kk], ds).T * scale
        unit, inverse = unit_heads(qraw[rs, qc].astype(f32))
        t = slice(rows + i * tile, rows + (i + 1) * tile)
        back = turn_back(dq, cos[t, :], sin[t, :])
        fold(sum_q, back * unit)
        q[rs, qc] = norm_back_heads(back, unit, inverse, query_gain[...]).astype(bf16)

    def piece_keys(h):
        cc = slice(h * hd, (h + 1) * hd)
        for r in range(0, 2 * rows, tile):
            rr = slice(r, r + tile)
            unit, inverse = unit_heads(kraw[rr, cc].astype(f32))
            back = turn_back(dk[rr, :] * scale, cos[rr, :], sin[rr, :])
            fold(sum_k, back * unit)
            k[rr, cc] = norm_back_heads(back, unit, inverse, key_gain[...]).astype(bf16)
            v[rr, cc] = dv[rr, :].astype(bf16)

    at_kv = at_out + n_out
    early_rows = rows // 8

    def handed(n):
        part = pl.ds(n * early_rows, early_rows)
        return pltpu.make_async_remote_copy(
            src_ref=gproj.at[part, :], dst_ref=earlier.at[part, :], send_sem=early_sem.at[0, n], recv_sem=early_sem.at[1, n],
            device_id=(z * 4 + y * 2 + c, 1 - x), device_id_type=MESH)

    def piece_hand(n):
        @pl.when(x == 1)
        def _():
            handed(n).start()

    def piece_queries(j):
        acc[...] += dot_nt(q[:, j * span:(j + 1) * span], weight(at_kv + 2 + j))
        used(at_kv + 2 + j)

    x_in, x_out = mlp, ggate.at[:, pl.ds(0, span)]
    late = []

    def piece_gain():
        loads.wait(late[0])
        sum_one[...] = jnp.zeros_like(sum_one)

        def body(r, n):
            rr = pl.ds(r, n)
            unit, _ = unit_rows(x_in[rr, :].astype(f32))
            fold(sum_one, acc[rr, :] * unit)

        rows_loop(rows, 64, body)

        @pl.when(x == 1)
        def _():
            def more(r, n):
                rr = pl.ds(r, n)
                fold(sum_one, gproj[rr, :].astype(f32) * ain[rr, :].astype(f32) / norm_gain[...])

            rows_loop(rows, 64, more)

        gain_mine[0] = jnp.zeros_like(gain_mine[0])
        gain_mine[0, 0:1, :] = jnp.sum(sum_one[...], axis=0, keepdims=True)
        gain_mine[0, 1:2, :] = jnp.sum(sum_two[...], axis=0, keepdims=True)
        gain_mine[0, 2:3, 0:hd] = jnp.sum(sum_q[...], axis=0, keepdims=True)
        gain_mine[0, 3:4, 0:hd] = jnp.sum(sum_k[...], axis=0, keepdims=True)

    def piece_last():
        @pl.when(x == 0)
        def _():
            for n in range(8):
                handed(n).wait_recv()

            def more(r, n):
                rr = pl.ds(r, n)
                acc[rr, :] += earlier[rr, :].astype(f32)

            rows_loop(rows, 64, more)

        def body(r, n):
            rr = pl.ds(r, n)
            unit, inverse = unit_rows(x_in[rr, :].astype(f32))
            x_out[rr, :] = (mid[rr, :] + norm_back(acc[rr, :], unit, inverse, norm_gain[...])).astype(bf16)

        rows_loop(rows, 64, body)
        loads.start(x_out, gin_o)

    def piece_earlier():
        w_k, w_v = weight(at_kv), weight(at_kv + 1)

        @pl.when(x == 1)
        def _():
            gproj[...] = (dot_nt(k[first, :], w_k) + dot_nt(v[first, :], w_v)).astype(bf16)

    def piece_own():
        acc[...] = dot_nt(k[second, :], wbuf[at_kv % 2]) + dot_nt(v[second, :], wbuf[(at_kv + 1) % 2])
        used(at_kv)
        used(at_kv + 1)
        late.append(loads.start(hid_i, x_in))

    totals = Totals(gain_mine, gain_got, gain_sem, at)
    chain = []
    for j in range(nb):
        chain += [(piece_down, j), (piece_act, j, 0), (piece_act, j, 1)]
    for j in range(nb):
        chain += [(piece_mlp, j, 0), (piece_mlp, j, 1)]
    chain += [(piece_mid, 0), (piece_mid, 1)] + [(piece_attn_grad, j) for j in range(n_out)] + [(piece_ready,)]
    for h in range(kv):
        chain += [(piece_head, h, g, i) for g in range(group) for i in range(2)] + [(piece_keys, h)]
    chain += [(piece_earlier,), (piece_own,)] + [(piece_queries, j) for j in range(n_out)] + [(piece_gain,)]
    chain += [(totals.step, s) for s in range(6)] + [(piece_last,)]
    made, ended = 0, []
    for kind, index, name in order:
        if kind == 0:
            if name == 0:
                if todo[index][0] is not None:
                    todo[index][0](index)
                    if made == 0:
                        head_l = [loads.start(a, b) for a, b in ((q_i, q), (k_i, k), (v_i, v), (qraw_i, qraw), (kraw_i, kraw))]
                        ain_l = loads.start(ain_i, ain)
                        made = 1
                chunks[index].step("go")
            elif name <= 2:
                chunks[index].step(("over_c", "over_x")[name - 1])
            elif name == 8:
                chunks[index].st = bufs[6].at[len(ended) % 2]
                chunks[index].step("finish", ended[-2] if len(ended) > 1 else None)
                ended.append(chunks[index])
            else:
                if name == 3:
                    chunks[index].step("over_y")
                chunks[index].step("over_z", name - 3)
                if name == 6:
                    chunks[index].step("hand")
        elif kind == 1:
            chain[index][0](*chain[index][1:])
            if index == 3 * nb - 1:
                piece_output()
        else:
            piece_hand(index)
    for ch in ended[-2:]:
        ch.o_copy().wait()

    @pl.when(x == 1)
    def _():
        for n in range(8):
            handed(n).wait_send()

    loads.wait_all()
    norm_o[...] = gain_mine[5, 0:1, :]
    mlp_o[...] = gain_mine[5, 1:2, :]
    query_o[...] = gain_mine[5, 2:3, 0:hd]
    key_o[...] = gain_mine[5, 3:4, 0:hd]


def backward(hid, cot, gains, saved, shards):
    rows, width = hid.shape
    full = saved[:7]
    q, k, v, qraw, kraw, ain, attn, lse, mid, mlp, gate, up, hidden, cos, sin, start = saved[7:]
    hd = cos.shape[1]
    shape, vm, dma = jax.ShapeDtypeStruct, pltpu.VMEM, pltpu.SemaphoreType.DMA
    heads, keys, ff = q.shape[1], k.shape[1], gate.shape[1]
    span = keys
    outs = [shape(s.shape, f32) for s in shards] + [
        shape((rows, width), bf16), shape((rows, width), bf16), shape((1, width), f32), shape((1, hd), f32), shape((1, hd), f32), shape((1, width), f32)]
    n = sum(s.shape[0] // 64 * (s.shape[1] // 512) for s in shards)
    return pl.pallas_call(
        functools.partial(backward_kernel, BACKWARD_PLAN),
        out_shape=outs,
        in_specs=[VMEM] * 9 + [HBM] * 20,
        out_specs=[HBM] * 9 + [VMEM] * 4,
        scratch_shapes=[
            vm((rows, ff), bf16), vm((rows, width), bf16), vm((rows, ff), bf16), vm((rows, ff), bf16), vm((rows, width), f32), vm((rows, width), f32),
            vm((rows, width), bf16), vm((heads, rows), bf16), vm((rows, heads), bf16), vm((2 * rows, keys), bf16), vm((2 * rows, keys), bf16),
            vm((rows, heads), bf16), vm((2 * rows, keys), bf16), vm((2 * rows, width), bf16), vm((2 * rows, hd), f32), vm((2 * rows, hd), f32),
            vm((hd, 2 * rows), bf16), vm((2 * rows, rows), f32), vm((2, span, span), bf16), vm((rows, width), bf16),
            vm((8, width), f32), vm((8, width), f32), vm((8, hd), f32), vm((8, hd), f32), vm((6, 8, width), f32), vm((5, 8, width), f32),
            dma((5, 2)), dma((24,)), dma((2,)), dma((2, 8))] + chunk_bufs(64, 512) + chunk_sems(n),
        compiler_params=pltpu.CompilerParams(collective_id=2, has_side_effects=True, vmem_limit_bytes=63 * 2**20),
        name="backward_reduce",
    )(cot, cos, sin, start, *gains, lse, *full, hid, q, k, v, qraw, kraw, ain, attn, mid, mlp, gate, up, hidden)


def place_kernel(*refs):
    n = len(refs) // 2
    copies = [pltpu.make_async_copy(refs[i], refs[n + i], refs[-1].at[i]) for i in range(n)]
    for copy in copies:
        copy.start()
    for copy in copies:
        copy.wait()


def placed(arrays):
    n = len(arrays)
    return pl.pallas_call(
        place_kernel,
        out_shape=[jax.ShapeDtypeStruct(a.shape, a.dtype) for a in arrays],
        in_specs=[HBM] * n,
        out_specs=[HBM] * n,
        scratch_shapes=[pltpu.SemaphoreType.DMA((n,))],
        name="place_results",
    )(*arrays)


def as_sent(shard):

    def short(part):
        return part.astype(jnp.bfloat16) if part.dtype == jnp.float32 else part

    return jax.tree.map(short, shard)


def norm_rows(values, gain_vec):
    inverse = lax.rsqrt(jnp.mean(values * values, axis=-1, keepdims=True) + epsilon)
    normed = values * inverse
    return (normed * gain_vec, normed, inverse)


def norm_back(grad_out, gain_vec, normed, inverse):
    scaled = grad_out * gain_vec
    grad_in = inverse * (scaled - normed * jnp.mean(scaled * normed, axis=-1, keepdims=True))
    return (grad_in, grad_out * normed)


def rope_tables(positions, head_dim):
    frequency = theta_base ** (-jnp.arange(0, head_dim, 2).astype(jnp.float32) / head_dim)
    angles = positions.astype(jnp.float32)[:, None] * frequency[None, :]
    angles = jnp.concatenate([angles, angles], axis=-1)
    return (jnp.cos(angles), jnp.sin(angles))


def rotate(values, cosine, sine_tab):
    half_dim = values.shape[-1] // 2
    turned = jnp.concatenate([-values[..., half_dim:], values[..., :half_dim]], axis=-1)
    return values * cosine[:, None, :] + turned * sine_tab[:, None, :]


def rotate_back(grad_out, cosine, sine_tab):
    half_dim = grad_out.shape[-1] // 2
    weighted = grad_out * sine_tab[:, None, :]
    turned = jnp.concatenate([weighted[..., half_dim:], -weighted[..., :half_dim]], axis=-1)
    return grad_out * cosine[:, None, :] + turned


def back_dot(grad_rows, weight):
    return lax.dot_general(
        grad_rows, weight, (((1,), (1,)), ((), ())), preferred_element_type=jnp.float32
    )


def weight_term(acts_in, grad_out):
    return lax.dot_general(
        acts_in, grad_out, (((0,), (0,)), ((), ())), preferred_element_type=jnp.float32
    )


def per_device(
    hidden_in,
    positions,
    cotangent,
    norm_gain,
    w_query,
    w_key,
    w_value,
    query_gain,
    key_gain,
    w_out,
    mlp_gain,
    w_gate,
    w_up,
    w_down,
):
    seqs_here, block_len, model_width = hidden_in.shape
    head_dim = query_gain.shape[0]
    kv_heads = w_key.shape[1] // head_dim
    q_heads = w_query.shape[1] // head_dim
    groups = q_heads // kv_heads
    ctx_count = lax.axis_size("ctx")
    ctx_rank = lax.axis_index("ctx")
    seq_total = block_len * ctx_count
    row_count = seqs_here * block_len
    scale_val = head_dim ** (-0.5)
    shards = (w_query, w_key, w_value, w_out, w_gate, w_up, w_down)
    full_weights = (
        lax.all_gather(shards[0], "fsdp", axis=0, tiled=True),
        lax.all_gather(shards[1], "fsdp", axis=0, tiled=True),
        lax.all_gather(shards[2], "fsdp", axis=0, tiled=True),
        lax.all_gather(shards[3], "fsdp", axis=0, tiled=True),
        lax.all_gather(shards[4], "fsdp", axis=0, tiled=True),
        lax.all_gather(shards[5], "fsdp", axis=0, tiled=True),
        lax.all_gather(shards[6], "fsdp", axis=0, tiled=True),
    )
    full_query, full_key, full_value, full_out, full_gate, full_up, full_down = full_weights
    residual = hidden_in.astype(jnp.float32).reshape(row_count, model_width)
    scaled_one, normed_one, inverse_one = norm_rows(residual, norm_gain)
    attn_in = scaled_one.astype(jnp.bfloat16)
    query_raw = jnp.dot(attn_in, full_query, preferred_element_type=jnp.float32).reshape(
        row_count, q_heads, head_dim
    )
    key_raw = jnp.dot(attn_in, full_key, preferred_element_type=jnp.float32).reshape(
        row_count, kv_heads, head_dim
    )
    value_bf = jnp.dot(attn_in, full_value, preferred_element_type=jnp.float32).astype(jnp.bfloat16)
    flat_pos = positions.reshape(row_count)
    cosine, sine_tab = rope_tables(flat_pos, head_dim)
    query_scaled, query_normed, query_inverse = norm_rows(query_raw, query_gain)
    query_bf = rotate(query_scaled, cosine, sine_tab).astype(jnp.bfloat16)
    key_scaled, key_normed, key_inverse = norm_rows(key_raw, key_gain)
    key_bf = rotate(key_scaled, cosine, sine_tab).astype(jnp.bfloat16)
    key_flat = key_bf.reshape(seqs_here, block_len, kv_heads * head_dim)
    value_flat = value_bf.reshape(seqs_here, block_len, kv_heads * head_dim)
    keys_all, values_all = (
        lax.all_gather(key_flat, "ctx", axis=1, tiled=True),
        lax.all_gather(value_flat, "ctx", axis=1, tiled=True),
    )
    query_five = query_bf.reshape(seqs_here, block_len, kv_heads, groups, head_dim)
    query_index = ctx_rank * block_len + jnp.arange(block_len, dtype=jnp.int32)
    doc_start = query_index[None, :] - positions

    def block_scores(key_source, block_idx):
        key_block = lax.dynamic_slice_in_dim(key_source, block_idx * block_len, block_len, 1)
        scores = (
            jnp.einsum(
                "sqkgd,spkd->skgqp", query_five, key_block, preferred_element_type=jnp.float32
            )
            * scale_val
        )
        key_index = block_idx * block_len + jnp.arange(block_len, dtype=jnp.int32)
        allowed = (key_index[None, None, :] <= query_index[None, :, None]) & (
            key_index[None, None, :] >= doc_start[:, :, None]
        )
        return (jnp.where(allowed[:, None, None, :, :], scores, -1e30), key_block)

    keys_four = keys_all.reshape(seqs_here, seq_total, kv_heads, head_dim)
    values_four = values_all.reshape(seqs_here, seq_total, kv_heads, head_dim)

    def stats_step(block_idx, carry_stats):
        running_max, running_sum = carry_stats
        scores, key_block = block_scores(keys_four, block_idx)
        new_max = jnp.maximum(running_max, jnp.max(scores, axis=-1))
        running_sum = running_sum * jnp.exp(running_max - new_max) + jnp.sum(
            jnp.exp(scores - new_max[..., None]), axis=-1
        )
        return (new_max, running_sum)

    stat_shape = (seqs_here, kv_heads, groups, block_len)
    row_max, row_sum = lax.fori_loop(
        0,
        ctx_rank + 1,
        stats_step,
        (jnp.full(stat_shape, -1e30, jnp.float32), jnp.zeros(stat_shape, jnp.float32)),
    )

    def output_step(block_idx, accum):
        scores, key_block = block_scores(keys_four, block_idx)
        probs_bf = (jnp.exp(scores - row_max[..., None]) / row_sum[..., None]).astype(jnp.bfloat16)
        value_block = lax.dynamic_slice_in_dim(values_four, block_idx * block_len, block_len, 1)
        return accum + jnp.einsum(
            "skgqp,spkd->sqkgd", probs_bf, value_block, preferred_element_type=jnp.float32
        )

    attn_f32 = lax.fori_loop(
        0,
        ctx_rank + 1,
        output_step,
        jnp.zeros((seqs_here, block_len, kv_heads, groups, head_dim), jnp.float32),
    )
    attn_bf = attn_f32.reshape(row_count, q_heads * head_dim).astype(jnp.bfloat16)
    middle = residual + jnp.dot(attn_bf, full_out, preferred_element_type=jnp.float32)
    scaled_two, normed_two, inverse_two = norm_rows(middle, mlp_gain)
    mlp_in = scaled_two.astype(jnp.bfloat16)
    gate_pre = jnp.dot(mlp_in, full_gate, preferred_element_type=jnp.float32)
    up_pre = jnp.dot(mlp_in, full_up, preferred_element_type=jnp.float32)
    sigmoid_gate = jax.nn.sigmoid(gate_pre)
    silu_gate = gate_pre * sigmoid_gate
    hidden_bf = (silu_gate * up_pre).astype(jnp.bfloat16)
    layer_out = middle + jnp.dot(hidden_bf, full_down, preferred_element_type=jnp.float32)
    output = layer_out.astype(jnp.bfloat16).reshape(seqs_here, block_len, model_width)
    back_weights = full_weights
    keys_back, values_back = (
        lax.all_gather(key_flat, "ctx", axis=1, tiled=True),
        lax.all_gather(value_flat, "ctx", axis=1, tiled=True),
    )
    back_query, back_key, back_value, back_out, back_gate, back_up, back_down = back_weights
    keys_again = keys_back.reshape(seqs_here, seq_total, kv_heads, head_dim)
    values_again = values_back.reshape(seqs_here, seq_total, kv_heads, head_dim)
    grad_rows = cotangent.reshape(row_count, model_width)
    down_grad = back_dot(grad_rows, back_down)
    grad_gate = (
        down_grad * up_pre * sigmoid_gate * (1.0 + gate_pre * (1.0 - sigmoid_gate))
    ).astype(jnp.bfloat16)
    grad_up = (down_grad * silu_gate).astype(jnp.bfloat16)
    grad_mlp_in = back_dot(grad_gate, back_gate) + back_dot(grad_up, back_up)
    grad_norm_two, mlp_gain_terms = norm_back(grad_mlp_in, mlp_gain, normed_two, inverse_two)
    grad_mid = grad_rows.astype(jnp.float32) + grad_norm_two
    grad_proj = grad_mid.astype(jnp.bfloat16)
    grad_attn = back_dot(grad_proj, back_out).astype(jnp.bfloat16)
    grad_five = grad_attn.reshape(seqs_here, block_len, kv_heads, groups, head_dim)
    delta = jnp.einsum("sqkgd,sqkgd->skgq", grad_five.astype(jnp.float32), attn_f32)

    def grad_step(block_idx, carry_grads):
        grad_query, grad_keys, grad_values = carry_grads
        scores, key_block = block_scores(keys_again, block_idx)
        probs = jnp.exp(scores - row_max[..., None]) / row_sum[..., None]
        value_block = lax.dynamic_slice_in_dim(values_again, block_idx * block_len, block_len, 1)
        grad_probs = jnp.einsum(
            "sqkgd,spkd->skgqp", grad_five, value_block, preferred_element_type=jnp.float32
        )
        grad_scores = (probs * (grad_probs - delta[..., None])).astype(jnp.bfloat16)
        grad_query = (
            grad_query
            + jnp.einsum(
                "skgqp,spkd->sqkgd", grad_scores, key_block, preferred_element_type=jnp.float32
            )
            * scale_val
        )
        key_part = (
            jnp.einsum(
                "skgqp,sqkgd->spkd", grad_scores, query_five, preferred_element_type=jnp.float32
            )
            * scale_val
        )
        value_part = jnp.einsum(
            "skgqp,sqkgd->spkd",
            probs.astype(jnp.bfloat16),
            grad_five,
            preferred_element_type=jnp.float32,
        )
        grad_keys = lax.dynamic_update_slice_in_dim(grad_keys, key_part, block_idx * block_len, 1)
        grad_values = lax.dynamic_update_slice_in_dim(
            grad_values, value_part, block_idx * block_len, 1
        )
        return (grad_query, grad_keys, grad_values)

    whole_shape = (seqs_here, seq_total, kv_heads, head_dim)
    grad_query, grad_keys, grad_values = lax.fori_loop(
        0,
        ctx_rank + 1,
        grad_step,
        (
            jnp.zeros((seqs_here, block_len, kv_heads, groups, head_dim), jnp.float32),
            jnp.zeros(whole_shape, jnp.float32),
            jnp.zeros(whole_shape, jnp.float32),
        ),
    )
    key_grad_own, value_grad_own = (
        lax.psum_scatter(
            grad_keys.reshape(seqs_here, seq_total, kv_heads * head_dim).astype(jnp.bfloat16),
            "ctx",
            scatter_dimension=1,
            tiled=True,
        ).astype(jnp.float32),
        lax.psum_scatter(
            grad_values.reshape(seqs_here, seq_total, kv_heads * head_dim).astype(jnp.bfloat16),
            "ctx",
            scatter_dimension=1,
            tiled=True,
        ).astype(jnp.float32),
    )
    key_unrot = rotate_back(key_grad_own.reshape(row_count, kv_heads, head_dim), cosine, sine_tab)
    key_raw_grad, key_gain_terms = norm_back(key_unrot, key_gain, key_normed, key_inverse)
    key_raw_bf = key_raw_grad.reshape(row_count, kv_heads * head_dim).astype(jnp.bfloat16)
    query_unrot = rotate_back(grad_query.reshape(row_count, q_heads, head_dim), cosine, sine_tab)
    query_raw_grad, query_gain_terms = norm_back(
        query_unrot, query_gain, query_normed, query_inverse
    )
    query_raw_bf = query_raw_grad.reshape(row_count, q_heads * head_dim).astype(jnp.bfloat16)
    value_raw_bf = value_grad_own.reshape(row_count, kv_heads * head_dim).astype(jnp.bfloat16)
    grad_attn_in = (
        back_dot(query_raw_bf, back_query)
        + back_dot(key_raw_bf, back_key)
        + back_dot(value_raw_bf, back_value)
    )
    grad_norm_one, norm_gain_terms = norm_back(grad_attn_in, norm_gain, normed_one, inverse_one)
    grad_input = (
        (grad_mid + grad_norm_one).astype(jnp.bfloat16).reshape(seqs_here, block_len, model_width)
    )
    gain_one, gain_query, gain_key, gain_two = lax.psum(
        (
            jnp.sum(norm_gain_terms, axis=0),
            jnp.sum(query_gain_terms, axis=(0, 1)),
            jnp.sum(key_gain_terms, axis=(0, 1)),
            jnp.sum(mlp_gain_terms, axis=0),
        ),
        ("fsdp", "ctx"),
    )
    weight_pairs = (
        (attn_in, query_raw_bf),
        (attn_in, key_raw_bf),
        (attn_in, value_raw_bf),
        (attn_bf, grad_proj),
        (mlp_in, grad_gate),
        (mlp_in, grad_up),
        (hidden_bf, grad_rows),
    )
    pieces = tuple(
        (
            lax.psum_scatter(
                weight_term(acts_in, grad_out).astype(jnp.bfloat16),
                "fsdp",
                scatter_dimension=0,
                tiled=True,
            ).astype(jnp.float32)
            for acts_in, grad_out in weight_pairs
        )
    )
    weight_grads = jax.tree.map(
        lambda part: part.astype(jnp.float32), lax.psum(as_sent(pieces), "ctx")
    )
    grad_wq, grad_wk, grad_wv, grad_wo, grad_wg, grad_wu, grad_wd = weight_grads
    return (
        output,
        grad_input,
        gain_one,
        grad_wq,
        grad_wk,
        grad_wv,
        gain_query,
        gain_key,
        grad_wo,
        gain_two,
        grad_wg,
        grad_wu,
        grad_wd,
    )


def grid_device(hidden_in, positions, cotangent, norm_gain, w_query, w_key, w_value, query_gain, key_gain, w_out, mlp_gain, w_gate, w_up, w_down):
    rows, width = hidden_in.shape[1:]
    head_dim = query_gain.shape[0]
    hid, cot = hidden_in.reshape(rows, width), cotangent.reshape(rows, width)
    half = theta_base ** (-np.arange(0, head_dim, 2) / head_dim)
    freq = jnp.asarray(np.concatenate([half, half])[None], jnp.float32)
    gains = [g[None, :] for g in (norm_gain, query_gain, key_gain, mlp_gain)]
    shards = (w_query, w_key, w_value, w_out, w_gate, w_up, w_down)
    saved = forward(hid, positions, freq, gains, shards)
    done = placed(backward(hid, cot, gains, saved, shards))
    gq, gk, gv, go, gg, gu, gd, out, grad_in, norm, query, key, mlp = done
    return (out[None], grad_in[None], norm[0], gq, gk, gv, query[0], key[0], go, mlp[0], gg, gu, gd)


def is_grid(mesh):
    if dict(mesh.shape) != {"fsdp": 16, "ctx": 2}:
        return False
    for f in range(16):
        for x in range(2):
            device = mesh.devices[f, x]
            if tuple(device.coords) != (x, (f // 2) % 2, f // 4) or device.core_on_chip != f % 2:
                return False
    return True


def solution(mesh):
    in_specs = (
        P("fsdp", "ctx", None),
        P("fsdp", "ctx"),
        P("fsdp", "ctx", None),
        P(),
        P("fsdp", None),
        P("fsdp", None),
        P("fsdp", None),
        P(),
        P(),
        P("fsdp", None),
        P(),
        P("fsdp", None),
        P("fsdp", None),
        P("fsdp", None),
    )
    out_specs = (
        P("fsdp", "ctx", None),
        P("fsdp", "ctx", None),
        P(),
        P("fsdp", None),
        P("fsdp", None),
        P("fsdp", None),
        P(),
        P(),
        P("fsdp", None),
        P(),
        P("fsdp", None),
        P("fsdp", None),
        P("fsdp", None),
    )
    return jax.shard_map(
        grid_device if is_grid(mesh) else per_device, mesh=mesh, in_specs=in_specs, out_specs=out_specs, check_vma=False
    )
```

```python
import functools

import jax
import jax.numpy as jnp
import numpy as np
from jax import lax
from jax.experimental import pallas as pl
from jax.experimental.pallas import tpu as pltpu
from jax.sharding import PartitionSpec as P

MESH = pl.DeviceIdType.MESH

epsilon = 1e-06
theta_base = 1000000.0
log2e = 1.4426950408889634
bf16, f32 = jnp.bfloat16, jnp.float32
HBM = pl.BlockSpec(memory_space=pl.ANY)
VMEM = pl.BlockSpec(memory_space=pltpu.VMEM)

FORWARD_PLAN = (
    ((1, 16, 3, 6), (1, 8, 3, 3), (1, 8, 2, 2), (1, 8, 3, 3), (1, 24, 7, 8), (1, 24, 9, 9), (0, 12, 4, 3)),
    (0, 2, 9, 10, 17, 13, 24),
    (0, 2, 4, 6, 5, 7, 9, 9, 11, 11, 12, 12, 12),
    (1, 0, 13, 0, 0, 7, 6, 2, 3, 0, 1, 1, 0, 1, 7, 1, 0, 3, 0, 3, 0, 2, 0, 1, 0, 1, 0, 0, 2, 2, 0, 36, 25, 3, 8, 20),
    2,
    4,
)

BACKWARD_PLAN = (
    ((1, 1), (1, 1), (1, 1), (1, 1), (1, 1), (1, 1), (1, 1), (1, 1), (1, 1), (1, 1), (1, 1), (1, 1), (1, 1), (1, 1), (1, 1), (1, 1), (1, 1), (1, 1), (1, 1), (1, 1), (1, 1), (1, 1), (1, 1), (1, 1), (1, 1), (1, 1), (0, 0), (0, 0), (0, 0), (0, 0)),
    (
        (0, 0, 0), (1, 0, 0), (1, 1, 0), (0, 0, 1), (1, 2, 0), (0, 1, 0), (0, 2, 0), (1, 3, 0), (0, 0, 2), (0, 1, 1),
        (0, 3, 0), (1, 4, 0), (0, 2, 1), (0, 1, 2), (1, 5, 0), (0, 3, 1), (0, 4, 0), (1, 6, 0), (0, 2, 2), (0, 0, 3),
        (1, 7, 0), (0, 5, 0), (1, 8, 0), (0, 1, 3), (0, 4, 1), (0, 3, 2), (1, 9, 0), (0, 5, 1), (0, 6, 0), (1, 10, 0),
        (0, 4, 2), (0, 0, 4), (0, 2, 3), (0, 7, 0), (0, 6, 1), (1, 11, 0), (0, 1, 4), (1, 12, 0), (0, 5, 2), (0, 7, 1),
        (0, 2, 4), (0, 0, 5), (1, 13, 0), (0, 3, 3), (0, 4, 3), (0, 6, 2), (0, 1, 5), (0, 8, 0), (1, 14, 0), (0, 9, 0),
        (0, 0, 6), (0, 8, 1), (0, 2, 5), (0, 3, 4), (0, 1, 6), (1, 15, 0), (1, 16, 0), (0, 4, 4), (0, 5, 3), (0, 9, 1),
        (1, 17, 0), (0, 7, 2), (0, 6, 3), (0, 3, 5), (0, 8, 2), (0, 0, 8), (0, 2, 6), (0, 10, 0), (0, 4, 5), (0, 5, 4),
        (1, 18, 0), (1, 19, 0), (0, 5, 5), (0, 1, 8), (0, 3, 6), (1, 20, 0), (0, 4, 6), (0, 9, 2), (0, 11, 0), (0, 10, 1),
        (0, 7, 3), (0, 6, 4), (1, 21, 0), (0, 2, 8), (0, 12, 0), (0, 3, 8), (1, 22, 0), (0, 8, 3), (0, 11, 1), (1, 23, 0),
        (1, 24, 0), (0, 6, 5), (0, 7, 4), (0, 12, 1), (0, 10, 2), (1, 25, 0), (0, 5, 6), (0, 13, 0), (0, 4, 8), (1, 26, 0),
        (0, 7, 5), (0, 9, 3), (0, 11, 2), (0, 8, 4), (0, 14, 0), (1, 27, 0), (1, 28, 0), (0, 6, 6), (0, 7, 6), (0, 9, 4),
        (0, 10, 3), (0, 5, 8), (0, 8, 5), (0, 14, 1), (0, 13, 1), (1, 29, 0), (0, 15, 0), (0, 12, 2), (1, 30, 0), (1, 31, 0),
        (0, 9, 5), (0, 11, 3), (0, 6, 8), (1, 32, 0), (0, 8, 6), (0, 10, 4), (0, 16, 0), (0, 15, 1), (0, 14, 2), (1, 33, 0),
        (0, 7, 8), (1, 34, 0), (0, 9, 6), (0, 12, 3), (0, 10, 5), (1, 35, 0), (1, 36, 0), (0, 8, 8), (0, 11, 4), (0, 13, 2),
        (0, 17, 0), (0, 16, 1), (1, 37, 0), (0, 10, 6), (1, 38, 0), (1, 39, 0), (0, 11, 5), (0, 9, 8), (0, 12, 4), (0, 15, 2),
        (0, 18, 0), (0, 14, 3), (1, 40, 0), (0, 11, 6), (0, 12, 5), (0, 17, 1), (1, 41, 0), (0, 16, 2), (0, 19, 0), (0, 13, 3),
        (1, 42, 0), (0, 10, 8), (1, 43, 0), (0, 14, 4), (0, 18, 1), (1, 44, 0), (0, 15, 3), (0, 11, 8), (0, 17, 2), (1, 45, 0),
        (0, 19, 1), (0, 13, 4), (0, 20, 0), (0, 18, 2), (0, 21, 0), (0, 15, 4), (1, 46, 0), (0, 16, 3), (0, 12, 6), (1, 47, 0),
        (0, 20, 1), (0, 13, 5), (0, 16, 4), (1, 48, 0), (1, 49, 0), (0, 13, 6), (0, 20, 2), (0, 16, 5), (0, 17, 3), (1, 50, 0),
        (0, 21, 1), (0, 15, 5), (1, 51, 0), (0, 19, 2), (1, 52, 0), (0, 12, 8), (0, 14, 5), (0, 22, 0), (1, 53, 0), (0, 18, 3),
        (0, 21, 2), (0, 13, 8), (1, 54, 0), (0, 23, 0), (0, 14, 6), (0, 22, 1), (1, 55, 0), (0, 17, 4), (0, 15, 6), (1, 56, 0),
        (0, 18, 4), (0, 19, 3), (1, 57, 0), (0, 23, 1), (0, 14, 8), (0, 22, 2), (0, 24, 0), (0, 17, 5), (1, 58, 0), (0, 20, 3),
        (1, 59, 0), (0, 19, 4), (0, 18, 5), (0, 16, 6), (0, 15, 8), (0, 23, 2), (0, 24, 1), (0, 25, 0), (0, 21, 3), (0, 17, 6),
        (1, 60, 0), (0, 25, 1), (0, 18, 6), (0, 20, 4), (0, 19, 5), (0, 24, 2), (0, 16, 8), (0, 17, 8), (0, 21, 4), (0, 22, 3),
        (0, 22, 4), (0, 20, 5), (0, 25, 2), (0, 26, 0), (0, 21, 5), (0, 19, 6), (2, 0, 0), (0, 23, 3), (0, 27, 0), (0, 24, 3),
        (0, 21, 6), (0, 20, 6), (0, 23, 4), (0, 26, 1), (2, 1, 0), (0, 22, 5), (0, 27, 1), (1, 61, 0), (0, 25, 3), (0, 18, 8),
        (2, 2, 0), (0, 19, 8), (0, 28, 0), (0, 24, 4), (0, 25, 4), (1, 62, 0), (1, 63, 0), (0, 26, 3), (2, 3, 0), (2, 4, 0),
        (0, 20, 8), (0, 24, 5), (0, 23, 5), (0, 29, 0), (0, 21, 8), (0, 22, 6), (1, 64, 0), (0, 29, 1), (0, 26, 4), (1, 65, 0),
        (0, 24, 6), (0, 23, 6), (1, 66, 0), (0, 27, 3), (0, 25, 5), (0, 25, 6), (0, 28, 1), (2, 5, 0), (2, 6, 0), (0, 27, 4),
        (2, 7, 0), (0, 24, 8), (0, 27, 5), (0, 26, 5), (0, 29, 3), (0, 29, 4), (0, 26, 6), (1, 67, 0), (0, 23, 8), (0, 29, 5),
        (0, 27, 6), (0, 28, 3), (0, 25, 8), (0, 22, 8), (1, 68, 0), (0, 28, 4), (0, 29, 6), (1, 69, 0), (0, 28, 5), (1, 71, 0),
        (0, 28, 6), (0, 27, 8), (1, 70, 0), (0, 26, 8), (0, 29, 8), (0, 28, 8),
    ),
)


def place():
    f = lax.axis_index("fsdp")
    return f // 4, (f // 2) % 2, f % 2, lax.axis_index("ctx")


def enter(z, y, c, x, ends=False):
    bar = pltpu.get_barrier_semaphore()

    def hail(z2, y2, c2, x2):
        pl.semaphore_signal(bar, inc=1, device_id=(z2 * 4 + y2 * 2 + c2, x2), device_id_type=MESH)

    hail(z, y, c, 1 - x)
    hail(z, 1 - y, c, x)
    hail(z, y, 1 - c, x)

    @pl.when(z > 0)
    def _():
        hail(z - 1, y, c, x)

    @pl.when(z < 3)
    def _():
        hail(z + 1, y, c, x)

    if ends:
        @pl.when(z % 3 == 0)
        def _():
            hail(3 - z, y, c, x)

    pl.semaphore_wait(bar, 5 if ends else 4 + (z * (3 - z)) // 2)


class Gather:
    def __init__(self, index, own, full, sems, at, cut):
        self.g, self.own, self.full = index, own, full
        self.zr, self.yr, self.xr, self.cr, self.zs, self.ys, self.xs, self.cs, self.ls = sems
        self.z, self.y, self.c, self.x = at
        self.rows, self.cols = own.shape
        self.dim, units, ones, twos = cut
        step = own.shape[self.dim] // units
        low, middle, high = (0, ones * step), (ones * step, (units - twos - ones) * step), ((units - twos) * step, twos * step)
        self.plans = ((0, low[1] + middle[1]), low, high), ((low[1], middle[1] + high[1]), high, low)
        self.all = None

    def step(self, name, *args):
        for x in (0, 1):
            @pl.when(self.x == x)
            def _():
                self.ywin, self.xwin, self.xgot = self.plans[x]
                getattr(self, name)(*args)

    def window(self, ref, row, win):
        if win is None:
            return ref.at[pl.ds(row, self.rows), :]
        if self.dim == 0:
            return ref.at[pl.ds(row + win[0], win[1]), :]
        return ref.at[pl.ds(row, self.rows), pl.ds(*win)]

    def part(self, z2, y2, c2, win):
        f2 = z2 * 4 + y2 * 2 + c2
        return self.window(self.full, pl.multiple_of(f2 * self.rows, 16), win)

    def mine(self):
        return self.window(self.own, 0, self.ywin)

    def send(self, src, dst, ssem, rsem, to):
        z2, y2, c2, x2 = to
        return pltpu.make_async_remote_copy(
            src_ref=src, dst_ref=dst, send_sem=ssem, recv_sem=rsem,
            device_id=(z2 * 4 + y2 * 2 + c2, x2), device_id_type=MESH)

    def z_copy(self, zs, up, first):
        dst = self.part(zs, self.y, self.c, self.ywin)
        src = self.mine() if first else dst
        z2 = self.z + 1 if up else self.z - 1
        return self.send(src, dst, self.zs.at[self.g, zs, 1 if up else 0], self.zr.at[self.g, zs], (z2, self.y, self.c, self.x))

    def y_copy(self, zs, first):
        dst = self.part(zs, self.y, self.c, self.ywin)
        src = self.mine() if first else dst
        return self.send(src, dst, self.ys.at[self.g, zs], self.yr.at[self.g, zs], (self.z, 1 - self.y, self.c, self.x))

    def x_copy(self, zs, y2):
        dst = self.part(zs, y2, self.c, self.xwin)
        s = zs * 2 + y2
        return self.send(dst, dst, self.xs.at[self.g, s], self.xr.at[self.g, s], (self.z, self.y, self.c, 1 - self.x))

    def c_copy(self, zs, y2, win, piece, first=False):
        dst = self.part(zs, y2, self.c, win)
        src = self.own if first else dst
        s = (zs * 2 + y2) * 2 + piece
        return self.send(src, dst, self.cs.at[self.g, s], self.cr.at[self.g, s], (self.z, self.y, 1 - self.c, self.x))

    def await_(self, dst, sem):
        pltpu.make_async_copy(dst, dst, sem).wait()

    def local(self):
        return pltpu.make_async_copy(self.own, self.part(self.z, self.y, self.c, self.all), self.ls.at[self.g])

    def begin(self):
        z = self.z

        @pl.when(z < 3)
        def _():
            self.z_copy(z, True, True).start()

        @pl.when(z > 0)
        def _():
            self.z_copy(z, False, True).start()

        self.y_copy(z, True).start()
        self.c_copy(z, self.y, self.all, 0, True).start()
        self.local().start()

    def spread(self, zs, up):
        self.await_(self.part(zs, self.y, self.c, self.ywin), self.zr.at[self.g, zs])

        @pl.when(self.z < 3 if up else self.z > 0)
        def _():
            self.z_copy(zs, up, False).start()

        self.y_copy(zs, False).start()
        self.x_copy(zs, self.y).start()
        self.c_copy(zs, self.y, self.ywin, 0).start()

    def along_z(self, k):
        @pl.when(self.z >= k)
        def _():
            self.spread(self.z - k, True)

        @pl.when(self.z + k <= 3)
        def _():
            self.spread(self.z + k, False)

    def over_y(self, zs):
        self.await_(self.part(zs, 1 - self.y, self.c, self.ywin), self.yr.at[self.g, zs])
        self.x_copy(zs, 1 - self.y).start()
        self.c_copy(zs, 1 - self.y, self.ywin, 0).start()

    def along_y(self, k):
        if k == 0:
            self.over_y(self.z)
            return

        @pl.when(self.z >= k)
        def _():
            self.over_y(self.z - k)

        @pl.when(self.z + k <= 3)
        def _():
            self.over_y(self.z + k)

    def over_x(self, zs, y2):
        self.await_(self.part(zs, y2, self.c, self.xgot), self.xr.at[self.g, zs * 2 + y2])
        self.c_copy(zs, y2, self.xgot, 1).start()

    def along_x(self, k):
        if k == 0:
            self.over_x(self.z, 1 - self.y)
            return

        for y2 in (self.y, 1 - self.y):
            @pl.when(self.z >= k)
            def _():
                self.over_x(self.z - k, y2)

            @pl.when(self.z + k <= 3)
            def _():
                self.over_x(self.z + k, y2)

    def finish(self):
        z, y = self.z, self.y
        self.local().wait()
        c = 1 - self.c
        self.await_(self.part(z, y, c, self.all), self.cr.at[self.g, (z * 2 + y) * 2])
        for k in range(0, 4):
            for y2 in ((y, 1 - y) if k else (1 - y,)):
                for zs, ok in ((z - k, z >= k), (z + k, z + k <= 3))[: 2 if k else 1]:
                    @pl.when(ok)
                    def _():
                        s = (zs * 2 + y2) * 2
                        self.await_(self.part(zs, y2, c, self.ywin), self.cr.at[self.g, s])
                        self.await_(self.part(zs, y2, c, self.xgot), self.cr.at[self.g, s + 1])

    def drain(self):
        z, y = self.z, self.y

        @pl.when(z < 3)
        def _():
            self.z_copy(z, True, True).wait_send()

        @pl.when(z > 0)
        def _():
            self.z_copy(z, False, True).wait_send()

        self.y_copy(z, True).wait_send()
        self.c_copy(z, y, self.all, 0, True).wait_send()
        self.x_copy(z, 1 - y).wait_send()
        self.c_copy(z, 1 - y, self.ywin, 0).wait_send()
        self.c_copy(z, 1 - y, self.xgot, 1).wait_send()
        for k in range(1, 4):
            for zs, ok, more, up in ((z - k, z >= k, z < 3, True), (z + k, z + k <= 3, z > 0, False)):
                @pl.when(ok)
                def _():
                    @pl.when(more)
                    def _():
                        self.z_copy(zs, up, False).wait_send()

                    self.y_copy(zs, False).wait_send()
                    for y2 in (y, 1 - y):
                        self.x_copy(zs, y2).wait_send()
                        self.c_copy(zs, y2, self.ywin, 0).wait_send()
                        self.c_copy(zs, y2, self.xgot, 1).wait_send()


def gather_sems(n):
    return [pltpu.SemaphoreType.DMA(s) for s in ((n, 4), (n, 4), (n, 8), (n, 16), (n, 4, 2), (n, 4), (n, 8), (n, 16), (n,))]


def dot_nn(a, b):
    return lax.dot_general(a, b, (((1,), (0,)), ((), ())), preferred_element_type=f32)


def dot_nt(a, b):
    return lax.dot_general(a, b, (((1,), (1,)), ((), ())), preferred_element_type=f32)


def dot_tn(a, b):
    return lax.dot_general(a, b, (((0,), (0,)), ((), ())), preferred_element_type=f32)


def rows_loop(count, step, body):
    @pl.loop(0, count // step)
    def _(i):
        body(pl.multiple_of(i * step, step), step)


class Writes:
    def __init__(self, sem):
        self.sem, self.all, self.open = sem, [], set()

    def start(self, src, dst):
        copy = pltpu.make_async_copy(src, dst, self.sem.at[len(self.all)])
        copy.start()
        self.open.add(len(self.all))
        self.all.append(copy)
        return len(self.all) - 1

    def wait(self, i):
        if i in self.open:
            self.all[i].wait()
            self.open.remove(i)

    def wait_all(self):
        for i in sorted(self.open):
            self.wait(i)


def unit_heads(values):
    size = values.shape[-1]
    mean = dot_nn((values * values).astype(bf16), jnp.full((size, size), 1.0 / size, bf16))
    inverse = lax.rsqrt(mean + epsilon)
    return values * inverse, inverse


def unit_rows(values):
    inverse = lax.rsqrt(jnp.mean(values * values, axis=-1, keepdims=True) + epsilon)
    return values * inverse, inverse


def turn(u, cos, sin):
    return u * cos + pltpu.roll(u, u.shape[-1] // 2, 1) * sin


def turn_back(u, cos, sin):
    return u * cos - pltpu.roll(u, u.shape[-1] // 2, 1) * sin


def mask_bias(bias, start_ref, rows):
    block = 128

    @pl.loop(0, bias.shape[0] // block)
    def _(i):
        rr = pl.ds(pl.multiple_of(i * block, block), block)
        key = lax.broadcasted_iota(jnp.int32, (block, rows), 0) + i * block
        query = lax.broadcasted_iota(jnp.int32, (block, rows), 1) + rows
        ok = (key >= start_ref[...]) & (key <= query)
        bias[rr, :] = jnp.where(ok, 0.0, -1e30)


class Schedule:
    def __init__(self, gathers, starts, after):
        steps = [("begin",)] + [("along_z", k) for k in (1, 2, 3)] + [("along_y", k) for k in range(4)] + [("along_x", k) for k in range(4)] + [("finish",)]
        slots = {}
        for i, g in reversed(list(enumerate(gathers))):
            for j, s in zip(after, steps):
                slots.setdefault(starts[i] + j, []).append((i, g, s))
        self.steps = [step for t in sorted(slots) for step in slots[t]]

    def run(self, count):
        for i, g, s in self.steps[:count]:
            g.step(*s)
        self.steps = self.steps[count:]

    def until(self, weight):
        ends = [n for n, (i, g, s) in enumerate(self.steps) if i == weight and s[0] == "finish"]
        if ends:
            self.run(ends[0] + 1)


def forward_kernel(plan, hid, pos, freq, norm_gain, query_gain, key_gain, mlp_gain, *refs):
    owns, refs = refs[:7], refs[7:]
    outs, refs = refs[:7], refs[7:]
    (q_o, k_o, v_o, qraw_o, kraw_o, ain_o, attn_o, lse_o, mid_o, mlp_o, gate_o, up_o, hidden_o, cos_o, sin_o, start, bias_o), refs = refs[:17], refs[17:]
    fulls, refs = refs[:6] + (outs[6],), refs[6:]
    (ain, q, k, vt, attn, bias, tmp, mid, stage, cos, sin, ain_sem, out_sem), sems = refs[:13], refs[13:]
    w_q, w_k, w_v, w_o, w_g, w_u = fulls[:6]
    cuts, starts, after, runs, early, _ = plan
    runs = list(runs)
    at = place()
    z, y, c, x = at
    rows, width = hid.shape
    hd = freq.shape[1]
    kv = w_k.shape[1] // hd
    qh = w_q.shape[1] // hd
    group = qh // kv
    span = tmp.shape[1]
    first, second = pl.ds(0, rows), pl.ds(rows, rows)
    enter(*at)
    gs = [Gather(i, owns[i], fulls[i], sems, at, cuts[i]) for i in range(7)]
    sched = Schedule(gs, starts, after)
    writes = Writes(out_sem)
    sched.run(1)

    def norm_one(r, n):
        unit, _ = unit_rows(hid[pl.ds(r, n), :].astype(f32))
        ain[pl.ds(pl.multiple_of(r + rows, n), n), :] = (unit * norm_gain[...]).astype(bf16)

    rows_loop(rows, 64, norm_one)
    count = ain_sem.shape[1]
    size = rows // count

    def handed(n):
        return pltpu.make_async_remote_copy(
            src_ref=ain.at[pl.ds(rows + n * size, size), :], dst_ref=ain.at[pl.ds(n * size, size), :],
            send_sem=ain_sem.at[0, n], recv_sem=ain_sem.at[1, n],
            device_id=(z * 4 + y * 2 + c, 1 - x), device_id_type=MESH)

    left = list(range(count))

    def hand():
        if left:
            n = left.pop(0)

            @pl.when(x == 0)
            def _():
                handed(n).start()

    def pump():
        sched.run(runs.pop(0))
        hand()

    hand()

    @pl.when(x == 0)
    def _():
        ain[first, :] = jnp.zeros((rows, width), bf16)

    index = lax.broadcasted_iota(jnp.int32, (1, rows), 1)
    head = jnp.sum(jnp.where(index == 0, pos[...], 0), axis=1, keepdims=True)
    own_start = index + rows - pos[...]
    start[...] = jnp.where(x == 0, jnp.maximum(own_start, rows), own_start)
    sign = jnp.where(lax.broadcasted_iota(jnp.int32, (rows, hd), 1) < hd // 2, -1.0, 1.0)
    for rr, row in ((second, pos[...]), (first, index - rows + head)):
        angle = jnp.broadcast_to(row.astype(f32), (hd, rows)).T * freq[...]
        cos[rr, :] = jnp.cos(angle)
        sin[rr, :] = jnp.sin(angle) * sign
    writes.start(cos, cos_o)
    writes.start(sin, sin_o)
    mask_bias(bias, start, rows)
    writes.start(bias, bias_o)
    for _ in range(early):
        sched.run(2)
        hand()
    sched.until(0)

    def heads(lhs, weight, base, count, gain, into, col):
        for r in range(0, count, rows):
            tmp[r:r + rows, :] = dot_nn(lhs[pl.ds(r, rows), :], weight)
            pump()
        for part in range(0, span // hd, 4):
            @pl.loop(part, part + 4)
            def _(h):
                cc = pl.ds(pl.multiple_of(h * hd, hd), hd)
                to = pl.ds(pl.multiple_of(col + h * hd, hd), hd)
                for r in range(0, count, 256):
                    raw = tmp[r:r + 256, cc]
                    stage[r:r + 256, cc] = raw.astype(bf16)
                    unit, _ = unit_heads(raw)
                    t = slice(base + r, base + r + 256)
                    into[r:r + 256, to] = turn(unit * gain[...], cos[t, :], sin[t, :]).astype(bf16)

            pump()

    last = None
    for b in range(w_q.shape[1] // span):
        if last is not None:
            writes.wait(last)
        heads(ain.at[second, :], w_q[:, b * span:(b + 1) * span], rows, rows, query_gain, q, b * span)
        last = writes.start(stage.at[first, :], qraw_o.at[:, pl.ds(b * span, span)])
    while left:
        hand()
    sched.until(1)

    @pl.when(x == 1)
    def _():
        for n in range(count):
            handed(n).wait_recv()

    writes.wait(last)
    heads(ain, w_k[...], 0, 2 * rows, key_gain, k, 0)
    last = writes.start(stage, kraw_o)
    writes.start(ain, ain_o)
    writes.start(q, q_o)
    writes.start(k, k_o)
    sched.until(2)
    for r in (first, second):
        tmp[r, :] = dot_nn(ain[r, :], w_v[...])
        pump()
    writes.wait(last)
    stage[...] = tmp[...].astype(bf16)
    last = writes.start(stage, v_o)

    @pl.loop(0, kv)
    def _(h):
        cc = pl.ds(pl.multiple_of(h * hd, hd), hd)
        vt[cc, :] = tmp[:, cc].astype(bf16).T

    pump()

    c2 = hd ** (-0.5) * log2e
    for part in range(kv):
        @pl.loop(part, part + 1)
        def _(h):
            cc = pl.ds(pl.multiple_of(h * hd, hd), hd)
            for g in range(group):
                n = h * group + g
                qc = pl.ds(pl.multiple_of(n * hd, hd), hd)
                p = jnp.exp2(dot_nt(k[:, cc], q[:, qc]) * c2 + bias[...])
                total = jnp.sum(p, axis=0, keepdims=True)
                o = dot_nn(vt[cc, :], p.astype(bf16))
                attn[qc, :] = (o * (1.0 / total)).astype(bf16)
                lse_o[pl.ds(n, 1), :] = jnp.log2(total)

        pump()
    writes.start(attn, attn_o)
    sched.until(3)
    for i in range(3):
        gs[i].step("drain")
    leaving = [writes.start(fulls[i], outs[i]) for i in range(3)]
    writes.start(w_o, outs[3])
    mid[...] = hid[...].astype(f32) + dot_tn(attn[...], w_o[...])
    pump()

    for n in leaving:
        writes.wait(n)
    writes.wait(last)
    blocks = w_g.shape[1] // span
    hidden = [w_q.at[first, pl.ds(0, span)], w_q.at[second, pl.ds(0, span)], w_q.at[first, pl.ds(span, span)]]
    mlp_in = w_q.at[second, pl.ds(span, span)]
    gates = [w_k.at[first, :], w_v.at[first, :], stage.at[first, :]]
    ups = [w_k.at[second, :], w_v.at[second, :], stage.at[second, :]]

    def norm_two(r, n):
        unit, _ = unit_rows(mid[pl.ds(r, n), :])
        mlp_in[pl.ds(r, n), :] = (unit * mlp_gain[...]).astype(bf16)

    rows_loop(rows, 64, norm_two)
    writes.start(mid, mid_o)
    writes.start(mlp_in, mlp_o)
    sched.until(4)
    sched.until(5)
    writes.start(w_g, outs[4])
    writes.start(w_u, outs[5])
    for j in range(blocks):
        cols = pl.ds(j * span, span)
        tmp[first, :] = dot_nn(mlp_in[...], w_g[:, cols])
        pump()
        tmp[second, :] = dot_nn(mlp_in[...], w_u[:, cols])
        pump()

        def act(r, n):
            rr = pl.ds(r, n)
            gate, up = tmp[rr, :], tmp[pl.ds(pl.multiple_of(r + rows, n), n), :]
            sig = jax.nn.sigmoid(gate)
            silu = gate * sig
            hidden[j][rr, :] = (silu * up).astype(bf16)
            gates[j][rr, :] = (up * (sig + silu * (1.0 - sig))).astype(bf16)
            ups[j][rr, :] = silu.astype(bf16)

        rows_loop(rows, 64, act)
        writes.start(gates[j], gate_o.at[:, cols])
        writes.start(ups[j], up_o.at[:, cols])
        writes.start(hidden[j], hidden_o.at[:, cols])
        pump()
    sched.until(6)
    sched.run(len(sched.steps))
    for g in gs[3:]:
        g.step("drain")

    @pl.when(x == 0)
    def _():
        for n in range(count):
            handed(n).wait_send()

    writes.wait_all()


def forward(hid, pos, freq, gains, shards):
    rows, width = hid.shape
    hd = freq.shape[1]
    fulls = [(s.shape[0] * 16, s.shape[1]) for s in shards]
    heads, keys, ff = shards[0].shape[1], shards[1].shape[1], shards[4].shape[1]
    shape = jax.ShapeDtypeStruct
    vm = pltpu.VMEM
    outs = [shape(s, bf16) for s in fulls] + [
        shape((rows, heads), bf16), shape((2 * rows, keys), bf16), shape((2 * rows, keys), bf16),
        shape((rows, heads), bf16), shape((2 * rows, keys), bf16), shape((2 * rows, width), bf16), shape((heads, rows), bf16),
        shape((heads // hd, rows), f32), shape((rows, width), f32), shape((rows, width), bf16),
        shape((rows, ff), bf16), shape((rows, ff), bf16), shape((rows, ff), bf16),
        shape((2 * rows, hd), f32), shape((2 * rows, hd), f32), shape((1, rows), jnp.int32), shape((2 * rows, rows), f32)]
    specs = [HBM] * 7 + [VMEM if i in (7, 15) else HBM for i in range(17)]
    return pl.pallas_call(
        functools.partial(forward_kernel, FORWARD_PLAN),
        out_shape=outs,
        in_specs=[VMEM] * 7 + [HBM] * 7,
        out_specs=specs,
        scratch_shapes=[vm(s, bf16) for s in fulls[:6]] + [
            vm((2 * rows, width), bf16), vm((rows, heads), bf16), vm((2 * rows, keys), bf16), vm((keys, 2 * rows), bf16),
            vm((heads, rows), bf16), vm((2 * rows, rows), f32), vm((2 * rows, keys), f32), vm((rows, width), f32),
            vm((2 * rows, keys), bf16), vm((2 * rows, hd), f32), vm((2 * rows, hd), f32), pltpu.SemaphoreType.DMA((2, FORWARD_PLAN[5])), pltpu.SemaphoreType.DMA((32,))] + gather_sems(7),
        compiler_params=pltpu.CompilerParams(collective_id=1, has_side_effects=True, vmem_limit_bytes=62 * 2**20),
        name="forward_gather",
    )(hid, pos, freq, *gains, *shards)


class Chunk:
    def __init__(self, index, bufs, sems, at, out, ones, twos):
        self.i, self.out, self.ones, self.twos = index, out, ones, twos
        ring = [index % b.shape[0] for b in bufs]
        self.g, self.cb, self.xb, self.yb, self.zb, self.fb, self.st = [b.at[r] for b, r in zip(bufs, ring)]
        self.sc, self.sx, self.sy, self.zs, self.zr, self.sf, self.so = [s.at[index] for s in sems]
        self.z, self.y, self.c, self.x = at
        self.unit = self.g.shape[3] // 4

    def step(self, name, *args):
        u = self.unit
        if self.ones == self.twos and name != "finish":
            t = self.ones
            self.first = self.x * t
            self.keep, self.send_x, self.got_x, self.theirs = 4 - t, t, t, 4 - t
            self.ywin = pl.ds(pl.multiple_of(self.first * u, 16), self.keep * u)
            self.xsend = pl.ds(pl.multiple_of((1 - self.x) * (4 - t) * u, 16), t * u)
            self.xgot = pl.ds(pl.multiple_of(self.x * (4 - t) * u, 16), t * u)
            getattr(self, name)(*args)
            return
        for x in (0, 1):
            @pl.when(self.x == x)
            def _():
                spans = ((0, 4 - self.twos), (self.ones, 4))
                lows, highs = (0, self.ones), (4 - self.twos, 4)
                self.span, self.other = spans[x], spans[1 - x]
                self.keep, self.theirs = self.span[1] - self.span[0], self.other[1] - self.other[0]
                out, into = (highs, lows) if x == 0 else (lows, highs)
                self.send_x, self.got_x = out[1] - out[0], into[1] - into[0]
                self.ywin = pl.ds(self.span[0] * u, self.keep * u)
                self.xsend, self.xgot = pl.ds(out[0] * u, self.send_x * u), pl.ds(into[0] * u, self.got_x * u)
                getattr(self, name)(*args)

    def send(self, src, dst, ssem, rsem, z2, y2, c2, x2):
        return pltpu.make_async_remote_copy(
            src_ref=src, dst_ref=dst, send_sem=ssem, recv_sem=rsem,
            device_id=(z2 * 4 + y2 * 2 + c2, x2), device_id_type=MESH)

    def c_copy(self):
        return self.send(self.g.at[:, :, 1 - self.c], self.cb, self.sc.at[0], self.sc.at[1], self.z, self.y, 1 - self.c, self.x)

    def x_copy(self):
        return self.send(
            self.g.at[:, :, self.c, self.xsend], self.xb.at[:, :, pl.ds(0, self.send_x * self.unit)], self.sx.at[0], self.sx.at[1],
            self.z, self.y, self.c, 1 - self.x)

    def y_copy(self):
        return self.send(
            self.g.at[:, 1 - self.y, self.c, self.ywin], self.yb.at[:, pl.ds(0, self.keep * self.unit)], self.sy.at[0], self.sy.at[1],
            self.z, 1 - self.y, self.c, self.x)

    def z_slot(self, slot):
        return self.zb.at[slot, pl.ds(0, self.keep * self.unit)]

    def z_copy(self, here, to, up):
        there = here + 1 if up else here - 1
        slot = 4 if to == there and not up else to
        return self.send(
            self.g.at[to, self.y, self.c, self.ywin], self.z_slot(slot), self.zs.at[to], self.zr.at[slot], there, self.y, self.c, self.x)

    def f_copy(self):
        return self.send(
            self.g.at[self.z, self.y, self.c, self.ywin], self.fb.at[pl.ds(0, self.keep * self.unit)], self.sf.at[0], self.sf.at[1],
            self.z, self.y, self.c, 1 - self.x)

    def o_copy(self):
        return pltpu.make_async_copy(self.st, self.out, self.so)

    def arrived(self, dst, sem):
        pltpu.make_async_copy(dst, dst, sem).wait()

    def add(self, zz, yy, win, src):
        dst = self.g.at[zz, yy, self.c, win]
        dst[...] = dst[...] + src[...]

    def go(self):
        self.c_copy().start()

    def over_c(self):
        self.c_copy().wait_recv()

        @pl.loop(0, 4)
        def _(zz):
            for yy in (0, 1):
                self.add(zz, yy, slice(None), self.cb.at[zz, yy])

        if self.send_x:
            self.x_copy().start()
        if not self.ones and not self.twos:
            self.y_copy().start()

    def over_x(self):
        if self.got_x:
            got = self.xb.at[:, :, pl.ds(0, self.got_x * self.unit)]
            self.arrived(got, self.sx.at[1])

            @pl.loop(0, 4)
            def _(zz):
                for yy in (0, 1):
                    self.add(zz, yy, self.xgot, got.at[zz, yy])

        self.y_copy().start()

    def over_y(self):
        self.y_copy().wait_recv()

        @pl.loop(0, 4)
        def _(zz):
            self.add(zz, self.y, self.ywin, self.yb.at[zz, pl.ds(0, self.keep * self.unit)])

    def take(self, zz, slot):
        self.arrived(self.z_slot(slot), self.zr.at[slot])
        self.add(zz, self.y, self.ywin, self.z_slot(slot))

    def over_z(self, k):
        for up in (True, False):
            here = k if up else 3 - k

            @pl.when(self.z == here)
            def _():
                for to in (range(3, here, -1) if up else range(here)):
                    if k:
                        self.take(to, to)
                    self.z_copy(here, to, up).start()
                if k:
                    self.take(here, here if up else 4)

    def hand(self):
        self.f_copy().start()

    def finish(self, before):
        u = self.unit
        self.arrived(self.fb.at[pl.ds(0, self.theirs * u)], self.sf.at[1])
        if before is not None:
            before.o_copy().wait()
        own = self.g.at[self.z, self.y, self.c]
        (a, b), (c, d) = self.span, self.other
        for lo, hi in ((0, max(a, c)), (max(a, c), min(b, d)), (min(b, d), 4)):
            if lo < hi:
                mine, theirs = own[lo * u:hi * u, :].astype(f32), None
                if c <= lo and hi <= d:
                    theirs = self.fb[(lo - c) * u:(hi - c) * u, :].astype(f32)
                held = a <= lo and hi <= b
                self.st[lo * u:hi * u, :] = theirs if not held else mine if theirs is None else mine + theirs
        self.o_copy().start()
        self.c_copy().wait_send()
        if self.send_x:
            self.x_copy().wait_send()
        self.y_copy().wait_send()
        self.f_copy().wait_send()
        for here in range(4):
            @pl.when(self.z == here)
            def _():
                for to in range(4):
                    if to != here:
                        self.z_copy(here, to, to > here).wait_send()


def chunk_bufs(rows, cols):
    part = rows // 4
    sizes = ((10, 4, 2, 2, rows, cols), (4, 4, 2, rows, cols), (6, 4, 2, part, cols), (6, 4, rows, cols), (6, 5, rows, cols), (8, rows, cols))
    return [pltpu.VMEM(s, bf16) for s in sizes] + [pltpu.VMEM((2, rows, cols), f32)]


def chunk_sems(n):
    return [pltpu.SemaphoreType.DMA(s) for s in ((n, 2), (n, 2), (n, 2), (n, 4), (n, 5), (n, 2), (n,))]


class Totals:
    def __init__(self, mine, got, sem, at):
        self.mine, self.got, self.sem = mine, got, sem
        z, y, c, x = at
        self.to = [(z, y, 1 - c, x), (z, y, c, 1 - x), (z, 1 - y, c, x), (z + 1 - 2 * (z % 2), y, c, x), (3 - z, y, c, x)]

    def copy(self, s):
        z, y, c, x = self.to[s]
        return pltpu.make_async_remote_copy(
            src_ref=self.mine.at[s], dst_ref=self.got.at[s], send_sem=self.sem.at[s, 0], recv_sem=self.sem.at[s, 1],
            device_id=(z * 4 + y * 2 + c, x), device_id_type=MESH)

    def step(self, s):
        if s > 0:
            self.copy(s - 1).wait()
            self.mine[s] = self.mine[s - 1] + self.got[s - 1]
        if s < 5:
            self.copy(s).start()


def backward_kernel(plan, cot, cos, sin, norm_gain, query_gain, key_gain, mlp_gain, lse, *refs):
    full, refs = refs[:7], refs[7:]
    (hid_i, q_i, k_i, v_i, qraw_i, kraw_i, ain_i, attn_i, mid_i, mlp_i, gate_i, up_i, hidden_i, bias_i), refs = refs[:14], refs[14:]
    grads, refs = refs[:7], refs[7:]
    (out_o, gin_o, norm_o, query_o, key_o, mlp_o), refs = refs[:6], refs[6:]
    (hidden, mlp, ggate, gup, mid, acc, gproj, attn, q, k, v, qraw, kraw, ain, dk, dv, kt, bias, wbuf, earlier, sum_one, sum_two, sum_q, sum_k,
     gain_mine, gain_got, gain_sem, load_sem, w_sem, early_sem), refs = refs[:30], refs[30:]
    bufs, sems = refs[:7], refs[7:]
    at = place()
    z, y, c, x = at
    rows, width = cot.shape
    hd = cos.shape[1]
    kv, qh = k.shape[1] // hd, q.shape[1] // hd
    group = qh // kv
    span = wbuf.shape[1]
    ff = ggate.shape[1]
    cols = bufs[0].shape[-1]
    first, second = pl.ds(0, rows), pl.ds(rows, rows)
    scale = hd ** (-0.5)
    enter(*at, True)

    loads = Writes(load_sem)
    wide = hidden.shape[1] // 4
    hidden_l = [loads.start(hidden_i.at[:, pl.ds(b * wide, wide)], hidden.at[:, pl.ds(b * wide, wide)]) for b in range(4)]
    blocks = [full[6].at[pl.ds(j * span, span), :] for j in range(ff // span)]
    for j in range(ff // span):
        blocks += [full[4].at[:, pl.ds(j * span, span)], full[5].at[:, pl.ds(j * span, span)]]
    blocks += [full[3].at[pl.ds(j * span, span), :] for j in range(qh * hd // span)]
    blocks += [full[1], full[2]] + [full[0].at[:, pl.ds(j * span, span)] for j in range(qh * hd // span)]

    def fetch(n):
        return pltpu.make_async_copy(blocks[n], wbuf.at[n % 2], w_sem.at[n % 2])

    def weight(n):
        fetch(n).wait()
        return wbuf[n % 2]

    def used(n):
        if n + 2 < len(blocks):
            fetch(n + 2).start()

    fetch(0).start()
    fetch(1).start()
    gate_l = loads.start(gate_i, ggate)
    up_l = loads.start(up_i, gup)
    mlp_l, mid_l, attn_l = loads.start(mlp_i, mlp), loads.start(mid_i, mid), loads.start(attn_i, attn)
    later = []

    todo = []

    def put(val, spot, subs, shards_from):
        size = bufs[0].shape[4]
        for f in range(val.shape[0] // (size * subs)):
            for s in range(subs):
                owner = shards_from + f
                lo = (f * subs + s) * size
                bufs[0][(spot + s) % bufs[0].shape[0], owner // 4, owner // 2 % 2, owner % 2] = val[lo:lo + size, :].astype(bf16)

    def make_down(j):
        def run(spot):
            for b in range(4):
                loads.wait(hidden_l[b])
                put(dot_tn(hidden[:, b * wide:(b + 1) * wide], cot[:, j * cols:(j + 1) * cols]), spot, wide // 256, b * 4)
        return run

    def make_out(j):
        def run(spot):
            loads.wait(attn_l)
            tall = attn.shape[0] // 4
            for b in range(4):
                put(dot_nn(attn[b * tall:(b + 1) * tall, :], gproj[:, j * cols:(j + 1) * cols]), spot, tall // 256, b * 4)
        return run

    def make(lhs, rhs, j):
        def run(spot):
            put(dot_tn(lhs(), rhs[:, j * cols:(j + 1) * cols]), spot, 1, 0)
        return run

    def mlp_all():
        loads.wait(mlp_l)
        return mlp[...]

    def ain_own():
        return ain[second, :]

    def ain_all():
        return ain[...]

    def add_weight(w, subs, maker, count):
        for j in range(count):
            for s in range(subs):
                out = grads[w].at[pl.ds(s * 64, 64), pl.ds(j * cols, cols)]
                todo.append((maker(j) if s == 0 else None, out))

    add_weight(6, hidden.shape[1] // (64 * 16), make_down, width // cols)
    add_weight(4, 1, lambda j: make(mlp_all, ggate, j), ff // cols)
    add_weight(5, 1, lambda j: make(mlp_all, gup, j), ff // cols)
    add_weight(3, attn.shape[0] // (64 * 16), make_out, width // cols)
    add_weight(0, 1, lambda j: make(ain_own, q, j), qh * hd // cols)
    add_weight(1, 1, lambda j: make(ain_all, k, j), kv * hd // cols)
    add_weight(2, 1, lambda j: make(ain_all, v, j), kv * hd // cols)
    kinds, order = plan
    chunks = [Chunk(i, bufs, sems, at, out, *kinds[i]) for i, (_, out) in enumerate(todo)]

    nb = ff // span

    def piece_down(j):
        block = weight(j)
        acc[...] = dot_nt(cot[...], block)
        cc = slice(j * span, (j + 1) * span)
        for part in range(2):
            more = dot_nn(hidden[:, cc], wbuf[j % 2, :, part * rows:(part + 1) * rows])
            rr = pl.ds(part * rows, rows)
            bias[rr, :] = more if j == 0 else bias[rr, :] + more
        used(j)

    def piece_act(j, part):
        cc = slice(j * span, (j + 1) * span)
        loads.wait(gate_l)
        loads.wait(up_l)

        def act(r, n):
            rr = pl.ds(pl.multiple_of(r + part * (rows // 2), n), n)
            grad = acc[rr, :]
            ggate[rr, cc] = (grad * ggate[rr, cc].astype(f32)).astype(bf16)
            gup[rr, cc] = (grad * gup[rr, cc].astype(f32)).astype(bf16)

        rows_loop(rows // 2, 64, act)

    def piece_output():
        loads.wait(mid_l)
        for part in range(2):
            cc = slice(part * rows, (part + 1) * rows)
            gproj[:, cc] = (mid[:, cc] + bias[part * rows:(part + 1) * rows, :]).astype(bf16)
        later.append(loads.start(gproj, out_o))
        later.append(loads.start(bias_i, bias))

    def piece_mlp(j, part):
        n = nb + 2 * j + part
        cc = slice(j * span, (j + 1) * span)
        one = dot_nt((gup if part else ggate)[:, cc], weight(n))
        acc[...] = one if n == nb else acc[...] + one
        used(n)

    def fold(into, terms):
        into[...] += jnp.sum(terms.reshape(terms.shape[0] // 8, 8, terms.shape[1]), axis=0)

    def norm_back(grad, unit, inverse, gain):
        scaled = grad * gain
        return inverse * (scaled - unit * jnp.mean(scaled * unit, axis=-1, keepdims=True))

    def piece_mid(part):
        if part == 0:
            loads.wait(later[0])
            sum_two[...] = jnp.zeros_like(sum_two)

        def body(r, n):
            rr = pl.ds(pl.multiple_of(r + part * (rows // 2), n), n)
            unit, inverse = unit_rows(mid[rr, :])
            grad = acc[rr, :]
            fold(sum_two, grad * unit)
            out = cot[rr, :].astype(f32) + norm_back(grad, unit, inverse, mlp_gain[...])
            mid[rr, :] = out
            gproj[rr, :] = out.astype(bf16)

        rows_loop(rows // 2, 64, body)

    at_out = 3 * nb
    n_out = qh * hd // span

    def piece_attn_grad(j):
        hidden[:, j * span:(j + 1) * span] = dot_nt(gproj[...], weight(at_out + j)).astype(bf16)
        used(at_out + j)

    def piece_ready():
        loads.wait(later[1])
        sum_q[...] = jnp.zeros_like(sum_q)
        sum_k[...] = jnp.zeros_like(sum_k)
        loads.wait(attn_l)
        for n in head_l:
            loads.wait(n)
        loads.wait(ain_l)

    c2 = scale * log2e
    tile = rows // 2

    def norm_back_heads(grad, unit, inverse, gain):
        scaled = grad * gain
        mean = dot_nn((scaled * unit).astype(bf16), jnp.full((hd, hd), 1.0 / hd, bf16))
        return inverse * (scaled - unit * mean)

    def piece_head(h, g, i):
        cc = slice(h * hd, (h + 1) * hd)
        n = h * group + g
        qc = slice(n * hd, (n + 1) * hd)
        if g == 0 and i == 0:
            kt[...] = k[:, cc].T
            dk[...] = jnp.zeros_like(dk)
            dv[...] = jnp.zeros_like(dv)
        rs = slice(i * tile, (i + 1) * tile)
        kk = rows + (i + 1) * tile
        query, grad = q[rs, qc], hidden[rs, qc]
        delta = jnp.sum(attn[qc, rs].astype(f32) * grad.T.astype(f32), axis=0, keepdims=True)
        p = jnp.exp2(dot_nt(k[:kk, cc], query) * c2 + (bias[:kk, rs] - lse[n:n + 1, rs]))
        gp = dot_nt(v[:kk, cc], grad)
        ds = (p * (gp - delta)).astype(bf16)
        dv[:kk, :] += dot_nn(p.astype(bf16), grad)
        dk[:kk, :] += dot_nn(ds, query)
        dq = dot_nn(kt[:, :kk], ds).T * scale
        unit, inverse = unit_heads(qraw[rs, qc].astype(f32))
        t = slice(rows + i * tile, rows + (i + 1) * tile)
        back = turn_back(dq, cos[t, :], sin[t, :])
        fold(sum_q, back * unit)
        q[rs, qc] = norm_back_heads(back, unit, inverse, query_gain[...]).astype(bf16)

    def piece_keys(h):
        cc = slice(h * hd, (h + 1) * hd)
        for r in range(0, 2 * rows, tile):
            rr = slice(r, r + tile)
            unit, inverse = unit_heads(kraw[rr, cc].astype(f32))
            back = turn_back(dk[rr, :] * scale, cos[rr, :], sin[rr, :])
            fold(sum_k, back * unit)
            k[rr, cc] = norm_back_heads(back, unit, inverse, key_gain[...]).astype(bf16)
            v[rr, cc] = dv[rr, :].astype(bf16)

    at_kv = at_out + n_out
    early_rows = rows // 8

    def handed(n):
        part = pl.ds(n * early_rows, early_rows)
        return pltpu.make_async_remote_copy(
            src_ref=gproj.at[part, :], dst_ref=earlier.at[part, :], send_sem=early_sem.at[0, n], recv_sem=early_sem.at[1, n],
            device_id=(z * 4 + y * 2 + c, 1 - x), device_id_type=MESH)

    def piece_hand(n):
        @pl.when(x == 1)
        def _():
            handed(n).start()

    def piece_queries(j):
        acc[...] += dot_nt(q[:, j * span:(j + 1) * span], weight(at_kv + 2 + j))
        used(at_kv + 2 + j)

    x_in, x_out = mlp, ggate.at[:, pl.ds(0, span)]
    late = []

    def piece_gain():
        loads.wait(late[0])
        sum_one[...] = jnp.zeros_like(sum_one)

        def body(r, n):
            rr = pl.ds(r, n)
            unit, _ = unit_rows(x_in[rr, :].astype(f32))
            fold(sum_one, acc[rr, :] * unit)

        rows_loop(rows, 64, body)

        @pl.when(x == 1)
        def _():
            def more(r, n):
                rr = pl.ds(r, n)
                fold(sum_one, gproj[rr, :].astype(f32) * ain[rr, :].astype(f32) / norm_gain[...])

            rows_loop(rows, 64, more)

        gain_mine[0] = jnp.zeros_like(gain_mine[0])
        gain_mine[0, 0:1, :] = jnp.sum(sum_one[...], axis=0, keepdims=True)
        gain_mine[0, 1:2, :] = jnp.sum(sum_two[...], axis=0, keepdims=True)
        gain_mine[0, 2:3, 0:hd] = jnp.sum(sum_q[...], axis=0, keepdims=True)
        gain_mine[0, 3:4, 0:hd] = jnp.sum(sum_k[...], axis=0, keepdims=True)

    def piece_last():
        @pl.when(x == 0)
        def _():
            for n in range(8):
                handed(n).wait_recv()

            def more(r, n):
                rr = pl.ds(r, n)
                acc[rr, :] += earlier[rr, :].astype(f32)

            rows_loop(rows, 64, more)

        def body(r, n):
            rr = pl.ds(r, n)
            unit, inverse = unit_rows(x_in[rr, :].astype(f32))
            x_out[rr, :] = (mid[rr, :] + norm_back(acc[rr, :], unit, inverse, norm_gain[...])).astype(bf16)

        rows_loop(rows, 64, body)
        loads.start(x_out, gin_o)

    def piece_earlier():
        w_k, w_v = weight(at_kv), weight(at_kv + 1)

        @pl.when(x == 1)
        def _():
            gproj[...] = (dot_nt(k[first, :], w_k) + dot_nt(v[first, :], w_v)).astype(bf16)

    def piece_own():
        acc[...] = dot_nt(k[second, :], wbuf[at_kv % 2]) + dot_nt(v[second, :], wbuf[(at_kv + 1) % 2])
        used(at_kv)
        used(at_kv + 1)
        late.append(loads.start(hid_i, x_in))

    totals = Totals(gain_mine, gain_got, gain_sem, at)
    chain = []
    for j in range(nb):
        chain += [(piece_down, j), (piece_act, j, 0), (piece_act, j, 1)]
    for j in range(nb):
        chain += [(piece_mlp, j, 0), (piece_mlp, j, 1)]
    chain += [(piece_mid, 0), (piece_mid, 1)] + [(piece_attn_grad, j) for j in range(n_out)] + [(piece_ready,)]
    for h in range(kv):
        chain += [(piece_head, h, g, i) for g in range(group) for i in range(2)] + [(piece_keys, h)]
    chain += [(piece_earlier,), (piece_own,)] + [(piece_queries, j) for j in range(n_out)] + [(piece_gain,)]
    chain += [(totals.step, s) for s in range(6)] + [(piece_last,)]
    made, ended = 0, []
    for kind, index, name in order:
        if kind == 0:
            if name == 0:
                if todo[index][0] is not None:
                    todo[index][0](index)
                    if made == 0:
                        head_l = [loads.start(a, b) for a, b in ((q_i, q), (k_i, k), (v_i, v), (qraw_i, qraw), (kraw_i, kraw))]
                        ain_l = loads.start(ain_i, ain)
                        made = 1
                chunks[index].step("go")
            elif name <= 2:
                chunks[index].step(("over_c", "over_x")[name - 1])
            elif name == 8:
                chunks[index].st = bufs[6].at[len(ended) % 2]
                chunks[index].step("finish", ended[-2] if len(ended) > 1 else None)
                ended.append(chunks[index])
            else:
                if name == 3:
                    chunks[index].step("over_y")
                chunks[index].step("over_z", name - 3)
                if name == 6:
                    chunks[index].step("hand")
        elif kind == 1:
            chain[index][0](*chain[index][1:])
            if index == 3 * nb - 1:
                piece_output()
        else:
            piece_hand(index)
    for ch in ended[-2:]:
        ch.o_copy().wait()

    @pl.when(x == 1)
    def _():
        for n in range(8):
            handed(n).wait_send()

    loads.wait_all()
    norm_o[...] = gain_mine[5, 0:1, :]
    mlp_o[...] = gain_mine[5, 1:2, :]
    query_o[...] = gain_mine[5, 2:3, 0:hd]
    key_o[...] = gain_mine[5, 3:4, 0:hd]


def backward(hid, cot, gains, saved, shards):
    rows, width = hid.shape
    full = saved[:7]
    q, k, v, qraw, kraw, ain, attn, lse, mid, mlp, gate, up, hidden, cos, sin, _, bias = saved[7:]
    hd = cos.shape[1]
    shape, vm, dma = jax.ShapeDtypeStruct, pltpu.VMEM, pltpu.SemaphoreType.DMA
    heads, keys, ff = q.shape[1], k.shape[1], gate.shape[1]
    span = keys
    outs = [shape(s.shape, f32) for s in shards] + [
        shape((rows, width), bf16), shape((rows, width), bf16), shape((1, width), f32), shape((1, hd), f32), shape((1, hd), f32), shape((1, width), f32)]
    n = sum(s.shape[0] // 64 * (s.shape[1] // 512) for s in shards)
    return pl.pallas_call(
        functools.partial(backward_kernel, BACKWARD_PLAN),
        out_shape=outs,
        in_specs=[VMEM] * 8 + [HBM] * 21,
        out_specs=[HBM] * 9 + [VMEM] * 4,
        scratch_shapes=[
            vm((rows, ff), bf16), vm((rows, width), bf16), vm((rows, ff), bf16), vm((rows, ff), bf16), vm((rows, width), f32), vm((rows, width), f32),
            vm((rows, width), bf16), vm((heads, rows), bf16), vm((rows, heads), bf16), vm((2 * rows, keys), bf16), vm((2 * rows, keys), bf16),
            vm((rows, heads), bf16), vm((2 * rows, keys), bf16), vm((2 * rows, width), bf16), vm((2 * rows, hd), f32), vm((2 * rows, hd), f32),
            vm((hd, 2 * rows), bf16), vm((2 * rows, rows), f32), vm((2, span, span), bf16), vm((rows, width), bf16),
            vm((8, width), f32), vm((8, width), f32), vm((8, hd), f32), vm((8, hd), f32), vm((6, 8, width), f32), vm((5, 8, width), f32),
            dma((5, 2)), dma((32,)), dma((2,)), dma((2, 8))] + chunk_bufs(64, 512) + chunk_sems(n),
        compiler_params=pltpu.CompilerParams(collective_id=2, has_side_effects=True, vmem_limit_bytes=63 * 2**20),
        name="backward_reduce",
    )(cot, cos, sin, *gains, lse, *full, hid, q, k, v, qraw, kraw, ain, attn, mid, mlp, gate, up, hidden, bias)


def place_kernel(*refs):
    n = (len(refs) - 1) // 3
    first = [pltpu.make_async_copy(refs[i], refs[2 * n + i], refs[-1].at[0, i]) for i in range(n)]
    second = [pltpu.make_async_copy(refs[2 * n + i], refs[n + i], refs[-1].at[1, i]) for i in range(n)]
    for copy in first:
        copy.start()
    for i in range(n):
        first[i].wait()
        second[i].start()
    for copy in second:
        copy.wait()


def placed(arrays):
    n = len(arrays)
    return pl.pallas_call(
        place_kernel,
        out_shape=[jax.ShapeDtypeStruct(a.shape, a.dtype) for a in arrays],
        in_specs=[HBM] * n,
        out_specs=[HBM] * n,
        scratch_shapes=[pltpu.VMEM(a.shape, a.dtype) for a in arrays] + [pltpu.SemaphoreType.DMA((2, n))],
        compiler_params=pltpu.CompilerParams(vmem_limit_bytes=32 * 2**20),
        name="place_results",
    )(*arrays)


def as_sent(shard):

    def short(part):
        return part.astype(jnp.bfloat16) if part.dtype == jnp.float32 else part

    return jax.tree.map(short, shard)


def norm_rows(values, gain_vec):
    inverse = lax.rsqrt(jnp.mean(values * values, axis=-1, keepdims=True) + epsilon)
    normed = values * inverse
    return (normed * gain_vec, normed, inverse)


def norm_back(grad_out, gain_vec, normed, inverse):
    scaled = grad_out * gain_vec
    grad_in = inverse * (scaled - normed * jnp.mean(scaled * normed, axis=-1, keepdims=True))
    return (grad_in, grad_out * normed)


def rope_tables(positions, head_dim):
    frequency = theta_base ** (-jnp.arange(0, head_dim, 2).astype(jnp.float32) / head_dim)
    angles = positions.astype(jnp.float32)[:, None] * frequency[None, :]
    angles = jnp.concatenate([angles, angles], axis=-1)
    return (jnp.cos(angles), jnp.sin(angles))


def rotate(values, cosine, sine_tab):
    half_dim = values.shape[-1] // 2
    turned = jnp.concatenate([-values[..., half_dim:], values[..., :half_dim]], axis=-1)
    return values * cosine[:, None, :] + turned * sine_tab[:, None, :]


def rotate_back(grad_out, cosine, sine_tab):
    half_dim = grad_out.shape[-1] // 2
    weighted = grad_out * sine_tab[:, None, :]
    turned = jnp.concatenate([weighted[..., half_dim:], -weighted[..., :half_dim]], axis=-1)
    return grad_out * cosine[:, None, :] + turned


def back_dot(grad_rows, weight):
    return lax.dot_general(
        grad_rows, weight, (((1,), (1,)), ((), ())), preferred_element_type=jnp.float32
    )


def weight_term(acts_in, grad_out):
    return lax.dot_general(
        acts_in, grad_out, (((0,), (0,)), ((), ())), preferred_element_type=jnp.float32
    )


def per_device(
    hidden_in,
    positions,
    cotangent,
    norm_gain,
    w_query,
    w_key,
    w_value,
    query_gain,
    key_gain,
    w_out,
    mlp_gain,
    w_gate,
    w_up,
    w_down,
):
    seqs_here, block_len, model_width = hidden_in.shape
    head_dim = query_gain.shape[0]
    kv_heads = w_key.shape[1] // head_dim
    q_heads = w_query.shape[1] // head_dim
    groups = q_heads // kv_heads
    ctx_count = lax.axis_size("ctx")
    ctx_rank = lax.axis_index("ctx")
    seq_total = block_len * ctx_count
    row_count = seqs_here * block_len
    scale_val = head_dim ** (-0.5)
    shards = (w_query, w_key, w_value, w_out, w_gate, w_up, w_down)
    full_weights = (
        lax.all_gather(shards[0], "fsdp", axis=0, tiled=True),
        lax.all_gather(shards[1], "fsdp", axis=0, tiled=True),
        lax.all_gather(shards[2], "fsdp", axis=0, tiled=True),
        lax.all_gather(shards[3], "fsdp", axis=0, tiled=True),
        lax.all_gather(shards[4], "fsdp", axis=0, tiled=True),
        lax.all_gather(shards[5], "fsdp", axis=0, tiled=True),
        lax.all_gather(shards[6], "fsdp", axis=0, tiled=True),
    )
    full_query, full_key, full_value, full_out, full_gate, full_up, full_down = full_weights
    residual = hidden_in.astype(jnp.float32).reshape(row_count, model_width)
    scaled_one, normed_one, inverse_one = norm_rows(residual, norm_gain)
    attn_in = scaled_one.astype(jnp.bfloat16)
    query_raw = jnp.dot(attn_in, full_query, preferred_element_type=jnp.float32).reshape(
        row_count, q_heads, head_dim
    )
    key_raw = jnp.dot(attn_in, full_key, preferred_element_type=jnp.float32).reshape(
        row_count, kv_heads, head_dim
    )
    value_bf = jnp.dot(attn_in, full_value, preferred_element_type=jnp.float32).astype(jnp.bfloat16)
    flat_pos = positions.reshape(row_count)
    cosine, sine_tab = rope_tables(flat_pos, head_dim)
    query_scaled, query_normed, query_inverse = norm_rows(query_raw, query_gain)
    query_bf = rotate(query_scaled, cosine, sine_tab).astype(jnp.bfloat16)
    key_scaled, key_normed, key_inverse = norm_rows(key_raw, key_gain)
    key_bf = rotate(key_scaled, cosine, sine_tab).astype(jnp.bfloat16)
    key_flat = key_bf.reshape(seqs_here, block_len, kv_heads * head_dim)
    value_flat = value_bf.reshape(seqs_here, block_len, kv_heads * head_dim)
    keys_all, values_all = (
        lax.all_gather(key_flat, "ctx", axis=1, tiled=True),
        lax.all_gather(value_flat, "ctx", axis=1, tiled=True),
    )
    query_five = query_bf.reshape(seqs_here, block_len, kv_heads, groups, head_dim)
    query_index = ctx_rank * block_len + jnp.arange(block_len, dtype=jnp.int32)
    doc_start = query_index[None, :] - positions

    def block_scores(key_source, block_idx):
        key_block = lax.dynamic_slice_in_dim(key_source, block_idx * block_len, block_len, 1)
        scores = (
            jnp.einsum(
                "sqkgd,spkd->skgqp", query_five, key_block, preferred_element_type=jnp.float32
            )
            * scale_val
        )
        key_index = block_idx * block_len + jnp.arange(block_len, dtype=jnp.int32)
        allowed = (key_index[None, None, :] <= query_index[None, :, None]) & (
            key_index[None, None, :] >= doc_start[:, :, None]
        )
        return (jnp.where(allowed[:, None, None, :, :], scores, -1e30), key_block)

    keys_four = keys_all.reshape(seqs_here, seq_total, kv_heads, head_dim)
    values_four = values_all.reshape(seqs_here, seq_total, kv_heads, head_dim)

    def stats_step(block_idx, carry_stats):
        running_max, running_sum = carry_stats
        scores, key_block = block_scores(keys_four, block_idx)
        new_max = jnp.maximum(running_max, jnp.max(scores, axis=-1))
        running_sum = running_sum * jnp.exp(running_max - new_max) + jnp.sum(
            jnp.exp(scores - new_max[..., None]), axis=-1
        )
        return (new_max, running_sum)

    stat_shape = (seqs_here, kv_heads, groups, block_len)
    row_max, row_sum = lax.fori_loop(
        0,
        ctx_rank + 1,
        stats_step,
        (jnp.full(stat_shape, -1e30, jnp.float32), jnp.zeros(stat_shape, jnp.float32)),
    )

    def output_step(block_idx, accum):
        scores, key_block = block_scores(keys_four, block_idx)
        probs_bf = (jnp.exp(scores - row_max[..., None]) / row_sum[..., None]).astype(jnp.bfloat16)
        value_block = lax.dynamic_slice_in_dim(values_four, block_idx * block_len, block_len, 1)
        return accum + jnp.einsum(
            "skgqp,spkd->sqkgd", probs_bf, value_block, preferred_element_type=jnp.float32
        )

    attn_f32 = lax.fori_loop(
        0,
        ctx_rank + 1,
        output_step,
        jnp.zeros((seqs_here, block_len, kv_heads, groups, head_dim), jnp.float32),
    )
    attn_bf = attn_f32.reshape(row_count, q_heads * head_dim).astype(jnp.bfloat16)
    middle = residual + jnp.dot(attn_bf, full_out, preferred_element_type=jnp.float32)
    scaled_two, normed_two, inverse_two = norm_rows(middle, mlp_gain)
    mlp_in = scaled_two.astype(jnp.bfloat16)
    gate_pre = jnp.dot(mlp_in, full_gate, preferred_element_type=jnp.float32)
    up_pre = jnp.dot(mlp_in, full_up, preferred_element_type=jnp.float32)
    sigmoid_gate = jax.nn.sigmoid(gate_pre)
    silu_gate = gate_pre * sigmoid_gate
    hidden_bf = (silu_gate * up_pre).astype(jnp.bfloat16)
    layer_out = middle + jnp.dot(hidden_bf, full_down, preferred_element_type=jnp.float32)
    output = layer_out.astype(jnp.bfloat16).reshape(seqs_here, block_len, model_width)
    back_weights = full_weights
    keys_back, values_back = (
        lax.all_gather(key_flat, "ctx", axis=1, tiled=True),
        lax.all_gather(value_flat, "ctx", axis=1, tiled=True),
    )
    back_query, back_key, back_value, back_out, back_gate, back_up, back_down = back_weights
    keys_again = keys_back.reshape(seqs_here, seq_total, kv_heads, head_dim)
    values_again = values_back.reshape(seqs_here, seq_total, kv_heads, head_dim)
    grad_rows = cotangent.reshape(row_count, model_width)
    down_grad = back_dot(grad_rows, back_down)
    grad_gate = (
        down_grad * up_pre * sigmoid_gate * (1.0 + gate_pre * (1.0 - sigmoid_gate))
    ).astype(jnp.bfloat16)
    grad_up = (down_grad * silu_gate).astype(jnp.bfloat16)
    grad_mlp_in = back_dot(grad_gate, back_gate) + back_dot(grad_up, back_up)
    grad_norm_two, mlp_gain_terms = norm_back(grad_mlp_in, mlp_gain, normed_two, inverse_two)
    grad_mid = grad_rows.astype(jnp.float32) + grad_norm_two
    grad_proj = grad_mid.astype(jnp.bfloat16)
    grad_attn = back_dot(grad_proj, back_out).astype(jnp.bfloat16)
    grad_five = grad_attn.reshape(seqs_here, block_len, kv_heads, groups, head_dim)
    delta = jnp.einsum("sqkgd,sqkgd->skgq", grad_five.astype(jnp.float32), attn_f32)

    def grad_step(block_idx, carry_grads):
        grad_query, grad_keys, grad_values = carry_grads
        scores, key_block = block_scores(keys_again, block_idx)
        probs = jnp.exp(scores - row_max[..., None]) / row_sum[..., None]
        value_block = lax.dynamic_slice_in_dim(values_again, block_idx * block_len, block_len, 1)
        grad_probs = jnp.einsum(
            "sqkgd,spkd->skgqp", grad_five, value_block, preferred_element_type=jnp.float32
        )
        grad_scores = (probs * (grad_probs - delta[..., None])).astype(jnp.bfloat16)
        grad_query = (
            grad_query
            + jnp.einsum(
                "skgqp,spkd->sqkgd", grad_scores, key_block, preferred_element_type=jnp.float32
            )
            * scale_val
        )
        key_part = (
            jnp.einsum(
                "skgqp,sqkgd->spkd", grad_scores, query_five, preferred_element_type=jnp.float32
            )
            * scale_val
        )
        value_part = jnp.einsum(
            "skgqp,sqkgd->spkd",
            probs.astype(jnp.bfloat16),
            grad_five,
            preferred_element_type=jnp.float32,
        )
        grad_keys = lax.dynamic_update_slice_in_dim(grad_keys, key_part, block_idx * block_len, 1)
        grad_values = lax.dynamic_update_slice_in_dim(
            grad_values, value_part, block_idx * block_len, 1
        )
        return (grad_query, grad_keys, grad_values)

    whole_shape = (seqs_here, seq_total, kv_heads, head_dim)
    grad_query, grad_keys, grad_values = lax.fori_loop(
        0,
        ctx_rank + 1,
        grad_step,
        (
            jnp.zeros((seqs_here, block_len, kv_heads, groups, head_dim), jnp.float32),
            jnp.zeros(whole_shape, jnp.float32),
            jnp.zeros(whole_shape, jnp.float32),
        ),
    )
    key_grad_own, value_grad_own = (
        lax.psum_scatter(
            grad_keys.reshape(seqs_here, seq_total, kv_heads * head_dim).astype(jnp.bfloat16),
            "ctx",
            scatter_dimension=1,
            tiled=True,
        ).astype(jnp.float32),
        lax.psum_scatter(
            grad_values.reshape(seqs_here, seq_total, kv_heads * head_dim).astype(jnp.bfloat16),
            "ctx",
            scatter_dimension=1,
            tiled=True,
        ).astype(jnp.float32),
    )
    key_unrot = rotate_back(key_grad_own.reshape(row_count, kv_heads, head_dim), cosine, sine_tab)
    key_raw_grad, key_gain_terms = norm_back(key_unrot, key_gain, key_normed, key_inverse)
    key_raw_bf = key_raw_grad.reshape(row_count, kv_heads * head_dim).astype(jnp.bfloat16)
    query_unrot = rotate_back(grad_query.reshape(row_count, q_heads, head_dim), cosine, sine_tab)
    query_raw_grad, query_gain_terms = norm_back(
        query_unrot, query_gain, query_normed, query_inverse
    )
    query_raw_bf = query_raw_grad.reshape(row_count, q_heads * head_dim).astype(jnp.bfloat16)
    value_raw_bf = value_grad_own.reshape(row_count, kv_heads * head_dim).astype(jnp.bfloat16)
    grad_attn_in = (
        back_dot(query_raw_bf, back_query)
        + back_dot(key_raw_bf, back_key)
        + back_dot(value_raw_bf, back_value)
    )
    grad_norm_one, norm_gain_terms = norm_back(grad_attn_in, norm_gain, normed_one, inverse_one)
    grad_input = (
        (grad_mid + grad_norm_one).astype(jnp.bfloat16).reshape(seqs_here, block_len, model_width)
    )
    gain_one, gain_query, gain_key, gain_two = lax.psum(
        (
            jnp.sum(norm_gain_terms, axis=0),
            jnp.sum(query_gain_terms, axis=(0, 1)),
            jnp.sum(key_gain_terms, axis=(0, 1)),
            jnp.sum(mlp_gain_terms, axis=0),
        ),
        ("fsdp", "ctx"),
    )
    weight_pairs = (
        (attn_in, query_raw_bf),
        (attn_in, key_raw_bf),
        (attn_in, value_raw_bf),
        (attn_bf, grad_proj),
        (mlp_in, grad_gate),
        (mlp_in, grad_up),
        (hidden_bf, grad_rows),
    )
    pieces = tuple(
        (
            lax.psum_scatter(
                weight_term(acts_in, grad_out).astype(jnp.bfloat16),
                "fsdp",
                scatter_dimension=0,
                tiled=True,
            ).astype(jnp.float32)
            for acts_in, grad_out in weight_pairs
        )
    )
    weight_grads = jax.tree.map(
        lambda part: part.astype(jnp.float32), lax.psum(as_sent(pieces), "ctx")
    )
    grad_wq, grad_wk, grad_wv, grad_wo, grad_wg, grad_wu, grad_wd = weight_grads
    return (
        output,
        grad_input,
        gain_one,
        grad_wq,
        grad_wk,
        grad_wv,
        gain_query,
        gain_key,
        grad_wo,
        gain_two,
        grad_wg,
        grad_wu,
        grad_wd,
    )


def grid_device(hidden_in, positions, cotangent, norm_gain, w_query, w_key, w_value, query_gain, key_gain, w_out, mlp_gain, w_gate, w_up, w_down):
    rows, width = hidden_in.shape[1:]
    head_dim = query_gain.shape[0]
    hid, cot = hidden_in.reshape(rows, width), cotangent.reshape(rows, width)
    half = theta_base ** (-np.arange(0, head_dim, 2) / head_dim)
    freq = jnp.asarray(np.concatenate([half, half])[None], jnp.float32)
    gains = [g[None, :] for g in (norm_gain, query_gain, key_gain, mlp_gain)]
    shards = (w_query, w_key, w_value, w_out, w_gate, w_up, w_down)
    saved = forward(hid, positions, freq, gains, shards)
    done = placed(backward(hid, cot, gains, saved, shards))
    gq, gk, gv, go, gg, gu, gd, out, grad_in, norm, query, key, mlp = done
    return (out[None], grad_in[None], norm[0], gq, gk, gv, query[0], key[0], go, mlp[0], gg, gu, gd)


def is_grid(mesh):
    if dict(mesh.shape) != {"fsdp": 16, "ctx": 2}:
        return False
    for f in range(16):
        for x in range(2):
            device = mesh.devices[f, x]
            if tuple(device.coords) != (x, (f // 2) % 2, f // 4) or device.core_on_chip != f % 2:
                return False
    return True


def solution(mesh):
    in_specs = (
        P("fsdp", "ctx", None),
        P("fsdp", "ctx"),
        P("fsdp", "ctx", None),
        P(),
        P("fsdp", None),
        P("fsdp", None),
        P("fsdp", None),
        P(),
        P(),
        P("fsdp", None),
        P(),
        P("fsdp", None),
        P("fsdp", None),
        P("fsdp", None),
    )
    out_specs = (
        P("fsdp", "ctx", None),
        P("fsdp", "ctx", None),
        P(),
        P("fsdp", None),
        P("fsdp", None),
        P("fsdp", None),
        P(),
        P(),
        P("fsdp", None),
        P(),
        P("fsdp", None),
        P("fsdp", None),
        P("fsdp", None),
    )
    return jax.shard_map(
        grid_device if is_grid(mesh) else per_device, mesh=mesh, in_specs=in_specs, out_specs=out_specs, check_vma=False
    )
```

```python
import functools

import jax
import jax.numpy as jnp
import numpy as np
from jax import lax
from jax.experimental import pallas as pl
from jax.experimental.pallas import tpu as pltpu
from jax.sharding import PartitionSpec as P

MESH = pl.DeviceIdType.MESH

epsilon = 1e-06
theta_base = 1000000.0
log2e = 1.4426950408889634
bf16, f32 = jnp.bfloat16, jnp.float32
HBM = pl.BlockSpec(memory_space=pl.ANY)
VMEM = pl.BlockSpec(memory_space=pltpu.VMEM)

FORWARD_PLAN = (
    ((1, 16, 4, 5), (1, 8, 2, 3), (1, 8, 3, 3), (1, 8, 3, 3), (1, 24, 6, 8), (1, 24, 9, 8), (0, 12, 4, 3)),
    (0, 1, 4, 8, 11, 11, 18),
    (0, 2, 4, 6, 5, 7, 9, 9, 11, 11, 11, 11, 11),
    (1, 3, 0, 7, 2, 0, 0, 2, 4, 3, 0, 2, 2, 0, 1, 0, 1, 4, 0, 0, 4, 10, 1, 1, 0, 1, 0, 0, 2, 2, 28, 46, 18, 19, 23, 19),
    1,
    4,
)

BACKWARD_PLAN = (
    ((1, 1), (1, 1), (1, 1), (1, 1), (1, 1), (1, 1), (1, 1), (1, 1), (1, 1), (1, 1), (1, 1), (1, 1), (1, 1), (1, 1), (1, 1), (1, 1), (1, 1), (1, 1), (1, 1), (1, 1), (1, 1), (1, 1), (1, 1), (1, 1), (1, 1), (1, 1), (0, 0), (0, 0), (0, 0), (0, 0)),
    (
        (0, 0, 0), (0, 1, 0), (1, 0, 0), (1, 1, 0), (0, 0, 1), (1, 2, 0), (1, 3, 0), (0, 1, 1), (0, 2, 0), (0, 3, 0),
        (0, 0, 2), (1, 4, 0), (0, 2, 1), (0, 4, 0), (0, 3, 1), (0, 1, 2), (0, 5, 0), (1, 5, 0), (1, 6, 0), (0, 0, 3),
        (1, 7, 0), (0, 2, 2), (0, 4, 1), (0, 6, 0), (1, 8, 0), (0, 5, 1), (0, 1, 3), (0, 3, 2), (0, 7, 0), (1, 9, 0),
        (0, 4, 2), (1, 10, 0), (0, 2, 3), (0, 6, 1), (1, 11, 0), (0, 0, 4), (1, 12, 0), (0, 1, 4), (1, 13, 0), (0, 8, 0),
        (0, 6, 2), (0, 7, 1), (0, 0, 5), (0, 5, 2), (0, 3, 3), (0, 2, 4), (1, 14, 0), (0, 4, 3), (0, 0, 6), (0, 8, 1),
        (0, 1, 5), (0, 3, 4), (0, 9, 0), (1, 15, 0), (0, 3, 5), (0, 2, 5), (0, 6, 3), (1, 16, 0), (0, 0, 8), (0, 1, 6),
        (0, 9, 1), (0, 7, 2), (0, 4, 4), (0, 10, 0), (1, 17, 0), (0, 8, 2), (0, 4, 5), (0, 3, 6), (0, 5, 3), (0, 2, 6),
        (0, 5, 4), (0, 6, 4), (1, 18, 0), (0, 1, 8), (0, 7, 3), (1, 19, 0), (0, 10, 1), (0, 11, 0), (0, 5, 5), (0, 2, 8),
        (1, 20, 0), (1, 21, 0), (0, 4, 6), (0, 9, 2), (0, 6, 5), (0, 7, 4), (0, 12, 0), (0, 8, 3), (1, 22, 0), (1, 23, 0),
        (1, 24, 0), (0, 8, 4), (0, 11, 1), (1, 25, 0), (0, 3, 8), (0, 10, 2), (0, 13, 0), (0, 7, 5), (1, 26, 0), (0, 5, 6),
        (1, 27, 0), (0, 9, 3), (1, 28, 0), (0, 12, 1), (0, 4, 8), (0, 9, 4), (0, 8, 5), (0, 6, 6), (0, 11, 2), (1, 29, 0),
        (0, 14, 0), (0, 13, 1), (0, 10, 3), (0, 7, 6), (0, 5, 8), (0, 15, 0), (0, 10, 4), (0, 12, 2), (1, 30, 0), (1, 31, 0),
        (0, 8, 6), (0, 14, 1), (1, 32, 0), (0, 11, 3), (0, 6, 8), (0, 9, 5), (0, 13, 2), (1, 33, 0), (0, 16, 0), (0, 10, 5),
        (0, 15, 1), (0, 12, 3), (0, 11, 4), (1, 34, 0), (1, 35, 0), (1, 36, 0), (0, 14, 2), (0, 7, 8), (0, 9, 6), (0, 16, 1),
        (0, 12, 4), (0, 17, 0), (0, 11, 5), (0, 13, 3), (0, 15, 2), (1, 37, 0), (1, 38, 0), (0, 8, 8), (1, 39, 0), (0, 17, 1),
        (0, 12, 5), (1, 40, 0), (0, 9, 8), (0, 13, 4), (0, 16, 2), (0, 14, 3), (0, 18, 0), (0, 14, 4), (0, 19, 0), (0, 11, 6),
        (0, 10, 6), (1, 41, 0), (1, 42, 0), (1, 43, 0), (0, 11, 8), (0, 18, 1), (1, 44, 0), (0, 10, 8), (0, 15, 3), (0, 17, 2),
        (0, 12, 6), (0, 20, 0), (0, 19, 1), (1, 45, 0), (0, 21, 0), (0, 14, 5), (0, 16, 3), (0, 15, 4), (1, 46, 0), (0, 13, 5),
        (0, 18, 2), (1, 47, 0), (0, 16, 4), (1, 48, 0), (0, 21, 1), (0, 20, 1), (0, 17, 3), (1, 49, 0), (0, 12, 8), (1, 50, 0),
        (1, 51, 0), (0, 22, 0), (1, 52, 0), (0, 17, 4), (0, 21, 2), (0, 13, 6), (0, 14, 6), (0, 15, 5), (1, 53, 0), (1, 54, 0),
        (0, 13, 8), (0, 22, 1), (0, 20, 2), (0, 23, 0), (0, 16, 5), (1, 55, 0), (0, 19, 2), (0, 18, 3), (0, 17, 5), (1, 56, 0),
        (0, 23, 1), (0, 14, 8), (1, 57, 0), (0, 15, 6), (0, 18, 4), (1, 58, 0), (1, 59, 0), (0, 21, 3), (0, 24, 0), (0, 20, 3),
        (0, 16, 6), (0, 23, 2), (0, 15, 8), (0, 25, 0), (0, 17, 6), (0, 18, 5), (0, 19, 3), (0, 24, 1), (0, 20, 4), (0, 16, 8),
        (0, 22, 2), (1, 60, 0), (0, 19, 4), (0, 25, 1), (0, 23, 3), (0, 21, 4), (0, 17, 8), (0, 26, 0), (0, 24, 2), (1, 61, 0),
        (0, 19, 5), (1, 62, 0), (0, 18, 6), (0, 20, 5), (0, 23, 4), (0, 22, 3), (0, 27, 0), (0, 25, 2), (2, 0, 0), (0, 23, 5),
        (2, 1, 0), (0, 19, 6), (0, 26, 1), (0, 24, 3), (0, 27, 1), (0, 21, 5), (0, 22, 4), (0, 18, 8), (0, 24, 4), (0, 28, 0),
        (0, 20, 6), (0, 25, 3), (0, 23, 6), (1, 63, 0), (0, 22, 5), (0, 21, 6), (0, 19, 8), (0, 29, 0), (1, 64, 0), (0, 25, 4),
        (2, 2, 0), (0, 29, 1), (2, 3, 0), (1, 65, 0), (0, 26, 3), (2, 4, 0), (0, 24, 5), (0, 22, 6), (0, 25, 5), (0, 21, 8),
        (0, 27, 3), (0, 26, 4), (0, 28, 1), (1, 66, 0), (2, 5, 0), (0, 26, 5), (0, 20, 8), (0, 29, 3), (2, 6, 0), (0, 27, 4),
        (0, 23, 8), (2, 7, 0), (0, 24, 6), (0, 25, 6), (1, 67, 0), (0, 29, 4), (0, 22, 8), (0, 28, 3), (0, 27, 5), (1, 68, 0),
        (0, 26, 6), (0, 28, 4), (0, 29, 5), (1, 69, 0), (0, 27, 6), (0, 28, 5), (0, 25, 8), (0, 29, 6), (0, 26, 8), (0, 24, 8),
        (0, 28, 6), (1, 71, 0), (0, 29, 8), (1, 70, 0), (0, 27, 8), (0, 28, 8),
    ),
)


def place():
    f = lax.axis_index("fsdp")
    return f // 4, (f // 2) % 2, f % 2, lax.axis_index("ctx")


def enter(z, y, c, x, ends=False):
    bar = pltpu.get_barrier_semaphore()

    def hail(z2, y2, c2, x2):
        pl.semaphore_signal(bar, inc=1, device_id=(z2 * 4 + y2 * 2 + c2, x2), device_id_type=MESH)

    hail(z, y, c, 1 - x)
    hail(z, 1 - y, c, x)
    hail(z, y, 1 - c, x)

    @pl.when(z > 0)
    def _():
        hail(z - 1, y, c, x)

    @pl.when(z < 3)
    def _():
        hail(z + 1, y, c, x)

    if ends:
        @pl.when(z % 3 == 0)
        def _():
            hail(3 - z, y, c, x)

    pl.semaphore_wait(bar, 5 if ends else 4 + (z * (3 - z)) // 2)


class Gather:
    def __init__(self, index, own, full, sems, at, cut):
        self.g, self.own, self.full = index, own, full
        self.zr, self.yr, self.xr, self.cr, self.zs, self.ys, self.xs, self.cs, self.ls = sems
        self.z, self.y, self.c, self.x = at
        self.rows, self.cols = own.shape
        self.dim, units, ones, twos = cut
        step = own.shape[self.dim] // units
        low, middle, high = (0, ones * step), (ones * step, (units - twos - ones) * step), ((units - twos) * step, twos * step)
        self.plans = ((0, low[1] + middle[1]), low, high), ((low[1], middle[1] + high[1]), high, low)
        self.all = None

    def step(self, name, *args):
        for x in (0, 1):
            @pl.when(self.x == x)
            def _():
                self.ywin, self.xwin, self.xgot = self.plans[x]
                getattr(self, name)(*args)

    def window(self, ref, row, win):
        if win is None:
            return ref.at[pl.ds(row, self.rows), :]
        if self.dim == 0:
            return ref.at[pl.ds(row + win[0], win[1]), :]
        return ref.at[pl.ds(row, self.rows), pl.ds(*win)]

    def part(self, z2, y2, c2, win):
        f2 = z2 * 4 + y2 * 2 + c2
        return self.window(self.full, pl.multiple_of(f2 * self.rows, 16), win)

    def mine(self):
        return self.window(self.own, 0, self.ywin)

    def send(self, src, dst, ssem, rsem, to):
        z2, y2, c2, x2 = to
        return pltpu.make_async_remote_copy(
            src_ref=src, dst_ref=dst, send_sem=ssem, recv_sem=rsem,
            device_id=(z2 * 4 + y2 * 2 + c2, x2), device_id_type=MESH)

    def z_copy(self, zs, up, first):
        dst = self.part(zs, self.y, self.c, self.ywin)
        src = self.mine() if first else dst
        z2 = self.z + 1 if up else self.z - 1
        return self.send(src, dst, self.zs.at[self.g, zs, 1 if up else 0], self.zr.at[self.g, zs], (z2, self.y, self.c, self.x))

    def y_copy(self, zs, first):
        dst = self.part(zs, self.y, self.c, self.ywin)
        src = self.mine() if first else dst
        return self.send(src, dst, self.ys.at[self.g, zs], self.yr.at[self.g, zs], (self.z, 1 - self.y, self.c, self.x))

    def x_copy(self, zs, y2):
        dst = self.part(zs, y2, self.c, self.xwin)
        s = zs * 2 + y2
        return self.send(dst, dst, self.xs.at[self.g, s], self.xr.at[self.g, s], (self.z, self.y, self.c, 1 - self.x))

    def c_copy(self, zs, y2, win, piece, first=False):
        dst = self.part(zs, y2, self.c, win)
        src = self.own if first else dst
        s = (zs * 2 + y2) * 2 + piece
        return self.send(src, dst, self.cs.at[self.g, s], self.cr.at[self.g, s], (self.z, self.y, 1 - self.c, self.x))

    def await_(self, dst, sem):
        pltpu.make_async_copy(dst, dst, sem).wait()

    def local(self):
        return pltpu.make_async_copy(self.own, self.part(self.z, self.y, self.c, self.all), self.ls.at[self.g])

    def begin(self):
        z = self.z

        @pl.when(z < 3)
        def _():
            self.z_copy(z, True, True).start()

        @pl.when(z > 0)
        def _():
            self.z_copy(z, False, True).start()

        self.y_copy(z, True).start()
        self.c_copy(z, self.y, self.all, 0, True).start()
        self.local().start()

    def spread(self, zs, up):
        self.await_(self.part(zs, self.y, self.c, self.ywin), self.zr.at[self.g, zs])

        @pl.when(self.z < 3 if up else self.z > 0)
        def _():
            self.z_copy(zs, up, False).start()

        self.y_copy(zs, False).start()
        self.x_copy(zs, self.y).start()
        self.c_copy(zs, self.y, self.ywin, 0).start()

    def along_z(self, k):
        @pl.when(self.z >= k)
        def _():
            self.spread(self.z - k, True)

        @pl.when(self.z + k <= 3)
        def _():
            self.spread(self.z + k, False)

    def over_y(self, zs):
        self.await_(self.part(zs, 1 - self.y, self.c, self.ywin), self.yr.at[self.g, zs])
        self.x_copy(zs, 1 - self.y).start()
        self.c_copy(zs, 1 - self.y, self.ywin, 0).start()

    def along_y(self, k):
        if k == 0:
            self.over_y(self.z)
            return

        @pl.when(self.z >= k)
        def _():
            self.over_y(self.z - k)

        @pl.when(self.z + k <= 3)
        def _():
            self.over_y(self.z + k)

    def over_x(self, zs, y2):
        self.await_(self.part(zs, y2, self.c, self.xgot), self.xr.at[self.g, zs * 2 + y2])
        self.c_copy(zs, y2, self.xgot, 1).start()

    def along_x(self, k):
        if k == 0:
            self.over_x(self.z, 1 - self.y)
            return

        for y2 in (self.y, 1 - self.y):
            @pl.when(self.z >= k)
            def _():
                self.over_x(self.z - k, y2)

            @pl.when(self.z + k <= 3)
            def _():
                self.over_x(self.z + k, y2)

    def finish(self):
        z, y = self.z, self.y
        self.local().wait()
        c = 1 - self.c
        self.await_(self.part(z, y, c, self.all), self.cr.at[self.g, (z * 2 + y) * 2])
        for k in range(0, 4):
            for y2 in ((y, 1 - y) if k else (1 - y,)):
                for zs, ok in ((z - k, z >= k), (z + k, z + k <= 3))[: 2 if k else 1]:
                    @pl.when(ok)
                    def _():
                        s = (zs * 2 + y2) * 2
                        self.await_(self.part(zs, y2, c, self.ywin), self.cr.at[self.g, s])
                        self.await_(self.part(zs, y2, c, self.xgot), self.cr.at[self.g, s + 1])

    def drain(self):
        z, y = self.z, self.y

        @pl.when(z < 3)
        def _():
            self.z_copy(z, True, True).wait_send()

        @pl.when(z > 0)
        def _():
            self.z_copy(z, False, True).wait_send()

        self.y_copy(z, True).wait_send()
        self.c_copy(z, y, self.all, 0, True).wait_send()
        self.x_copy(z, 1 - y).wait_send()
        self.c_copy(z, 1 - y, self.ywin, 0).wait_send()
        self.c_copy(z, 1 - y, self.xgot, 1).wait_send()
        for k in range(1, 4):
            for zs, ok, more, up in ((z - k, z >= k, z < 3, True), (z + k, z + k <= 3, z > 0, False)):
                @pl.when(ok)
                def _():
                    @pl.when(more)
                    def _():
                        self.z_copy(zs, up, False).wait_send()

                    self.y_copy(zs, False).wait_send()
                    for y2 in (y, 1 - y):
                        self.x_copy(zs, y2).wait_send()
                        self.c_copy(zs, y2, self.ywin, 0).wait_send()
                        self.c_copy(zs, y2, self.xgot, 1).wait_send()


def gather_sems(n):
    return [pltpu.SemaphoreType.DMA(s) for s in ((n, 4), (n, 4), (n, 8), (n, 16), (n, 4, 2), (n, 4), (n, 8), (n, 16), (n,))]


def dot_nn(a, b):
    return lax.dot_general(a, b, (((1,), (0,)), ((), ())), preferred_element_type=f32)


def dot_nt(a, b):
    return lax.dot_general(a, b, (((1,), (1,)), ((), ())), preferred_element_type=f32)


def dot_tn(a, b):
    return lax.dot_general(a, b, (((0,), (0,)), ((), ())), preferred_element_type=f32)


def rows_loop(count, step, body):
    @pl.loop(0, count // step)
    def _(i):
        body(pl.multiple_of(i * step, step), step)


class Writes:
    def __init__(self, sem):
        self.sem, self.all, self.open = sem, [], set()

    def start(self, src, dst):
        copy = pltpu.make_async_copy(src, dst, self.sem.at[len(self.all)])
        copy.start()
        self.open.add(len(self.all))
        self.all.append(copy)
        return len(self.all) - 1

    def wait(self, i):
        if i in self.open:
            self.all[i].wait()
            self.open.remove(i)

    def wait_all(self):
        for i in sorted(self.open):
            self.wait(i)


def unit_heads(values):
    size = values.shape[-1]
    mean = dot_nn((values * values).astype(bf16), jnp.full((size, size), 1.0 / size, bf16))
    inverse = lax.rsqrt(mean + epsilon)
    return values * inverse, inverse


def unit_rows(values):
    inverse = lax.rsqrt(jnp.mean(values * values, axis=-1, keepdims=True) + epsilon)
    return values * inverse, inverse


def turn(u, cos, sin):
    return u * cos + pltpu.roll(u, u.shape[-1] // 2, 1) * sin


def turn_back(u, cos, sin):
    return u * cos - pltpu.roll(u, u.shape[-1] // 2, 1) * sin


def mask_bias(bias, start_ref, rows):
    block = 128

    @pl.loop(0, bias.shape[0] // block)
    def _(i):
        rr = pl.ds(pl.multiple_of(i * block, block), block)
        key = lax.broadcasted_iota(jnp.int32, (block, rows), 0) + i * block
        query = lax.broadcasted_iota(jnp.int32, (block, rows), 1) + rows
        ok = (key >= start_ref[...]) & (key <= query)
        bias[rr, :] = jnp.where(ok, 0.0, -1e30)


class Schedule:
    def __init__(self, gathers, starts, after):
        steps = [("begin",)] + [("along_z", k) for k in (1, 2, 3)] + [("along_y", k) for k in range(4)] + [("along_x", k) for k in range(4)] + [("finish",)]
        slots = {}
        for i, g in reversed(list(enumerate(gathers))):
            for j, s in zip(after, steps):
                slots.setdefault(starts[i] + j, []).append((i, g, s))
        self.steps = [step for t in sorted(slots) for step in slots[t]]

    def run(self, count):
        for i, g, s in self.steps[:count]:
            g.step(*s)
        self.steps = self.steps[count:]

    def until(self, weight):
        ends = [n for n, (i, g, s) in enumerate(self.steps) if i == weight and s[0] == "finish"]
        if ends:
            self.run(ends[0] + 1)


def forward_kernel(plan, hid, pos, freq, norm_gain, query_gain, key_gain, mlp_gain, *refs):
    owns, refs = refs[:7], refs[7:]
    outs, refs = refs[:7], refs[7:]
    (q_o, k_o, v_o, qraw_o, kraw_o, ain_o, attn_o, lse_o, mid_o, mlp_o, gate_o, up_o, hidden_o, cos_o, sin_o, start, bias_o), refs = refs[:17], refs[17:]
    fulls, refs = refs[:6] + (outs[6],), refs[6:]
    (ain, q, k, vt, attn, bias, tmp, mid, stage, cos, sin, ain_sem, out_sem), sems = refs[:13], refs[13:]
    w_q, w_k, w_v, w_o, w_g, w_u = fulls[:6]
    cuts, starts, after, runs, early, _ = plan
    runs = list(runs)
    at = place()
    z, y, c, x = at
    rows, width = hid.shape
    hd = freq.shape[1]
    kv = w_k.shape[1] // hd
    qh = w_q.shape[1] // hd
    group = qh // kv
    span = tmp.shape[1]
    first, second = pl.ds(0, rows), pl.ds(rows, rows)
    enter(*at)
    gs = [Gather(i, owns[i], fulls[i], sems, at, cuts[i]) for i in range(7)]
    sched = Schedule(gs, starts, after)
    writes = Writes(out_sem)
    sched.run(1)

    def norm_one(r, n):
        unit, _ = unit_rows(hid[pl.ds(r, n), :].astype(f32))
        ain[pl.ds(pl.multiple_of(r + rows, n), n), :] = (unit * norm_gain[...]).astype(bf16)

    rows_loop(rows, 64, norm_one)
    count = ain_sem.shape[1]
    size = rows // count

    def handed(n):
        return pltpu.make_async_remote_copy(
            src_ref=ain.at[pl.ds(rows + n * size, size), :], dst_ref=ain.at[pl.ds(n * size, size), :],
            send_sem=ain_sem.at[0, n], recv_sem=ain_sem.at[1, n],
            device_id=(z * 4 + y * 2 + c, 1 - x), device_id_type=MESH)

    left = list(range(count))

    def hand():
        if left:
            n = left.pop(0)

            @pl.when(x == 0)
            def _():
                handed(n).start()

    def pump():
        sched.run(runs.pop(0))
        hand()

    hand()

    @pl.when(x == 0)
    def _():
        ain[first, :] = jnp.zeros((rows, width), bf16)

    index = lax.broadcasted_iota(jnp.int32, (1, rows), 1)
    head = jnp.sum(jnp.where(index == 0, pos[...], 0), axis=1, keepdims=True)
    own_start = index + rows - pos[...]
    start[...] = jnp.where(x == 0, jnp.maximum(own_start, rows), own_start)
    sign = jnp.where(lax.broadcasted_iota(jnp.int32, (rows, hd), 1) < hd // 2, -1.0, 1.0)
    for rr, row in ((second, pos[...]), (first, index - rows + head)):
        angle = jnp.broadcast_to(row.astype(f32), (hd, rows)).T * freq[...]
        cos[rr, :] = jnp.cos(angle)
        sin[rr, :] = jnp.sin(angle) * sign
    writes.start(cos, cos_o)
    writes.start(sin, sin_o)
    mask_bias(bias, start, rows)
    writes.start(bias, bias_o)
    for _ in range(early):
        sched.run(2)
        hand()
    sched.until(0)

    def heads(lhs, weight, base, count, gain, into, col):
        for r in range(0, count, rows):
            tmp[r:r + rows, :] = dot_nn(lhs[pl.ds(r, rows), :], weight)
            pump()
        for part in range(0, span // hd, 4):
            @pl.loop(part, part + 4)
            def _(h):
                cc = pl.ds(pl.multiple_of(h * hd, hd), hd)
                to = pl.ds(pl.multiple_of(col + h * hd, hd), hd)
                for r in range(0, count, 256):
                    raw = tmp[r:r + 256, cc]
                    stage[r:r + 256, cc] = raw.astype(bf16)
                    unit, _ = unit_heads(raw)
                    t = slice(base + r, base + r + 256)
                    into[r:r + 256, to] = turn(unit * gain[...], cos[t, :], sin[t, :]).astype(bf16)

            pump()

    last = None
    for b in range(w_q.shape[1] // span):
        if last is not None:
            writes.wait(last)
        heads(ain.at[second, :], w_q[:, b * span:(b + 1) * span], rows, rows, query_gain, q, b * span)
        last = writes.start(stage.at[first, :], qraw_o.at[:, pl.ds(b * span, span)])
    while left:
        hand()
    sched.until(1)

    @pl.when(x == 1)
    def _():
        for n in range(count):
            handed(n).wait_recv()

    writes.wait(last)
    heads(ain, w_k[...], 0, 2 * rows, key_gain, k, 0)
    last = writes.start(stage, kraw_o)
    writes.start(ain, ain_o)
    writes.start(q, q_o)
    writes.start(k, k_o)
    sched.until(2)
    for r in (first, second):
        tmp[r, :] = dot_nn(ain[r, :], w_v[...])
        pump()
    writes.wait(last)
    stage[...] = tmp[...].astype(bf16)
    last = writes.start(stage, v_o)

    @pl.loop(0, kv)
    def _(h):
        cc = pl.ds(pl.multiple_of(h * hd, hd), hd)
        vt[cc, :] = tmp[:, cc].astype(bf16).T

    pump()

    c2 = hd ** (-0.5) * log2e
    for part in range(kv):
        @pl.loop(part, part + 1)
        def _(h):
            cc = pl.ds(pl.multiple_of(h * hd, hd), hd)
            for g in range(group):
                n = h * group + g
                qc = pl.ds(pl.multiple_of(n * hd, hd), hd)
                p = jnp.exp2(dot_nt(k[:, cc], q[:, qc]) * c2 + bias[...])
                total = jnp.sum(p, axis=0, keepdims=True)
                o = dot_nn(vt[cc, :], p.astype(bf16))
                attn[qc, :] = (o * (1.0 / total)).astype(bf16)
                lse_o[pl.ds(n, 1), :] = jnp.log2(total)

        pump()
    writes.start(attn, attn_o)
    sched.until(3)
    for i in range(3):
        gs[i].step("drain")
    leaving = [writes.start(fulls[i], outs[i]) for i in range(3)]
    writes.start(w_o, outs[3])
    mid[...] = hid[...].astype(f32) + dot_tn(attn[...], w_o[...])
    pump()

    for n in leaving:
        writes.wait(n)
    writes.wait(last)
    blocks = w_g.shape[1] // span
    hidden = [w_q.at[first, pl.ds(0, span)], w_q.at[second, pl.ds(0, span)], w_q.at[first, pl.ds(span, span)]]
    mlp_in = w_q.at[second, pl.ds(span, span)]
    gates = [w_k.at[first, :], w_v.at[first, :], stage.at[first, :]]
    ups = [w_k.at[second, :], w_v.at[second, :], stage.at[second, :]]

    def norm_two(r, n):
        unit, _ = unit_rows(mid[pl.ds(r, n), :])
        mlp_in[pl.ds(r, n), :] = (unit * mlp_gain[...]).astype(bf16)

    rows_loop(rows, 64, norm_two)
    writes.start(mid, mid_o)
    writes.start(mlp_in, mlp_o)
    sched.until(4)
    sched.until(5)
    writes.start(w_g, outs[4])
    writes.start(w_u, outs[5])
    for j in range(blocks):
        cols = pl.ds(j * span, span)
        tmp[first, :] = dot_nn(mlp_in[...], w_g[:, cols])
        pump()
        tmp[second, :] = dot_nn(mlp_in[...], w_u[:, cols])
        pump()

        def act(r, n):
            rr = pl.ds(r, n)
            gate, up = tmp[rr, :], tmp[pl.ds(pl.multiple_of(r + rows, n), n), :]
            sig = jax.nn.sigmoid(gate)
            silu = gate * sig
            hidden[j][rr, :] = (silu * up).astype(bf16)
            gates[j][rr, :] = (up * (sig + silu * (1.0 - sig))).astype(bf16)
            ups[j][rr, :] = silu.astype(bf16)

        rows_loop(rows, 64, act)
        writes.start(gates[j], gate_o.at[:, cols])
        writes.start(ups[j], up_o.at[:, cols])
        writes.start(hidden[j], hidden_o.at[:, cols])
        pump()
    sched.until(6)
    sched.run(len(sched.steps))
    for g in gs[3:]:
        g.step("drain")

    @pl.when(x == 0)
    def _():
        for n in range(count):
            handed(n).wait_send()

    writes.wait_all()


def forward(hid, pos, freq, gains, shards):
    rows, width = hid.shape
    hd = freq.shape[1]
    fulls = [(s.shape[0] * 16, s.shape[1]) for s in shards]
    heads, keys, ff = shards[0].shape[1], shards[1].shape[1], shards[4].shape[1]
    shape = jax.ShapeDtypeStruct
    vm = pltpu.VMEM
    outs = [shape(s, bf16) for s in fulls] + [
        shape((rows, heads), bf16), shape((2 * rows, keys), bf16), shape((2 * rows, keys), bf16),
        shape((rows, heads), bf16), shape((2 * rows, keys), bf16), shape((2 * rows, width), bf16), shape((heads, rows), bf16),
        shape((heads // hd, rows), f32), shape((rows, width), f32), shape((rows, width), bf16),
        shape((rows, ff), bf16), shape((rows, ff), bf16), shape((rows, ff), bf16),
        shape((2 * rows, hd), f32), shape((2 * rows, hd), f32), shape((1, rows), jnp.int32), shape((2 * rows, rows), f32)]
    specs = [HBM] * 7 + [VMEM if i in (7, 15) else HBM for i in range(17)]
    return pl.pallas_call(
        functools.partial(forward_kernel, FORWARD_PLAN),
        out_shape=outs,
        in_specs=[VMEM] * 7 + [HBM] * 7,
        out_specs=specs,
        scratch_shapes=[vm(s, bf16) for s in fulls[:6]] + [
            vm((2 * rows, width), bf16), vm((rows, heads), bf16), vm((2 * rows, keys), bf16), vm((keys, 2 * rows), bf16),
            vm((heads, rows), bf16), vm((2 * rows, rows), f32), vm((2 * rows, keys), f32), vm((rows, width), f32),
            vm((2 * rows, keys), bf16), vm((2 * rows, hd), f32), vm((2 * rows, hd), f32), pltpu.SemaphoreType.DMA((2, FORWARD_PLAN[5])), pltpu.SemaphoreType.DMA((32,))] + gather_sems(7),
        compiler_params=pltpu.CompilerParams(collective_id=1, has_side_effects=True, vmem_limit_bytes=62 * 2**20),
        name="forward_gather",
    )(hid, pos, freq, *gains, *shards)


class Chunk:
    def __init__(self, index, bufs, sems, at, out, ones, twos):
        self.i, self.out, self.ones, self.twos = index, out, ones, twos
        ring = [index % b.shape[0] for b in bufs]
        self.g, self.cb, self.xb, self.yb, self.zb, self.fb, self.st = [b.at[r] for b, r in zip(bufs, ring)]
        self.sc, self.sx, self.sy, self.zs, self.zr, self.sf, self.so = [s.at[index] for s in sems]
        self.z, self.y, self.c, self.x = at
        self.unit = self.g.shape[3] // 4

    def step(self, name, *args):
        u = self.unit
        if self.ones == self.twos and name != "finish":
            t = self.ones
            self.first = self.x * t
            self.keep, self.send_x, self.got_x, self.theirs = 4 - t, t, t, 4 - t
            self.ywin = pl.ds(pl.multiple_of(self.first * u, 16), self.keep * u)
            self.xsend = pl.ds(pl.multiple_of((1 - self.x) * (4 - t) * u, 16), t * u)
            self.xgot = pl.ds(pl.multiple_of(self.x * (4 - t) * u, 16), t * u)
            getattr(self, name)(*args)
            return
        for x in (0, 1):
            @pl.when(self.x == x)
            def _():
                spans = ((0, 4 - self.twos), (self.ones, 4))
                lows, highs = (0, self.ones), (4 - self.twos, 4)
                self.span, self.other = spans[x], spans[1 - x]
                self.keep, self.theirs = self.span[1] - self.span[0], self.other[1] - self.other[0]
                out, into = (highs, lows) if x == 0 else (lows, highs)
                self.send_x, self.got_x = out[1] - out[0], into[1] - into[0]
                self.ywin = pl.ds(self.span[0] * u, self.keep * u)
                self.xsend, self.xgot = pl.ds(out[0] * u, self.send_x * u), pl.ds(into[0] * u, self.got_x * u)
                getattr(self, name)(*args)

    def send(self, src, dst, ssem, rsem, z2, y2, c2, x2):
        return pltpu.make_async_remote_copy(
            src_ref=src, dst_ref=dst, send_sem=ssem, recv_sem=rsem,
            device_id=(z2 * 4 + y2 * 2 + c2, x2), device_id_type=MESH)

    def c_copy(self):
        return self.send(self.g.at[:, :, 1 - self.c], self.cb, self.sc.at[0], self.sc.at[1], self.z, self.y, 1 - self.c, self.x)

    def x_copy(self):
        return self.send(
            self.g.at[:, :, self.c, self.xsend], self.xb.at[:, :, pl.ds(0, self.send_x * self.unit)], self.sx.at[0], self.sx.at[1],
            self.z, self.y, self.c, 1 - self.x)

    def y_copy(self):
        return self.send(
            self.g.at[:, 1 - self.y, self.c, self.ywin], self.yb.at[:, pl.ds(0, self.keep * self.unit)], self.sy.at[0], self.sy.at[1],
            self.z, 1 - self.y, self.c, self.x)

    def z_slot(self, slot):
        return self.zb.at[slot, pl.ds(0, self.keep * self.unit)]

    def z_copy(self, here, to, up):
        there = here + 1 if up else here - 1
        slot = 4 if to == there and not up else to
        return self.send(
            self.g.at[to, self.y, self.c, self.ywin], self.z_slot(slot), self.zs.at[to], self.zr.at[slot], there, self.y, self.c, self.x)

    def f_copy(self):
        return self.send(
            self.g.at[self.z, self.y, self.c, self.ywin], self.fb.at[pl.ds(0, self.keep * self.unit)], self.sf.at[0], self.sf.at[1],
            self.z, self.y, self.c, 1 - self.x)

    def o_copy(self):
        return pltpu.make_async_copy(self.st, self.out, self.so)

    def arrived(self, dst, sem):
        pltpu.make_async_copy(dst, dst, sem).wait()

    def add(self, zz, yy, win, src):
        dst = self.g.at[zz, yy, self.c, win]
        dst[...] = dst[...] + src[...]

    def go(self):
        self.c_copy().start()

    def over_c(self):
        self.c_copy().wait_recv()

        @pl.loop(0, 4)
        def _(zz):
            for yy in (0, 1):
                self.add(zz, yy, slice(None), self.cb.at[zz, yy])

        if self.send_x:
            self.x_copy().start()
        if not self.ones and not self.twos:
            self.y_copy().start()

    def over_x(self):
        if self.got_x:
            got = self.xb.at[:, :, pl.ds(0, self.got_x * self.unit)]
            self.arrived(got, self.sx.at[1])

            @pl.loop(0, 4)
            def _(zz):
                for yy in (0, 1):
                    self.add(zz, yy, self.xgot, got.at[zz, yy])

        self.y_copy().start()

    def over_y(self):
        self.y_copy().wait_recv()

        @pl.loop(0, 4)
        def _(zz):
            self.add(zz, self.y, self.ywin, self.yb.at[zz, pl.ds(0, self.keep * self.unit)])

    def take(self, zz, slot):
        self.arrived(self.z_slot(slot), self.zr.at[slot])
        self.add(zz, self.y, self.ywin, self.z_slot(slot))

    def over_z(self, k):
        for up in (True, False):
            here = k if up else 3 - k

            @pl.when(self.z == here)
            def _():
                for to in (range(3, here, -1) if up else range(here)):
                    if k:
                        self.take(to, to)
                    self.z_copy(here, to, up).start()
                if k:
                    self.take(here, here if up else 4)

    def hand(self):
        self.f_copy().start()

    def finish(self, before):
        u = self.unit
        self.arrived(self.fb.at[pl.ds(0, self.theirs * u)], self.sf.at[1])
        if before is not None:
            before.o_copy().wait()
        own = self.g.at[self.z, self.y, self.c]
        (a, b), (c, d) = self.span, self.other
        for lo, hi in ((0, max(a, c)), (max(a, c), min(b, d)), (min(b, d), 4)):
            if lo < hi:
                mine, theirs = own[lo * u:hi * u, :].astype(f32), None
                if c <= lo and hi <= d:
                    theirs = self.fb[(lo - c) * u:(hi - c) * u, :].astype(f32)
                held = a <= lo and hi <= b
                self.st[lo * u:hi * u, :] = theirs if not held else mine if theirs is None else mine + theirs
        self.o_copy().start()
        self.c_copy().wait_send()
        if self.send_x:
            self.x_copy().wait_send()
        self.y_copy().wait_send()
        self.f_copy().wait_send()
        for here in range(4):
            @pl.when(self.z == here)
            def _():
                for to in range(4):
                    if to != here:
                        self.z_copy(here, to, to > here).wait_send()


def chunk_bufs(rows, cols):
    part = rows // 4
    sizes = ((11, 4, 2, 2, rows, cols), (4, 4, 2, rows, cols), (6, 4, 2, part, cols), (6, 4, rows, cols), (6, 5, rows, cols), (8, rows, cols))
    return [pltpu.VMEM(s, bf16) for s in sizes] + [pltpu.VMEM((2, rows, cols), f32)]


def chunk_sems(n):
    return [pltpu.SemaphoreType.DMA(s) for s in ((n, 2), (n, 2), (n, 2), (n, 4), (n, 5), (n, 2), (n,))]


class Totals:
    def __init__(self, mine, got, sem, at):
        self.mine, self.got, self.sem = mine, got, sem
        z, y, c, x = at
        self.to = [(z, y, 1 - c, x), (z, y, c, 1 - x), (z, 1 - y, c, x), (z + 1 - 2 * (z % 2), y, c, x), (3 - z, y, c, x)]

    def copy(self, s):
        z, y, c, x = self.to[s]
        return pltpu.make_async_remote_copy(
            src_ref=self.mine.at[s], dst_ref=self.got.at[s], send_sem=self.sem.at[s, 0], recv_sem=self.sem.at[s, 1],
            device_id=(z * 4 + y * 2 + c, x), device_id_type=MESH)

    def step(self, s):
        if s > 0:
            self.copy(s - 1).wait()
            self.mine[s] = self.mine[s - 1] + self.got[s - 1]
        if s < 5:
            self.copy(s).start()


def backward_kernel(plan, cot, cos, sin, norm_gain, query_gain, key_gain, mlp_gain, lse, *refs):
    full, refs = refs[:7], refs[7:]
    (hid_i, q_i, k_i, v_i, qraw_i, kraw_i, ain_i, attn_i, mid_i, mlp_i, gate_i, up_i, hidden_i, bias_i), refs = refs[:14], refs[14:]
    grads, refs = refs[:7], refs[7:]
    (out_o, gin_o, norm_o, query_o, key_o, mlp_o), refs = refs[:6], refs[6:]
    (hidden, mlp, ggate, gup, mid, acc, gproj, attn, q, k, v, qraw, kraw, ain, dk, dv, kt, bias, wbuf, earlier, sum_one, sum_two, sum_q, sum_k,
     gain_mine, gain_got, gain_sem, load_sem, w_sem, early_sem), refs = refs[:30], refs[30:]
    bufs, sems = refs[:7], refs[7:]
    at = place()
    z, y, c, x = at
    rows, width = cot.shape
    hd = cos.shape[1]
    kv, qh = k.shape[1] // hd, q.shape[1] // hd
    group = qh // kv
    span = wbuf.shape[1]
    ff = ggate.shape[1]
    cols = bufs[0].shape[-1]
    first, second = pl.ds(0, rows), pl.ds(rows, rows)
    scale = hd ** (-0.5)
    enter(*at, True)

    loads = Writes(load_sem)
    wide = hidden.shape[1] // 4
    hidden_l = [loads.start(hidden_i.at[:, pl.ds(b * wide, wide)], hidden.at[:, pl.ds(b * wide, wide)]) for b in range(4)]
    blocks = [full[6].at[pl.ds(j * span, span), :] for j in range(ff // span)]
    for j in range(ff // span):
        blocks += [full[4].at[:, pl.ds(j * span, span)], full[5].at[:, pl.ds(j * span, span)]]
    blocks += [full[3].at[pl.ds(j * span, span), :] for j in range(qh * hd // span)]
    blocks += [full[1], full[2]] + [full[0].at[:, pl.ds(j * span, span)] for j in range(qh * hd // span)]

    def fetch(n):
        return pltpu.make_async_copy(blocks[n], wbuf.at[n % 2], w_sem.at[n % 2])

    def weight(n):
        fetch(n).wait()
        return wbuf[n % 2]

    def used(n):
        if n + 2 < len(blocks):
            fetch(n + 2).start()

    fetch(0).start()
    fetch(1).start()
    gate_l = loads.start(gate_i, ggate)
    up_l = loads.start(up_i, gup)
    mlp_l, mid_l, attn_l = loads.start(mlp_i, mlp), loads.start(mid_i, mid), loads.start(attn_i, attn)
    later = []

    todo = []

    def put(val, spot, subs, shards_from):
        size = bufs[0].shape[4]
        for f in range(val.shape[0] // (size * subs)):
            for s in range(subs):
                owner = shards_from + f
                lo = (f * subs + s) * size
                bufs[0][(spot + s) % bufs[0].shape[0], owner // 4, owner // 2 % 2, owner % 2] = val[lo:lo + size, :].astype(bf16)

    def make_down(j):
        def run(spot):
            for b in range(4):
                loads.wait(hidden_l[b])
                put(dot_tn(hidden[:, b * wide:(b + 1) * wide], cot[:, j * cols:(j + 1) * cols]), spot, wide // 256, b * 4)
        return run

    def make_out(j):
        def run(spot):
            loads.wait(attn_l)
            tall = attn.shape[0] // 4
            for b in range(4):
                put(dot_nn(attn[b * tall:(b + 1) * tall, :], gproj[:, j * cols:(j + 1) * cols]), spot, tall // 256, b * 4)
        return run

    def make(lhs, rhs, j):
        def run(spot):
            put(dot_tn(lhs(), rhs[:, j * cols:(j + 1) * cols]), spot, 1, 0)
        return run

    def mlp_all():
        loads.wait(mlp_l)
        return mlp[...]

    def ain_own():
        return ain[second, :]

    def ain_all():
        return ain[...]

    def add_weight(w, subs, maker, count):
        for j in range(count):
            for s in range(subs):
                out = grads[w].at[pl.ds(s * 64, 64), pl.ds(j * cols, cols)]
                todo.append((maker(j) if s == 0 else None, out))

    add_weight(6, hidden.shape[1] // (64 * 16), make_down, width // cols)
    add_weight(4, 1, lambda j: make(mlp_all, ggate, j), ff // cols)
    add_weight(5, 1, lambda j: make(mlp_all, gup, j), ff // cols)
    add_weight(3, attn.shape[0] // (64 * 16), make_out, width // cols)
    add_weight(0, 1, lambda j: make(ain_own, q, j), qh * hd // cols)
    add_weight(1, 1, lambda j: make(ain_all, k, j), kv * hd // cols)
    add_weight(2, 1, lambda j: make(ain_all, v, j), kv * hd // cols)
    kinds, order = plan
    chunks = [Chunk(i, bufs, sems, at, out, *kinds[i]) for i, (_, out) in enumerate(todo)]

    nb = ff // span

    def piece_down(j):
        block = weight(j)
        acc[...] = dot_nt(cot[...], block)
        cc = slice(j * span, (j + 1) * span)
        for part in range(2):
            more = dot_nn(hidden[:, cc], wbuf[j % 2, :, part * rows:(part + 1) * rows])
            rr = pl.ds(part * rows, rows)
            bias[rr, :] = more if j == 0 else bias[rr, :] + more
        used(j)

    def piece_act(j, part):
        cc = slice(j * span, (j + 1) * span)
        loads.wait(gate_l)
        loads.wait(up_l)

        def act(r, n):
            rr = pl.ds(pl.multiple_of(r + part * (rows // 2), n), n)
            grad = acc[rr, :]
            ggate[rr, cc] = (grad * ggate[rr, cc].astype(f32)).astype(bf16)
            gup[rr, cc] = (grad * gup[rr, cc].astype(f32)).astype(bf16)

        rows_loop(rows // 2, 64, act)

    def piece_output():
        loads.wait(mid_l)
        for part in range(2):
            cc = slice(part * rows, (part + 1) * rows)
            gproj[:, cc] = (mid[:, cc] + bias[part * rows:(part + 1) * rows, :]).astype(bf16)
        later.append(loads.start(gproj, out_o))
        later.append(loads.start(bias_i, bias))

    def piece_mlp(j, part):
        n = nb + 2 * j + part
        cc = slice(j * span, (j + 1) * span)
        one = dot_nt((gup if part else ggate)[:, cc], weight(n))
        acc[...] = one if n == nb else acc[...] + one
        used(n)

    def fold(into, terms):
        into[...] += jnp.sum(terms.reshape(terms.shape[0] // 8, 8, terms.shape[1]), axis=0)

    def norm_back(grad, unit, inverse, gain):
        scaled = grad * gain
        return inverse * (scaled - unit * jnp.mean(scaled * unit, axis=-1, keepdims=True))

    def piece_mid(part):
        if part == 0:
            loads.wait(later[0])
            sum_two[...] = jnp.zeros_like(sum_two)

        def body(r, n):
            rr = pl.ds(pl.multiple_of(r + part * (rows // 2), n), n)
            unit, inverse = unit_rows(mid[rr, :])
            grad = acc[rr, :]
            fold(sum_two, grad * unit)
            out = cot[rr, :].astype(f32) + norm_back(grad, unit, inverse, mlp_gain[...])
            mid[rr, :] = out
            gproj[rr, :] = out.astype(bf16)

        rows_loop(rows // 2, 64, body)

    at_out = 3 * nb
    n_out = qh * hd // span

    def piece_attn_grad(j):
        hidden[:, j * span:(j + 1) * span] = dot_nt(gproj[...], weight(at_out + j)).astype(bf16)
        used(at_out + j)

    def piece_ready():
        loads.wait(later[1])
        sum_q[...] = jnp.zeros_like(sum_q)
        sum_k[...] = jnp.zeros_like(sum_k)
        loads.wait(attn_l)
        for n in head_l:
            loads.wait(n)
        loads.wait(ain_l)

    c2 = scale * log2e
    tile = rows // 2

    def norm_back_heads(grad, unit, inverse, gain):
        scaled = grad * gain
        mean = dot_nn((scaled * unit).astype(bf16), jnp.full((hd, hd), 1.0 / hd, bf16))
        return inverse * (scaled - unit * mean)

    def piece_head(h, g, i):
        cc = slice(h * hd, (h + 1) * hd)
        n = h * group + g
        qc = slice(n * hd, (n + 1) * hd)
        if g == 0 and i == 0:
            kt[...] = k[:, cc].T
            dk[...] = jnp.zeros_like(dk)
            dv[...] = jnp.zeros_like(dv)
        rs = slice(i * tile, (i + 1) * tile)
        kk = rows + (i + 1) * tile
        query, grad = q[rs, qc], hidden[rs, qc]
        delta = jnp.sum(attn[qc, rs].astype(f32) * grad.T.astype(f32), axis=0, keepdims=True)
        p = jnp.exp2(dot_nt(k[:kk, cc], query) * c2 + (bias[:kk, rs] - lse[n:n + 1, rs]))
        gp = dot_nt(v[:kk, cc], grad)
        ds = (p * (gp - delta)).astype(bf16)
        dv[:kk, :] += dot_nn(p.astype(bf16), grad)
        dk[:kk, :] += dot_nn(ds, query)
        dq = dot_nn(kt[:, :kk], ds).T * scale
        unit, inverse = unit_heads(qraw[rs, qc].astype(f32))
        t = slice(rows + i * tile, rows + (i + 1) * tile)
        back = turn_back(dq, cos[t, :], sin[t, :])
        fold(sum_q, back * unit)
        q[rs, qc] = norm_back_heads(back, unit, inverse, query_gain[...]).astype(bf16)

    def piece_keys(h):
        cc = slice(h * hd, (h + 1) * hd)
        for r in range(0, 2 * rows, tile):
            rr = slice(r, r + tile)
            unit, inverse = unit_heads(kraw[rr, cc].astype(f32))
            back = turn_back(dk[rr, :] * scale, cos[rr, :], sin[rr, :])
            fold(sum_k, back * unit)
            k[rr, cc] = norm_back_heads(back, unit, inverse, key_gain[...]).astype(bf16)
            v[rr, cc] = dv[rr, :].astype(bf16)

    at_kv = at_out + n_out
    early_rows = rows // 8

    def handed(n):
        part = pl.ds(n * early_rows, early_rows)
        return pltpu.make_async_remote_copy(
            src_ref=gproj.at[part, :], dst_ref=earlier.at[part, :], send_sem=early_sem.at[0, n], recv_sem=early_sem.at[1, n],
            device_id=(z * 4 + y * 2 + c, 1 - x), device_id_type=MESH)

    def piece_hand(n):
        @pl.when(x == 1)
        def _():
            handed(n).start()

    def piece_queries(j):
        acc[...] += dot_nt(q[:, j * span:(j + 1) * span], weight(at_kv + 2 + j))
        used(at_kv + 2 + j)

    x_in, x_out = mlp, ggate.at[:, pl.ds(0, span)]
    late = []

    def piece_gain():
        loads.wait(late[0])
        sum_one[...] = jnp.zeros_like(sum_one)

        def body(r, n):
            rr = pl.ds(r, n)
            unit, _ = unit_rows(x_in[rr, :].astype(f32))
            fold(sum_one, acc[rr, :] * unit)

        rows_loop(rows, 64, body)

        @pl.when(x == 1)
        def _():
            def more(r, n):
                rr = pl.ds(r, n)
                fold(sum_one, gproj[rr, :].astype(f32) * ain[rr, :].astype(f32) / norm_gain[...])

            rows_loop(rows, 64, more)

        gain_mine[0] = jnp.zeros_like(gain_mine[0])
        gain_mine[0, 0:1, :] = jnp.sum(sum_one[...], axis=0, keepdims=True)
        gain_mine[0, 1:2, :] = jnp.sum(sum_two[...], axis=0, keepdims=True)
        gain_mine[0, 2:3, 0:hd] = jnp.sum(sum_q[...], axis=0, keepdims=True)
        gain_mine[0, 3:4, 0:hd] = jnp.sum(sum_k[...], axis=0, keepdims=True)

    def piece_last():
        @pl.when(x == 0)
        def _():
            for n in range(8):
                handed(n).wait_recv()

            def more(r, n):
                rr = pl.ds(r, n)
                acc[rr, :] += earlier[rr, :].astype(f32)

            rows_loop(rows, 64, more)

        def body(r, n):
            rr = pl.ds(r, n)
            unit, inverse = unit_rows(x_in[rr, :].astype(f32))
            x_out[rr, :] = (mid[rr, :] + norm_back(acc[rr, :], unit, inverse, norm_gain[...])).astype(bf16)

        rows_loop(rows, 64, body)
        loads.start(x_out, gin_o)

    def piece_earlier():
        w_k, w_v = weight(at_kv), weight(at_kv + 1)

        @pl.when(x == 1)
        def _():
            gproj[...] = (dot_nt(k[first, :], w_k) + dot_nt(v[first, :], w_v)).astype(bf16)

    def piece_own():
        acc[...] = dot_nt(k[second, :], wbuf[at_kv % 2]) + dot_nt(v[second, :], wbuf[(at_kv + 1) % 2])
        used(at_kv)
        used(at_kv + 1)
        late.append(loads.start(hid_i, x_in))

    totals = Totals(gain_mine, gain_got, gain_sem, at)
    chain = []
    for j in range(nb):
        chain += [(piece_down, j), (piece_act, j, 0), (piece_act, j, 1)]
    for j in range(nb):
        chain += [(piece_mlp, j, 0), (piece_mlp, j, 1)]
    chain += [(piece_mid, 0), (piece_mid, 1)] + [(piece_attn_grad, j) for j in range(n_out)] + [(piece_ready,)]
    for h in range(kv):
        chain += [(piece_head, h, g, i) for g in range(group) for i in range(2)] + [(piece_keys, h)]
    chain += [(piece_earlier,), (piece_own,)] + [(piece_queries, j) for j in range(n_out)] + [(piece_gain,)]
    chain += [(totals.step, s) for s in range(6)] + [(piece_last,)]
    made, ended = 0, []
    for kind, index, name in order:
        if kind == 0:
            if name == 0:
                if todo[index][0] is not None:
                    todo[index][0](index)
                    if made == 0:
                        head_l = [loads.start(a, b) for a, b in ((q_i, q), (k_i, k), (v_i, v), (qraw_i, qraw), (kraw_i, kraw))]
                        ain_l = loads.start(ain_i, ain)
                        made = 1
                chunks[index].step("go")
            elif name <= 2:
                chunks[index].step(("over_c", "over_x")[name - 1])
            elif name == 8:
                chunks[index].st = bufs[6].at[len(ended) % 2]
                chunks[index].step("finish", ended[-2] if len(ended) > 1 else None)
                ended.append(chunks[index])
            else:
                if name == 3:
                    chunks[index].step("over_y")
                chunks[index].step("over_z", name - 3)
                if name == 6:
                    chunks[index].step("hand")
        elif kind == 1:
            chain[index][0](*chain[index][1:])
            if index == 3 * nb - 1:
                piece_output()
        else:
            piece_hand(index)
    for ch in ended[-2:]:
        ch.o_copy().wait()

    @pl.when(x == 1)
    def _():
        for n in range(8):
            handed(n).wait_send()

    loads.wait_all()
    norm_o[...] = gain_mine[5, 0:1, :]
    mlp_o[...] = gain_mine[5, 1:2, :]
    query_o[...] = gain_mine[5, 2:3, 0:hd]
    key_o[...] = gain_mine[5, 3:4, 0:hd]


def backward(hid, cot, gains, saved, shards):
    rows, width = hid.shape
    full = saved[:7]
    q, k, v, qraw, kraw, ain, attn, lse, mid, mlp, gate, up, hidden, cos, sin, _, bias = saved[7:]
    hd = cos.shape[1]
    shape, vm, dma = jax.ShapeDtypeStruct, pltpu.VMEM, pltpu.SemaphoreType.DMA
    heads, keys, ff = q.shape[1], k.shape[1], gate.shape[1]
    span = keys
    outs = [shape(s.shape, f32) for s in shards] + [
        shape((rows, width), bf16), shape((rows, width), bf16), shape((1, width), f32), shape((1, hd), f32), shape((1, hd), f32), shape((1, width), f32)]
    n = sum(s.shape[0] // 64 * (s.shape[1] // 512) for s in shards)
    return pl.pallas_call(
        functools.partial(backward_kernel, BACKWARD_PLAN),
        out_shape=outs,
        in_specs=[VMEM] * 8 + [HBM] * 21,
        out_specs=[HBM] * 9 + [VMEM] * 4,
        scratch_shapes=[
            vm((rows, ff), bf16), vm((rows, width), bf16), vm((rows, ff), bf16), vm((rows, ff), bf16), vm((rows, width), f32), vm((rows, width), f32),
            vm((rows, width), bf16), vm((heads, rows), bf16), vm((rows, heads), bf16), vm((2 * rows, keys), bf16), vm((2 * rows, keys), bf16),
            vm((rows, heads), bf16), vm((2 * rows, keys), bf16), vm((2 * rows, width), bf16), vm((2 * rows, hd), f32), vm((2 * rows, hd), f32),
            vm((hd, 2 * rows), bf16), vm((2 * rows, rows), f32), vm((2, span, span), bf16), vm((rows, width), bf16),
            vm((8, width), f32), vm((8, width), f32), vm((8, hd), f32), vm((8, hd), f32), vm((6, 8, width), f32), vm((5, 8, width), f32),
            dma((5, 2)), dma((32,)), dma((2,)), dma((2, 8))] + chunk_bufs(64, 512) + chunk_sems(n),
        compiler_params=pltpu.CompilerParams(collective_id=2, has_side_effects=True, vmem_limit_bytes=63 * 2**20),
        name="backward_reduce",
    )(cot, cos, sin, *gains, lse, *full, hid, q, k, v, qraw, kraw, ain, attn, mid, mlp, gate, up, hidden, bias)


def place_kernel(*refs):
    n = (len(refs) - 1) // 3
    first = [pltpu.make_async_copy(refs[i], refs[2 * n + i], refs[-1].at[0, i]) for i in range(n)]
    second = [pltpu.make_async_copy(refs[2 * n + i], refs[n + i], refs[-1].at[1, i]) for i in range(n)]
    for copy in first:
        copy.start()
    for i in range(n):
        first[i].wait()
        second[i].start()
    for copy in second:
        copy.wait()


def placed(arrays):
    n = len(arrays)
    return pl.pallas_call(
        place_kernel,
        out_shape=[jax.ShapeDtypeStruct(a.shape, a.dtype) for a in arrays],
        in_specs=[HBM] * n,
        out_specs=[HBM] * n,
        scratch_shapes=[pltpu.VMEM(a.shape, a.dtype) for a in arrays] + [pltpu.SemaphoreType.DMA((2, n))],
        compiler_params=pltpu.CompilerParams(vmem_limit_bytes=62 * 2**20),
        name="place_results",
    )(*arrays)


def as_sent(shard):

    def short(part):
        return part.astype(jnp.bfloat16) if part.dtype == jnp.float32 else part

    return jax.tree.map(short, shard)


def norm_rows(values, gain_vec):
    inverse = lax.rsqrt(jnp.mean(values * values, axis=-1, keepdims=True) + epsilon)
    normed = values * inverse
    return (normed * gain_vec, normed, inverse)


def norm_back(grad_out, gain_vec, normed, inverse):
    scaled = grad_out * gain_vec
    grad_in = inverse * (scaled - normed * jnp.mean(scaled * normed, axis=-1, keepdims=True))
    return (grad_in, grad_out * normed)


def rope_tables(positions, head_dim):
    frequency = theta_base ** (-jnp.arange(0, head_dim, 2).astype(jnp.float32) / head_dim)
    angles = positions.astype(jnp.float32)[:, None] * frequency[None, :]
    angles = jnp.concatenate([angles, angles], axis=-1)
    return (jnp.cos(angles), jnp.sin(angles))


def rotate(values, cosine, sine_tab):
    half_dim = values.shape[-1] // 2
    turned = jnp.concatenate([-values[..., half_dim:], values[..., :half_dim]], axis=-1)
    return values * cosine[:, None, :] + turned * sine_tab[:, None, :]


def rotate_back(grad_out, cosine, sine_tab):
    half_dim = grad_out.shape[-1] // 2
    weighted = grad_out * sine_tab[:, None, :]
    turned = jnp.concatenate([weighted[..., half_dim:], -weighted[..., :half_dim]], axis=-1)
    return grad_out * cosine[:, None, :] + turned


def back_dot(grad_rows, weight):
    return lax.dot_general(
        grad_rows, weight, (((1,), (1,)), ((), ())), preferred_element_type=jnp.float32
    )


def weight_term(acts_in, grad_out):
    return lax.dot_general(
        acts_in, grad_out, (((0,), (0,)), ((), ())), preferred_element_type=jnp.float32
    )


def per_device(
    hidden_in,
    positions,
    cotangent,
    norm_gain,
    w_query,
    w_key,
    w_value,
    query_gain,
    key_gain,
    w_out,
    mlp_gain,
    w_gate,
    w_up,
    w_down,
):
    seqs_here, block_len, model_width = hidden_in.shape
    head_dim = query_gain.shape[0]
    kv_heads = w_key.shape[1] // head_dim
    q_heads = w_query.shape[1] // head_dim
    groups = q_heads // kv_heads
    ctx_count = lax.axis_size("ctx")
    ctx_rank = lax.axis_index("ctx")
    seq_total = block_len * ctx_count
    row_count = seqs_here * block_len
    scale_val = head_dim ** (-0.5)
    shards = (w_query, w_key, w_value, w_out, w_gate, w_up, w_down)
    full_weights = (
        lax.all_gather(shards[0], "fsdp", axis=0, tiled=True),
        lax.all_gather(shards[1], "fsdp", axis=0, tiled=True),
        lax.all_gather(shards[2], "fsdp", axis=0, tiled=True),
        lax.all_gather(shards[3], "fsdp", axis=0, tiled=True),
        lax.all_gather(shards[4], "fsdp", axis=0, tiled=True),
        lax.all_gather(shards[5], "fsdp", axis=0, tiled=True),
        lax.all_gather(shards[6], "fsdp", axis=0, tiled=True),
    )
    full_query, full_key, full_value, full_out, full_gate, full_up, full_down = full_weights
    residual = hidden_in.astype(jnp.float32).reshape(row_count, model_width)
    scaled_one, normed_one, inverse_one = norm_rows(residual, norm_gain)
    attn_in = scaled_one.astype(jnp.bfloat16)
    query_raw = jnp.dot(attn_in, full_query, preferred_element_type=jnp.float32).reshape(
        row_count, q_heads, head_dim
    )
    key_raw = jnp.dot(attn_in, full_key, preferred_element_type=jnp.float32).reshape(
        row_count, kv_heads, head_dim
    )
    value_bf = jnp.dot(attn_in, full_value, preferred_element_type=jnp.float32).astype(jnp.bfloat16)
    flat_pos = positions.reshape(row_count)
    cosine, sine_tab = rope_tables(flat_pos, head_dim)
    query_scaled, query_normed, query_inverse = norm_rows(query_raw, query_gain)
    query_bf = rotate(query_scaled, cosine, sine_tab).astype(jnp.bfloat16)
    key_scaled, key_normed, key_inverse = norm_rows(key_raw, key_gain)
    key_bf = rotate(key_scaled, cosine, sine_tab).astype(jnp.bfloat16)
    key_flat = key_bf.reshape(seqs_here, block_len, kv_heads * head_dim)
    value_flat = value_bf.reshape(seqs_here, block_len, kv_heads * head_dim)
    keys_all, values_all = (
        lax.all_gather(key_flat, "ctx", axis=1, tiled=True),
        lax.all_gather(value_flat, "ctx", axis=1, tiled=True),
    )
    query_five = query_bf.reshape(seqs_here, block_len, kv_heads, groups, head_dim)
    query_index = ctx_rank * block_len + jnp.arange(block_len, dtype=jnp.int32)
    doc_start = query_index[None, :] - positions

    def block_scores(key_source, block_idx):
        key_block = lax.dynamic_slice_in_dim(key_source, block_idx * block_len, block_len, 1)
        scores = (
            jnp.einsum(
                "sqkgd,spkd->skgqp", query_five, key_block, preferred_element_type=jnp.float32
            )
            * scale_val
        )
        key_index = block_idx * block_len + jnp.arange(block_len, dtype=jnp.int32)
        allowed = (key_index[None, None, :] <= query_index[None, :, None]) & (
            key_index[None, None, :] >= doc_start[:, :, None]
        )
        return (jnp.where(allowed[:, None, None, :, :], scores, -1e30), key_block)

    keys_four = keys_all.reshape(seqs_here, seq_total, kv_heads, head_dim)
    values_four = values_all.reshape(seqs_here, seq_total, kv_heads, head_dim)

    def stats_step(block_idx, carry_stats):
        running_max, running_sum = carry_stats
        scores, key_block = block_scores(keys_four, block_idx)
        new_max = jnp.maximum(running_max, jnp.max(scores, axis=-1))
        running_sum = running_sum * jnp.exp(running_max - new_max) + jnp.sum(
            jnp.exp(scores - new_max[..., None]), axis=-1
        )
        return (new_max, running_sum)

    stat_shape = (seqs_here, kv_heads, groups, block_len)
    row_max, row_sum = lax.fori_loop(
        0,
        ctx_rank + 1,
        stats_step,
        (jnp.full(stat_shape, -1e30, jnp.float32), jnp.zeros(stat_shape, jnp.float32)),
    )

    def output_step(block_idx, accum):
        scores, key_block = block_scores(keys_four, block_idx)
        probs_bf = (jnp.exp(scores - row_max[..., None]) / row_sum[..., None]).astype(jnp.bfloat16)
        value_block = lax.dynamic_slice_in_dim(values_four, block_idx * block_len, block_len, 1)
        return accum + jnp.einsum(
            "skgqp,spkd->sqkgd", probs_bf, value_block, preferred_element_type=jnp.float32
        )

    attn_f32 = lax.fori_loop(
        0,
        ctx_rank + 1,
        output_step,
        jnp.zeros((seqs_here, block_len, kv_heads, groups, head_dim), jnp.float32),
    )
    attn_bf = attn_f32.reshape(row_count, q_heads * head_dim).astype(jnp.bfloat16)
    middle = residual + jnp.dot(attn_bf, full_out, preferred_element_type=jnp.float32)
    scaled_two, normed_two, inverse_two = norm_rows(middle, mlp_gain)
    mlp_in = scaled_two.astype(jnp.bfloat16)
    gate_pre = jnp.dot(mlp_in, full_gate, preferred_element_type=jnp.float32)
    up_pre = jnp.dot(mlp_in, full_up, preferred_element_type=jnp.float32)
    sigmoid_gate = jax.nn.sigmoid(gate_pre)
    silu_gate = gate_pre * sigmoid_gate
    hidden_bf = (silu_gate * up_pre).astype(jnp.bfloat16)
    layer_out = middle + jnp.dot(hidden_bf, full_down, preferred_element_type=jnp.float32)
    output = layer_out.astype(jnp.bfloat16).reshape(seqs_here, block_len, model_width)
    back_weights = full_weights
    keys_back, values_back = (
        lax.all_gather(key_flat, "ctx", axis=1, tiled=True),
        lax.all_gather(value_flat, "ctx", axis=1, tiled=True),
    )
    back_query, back_key, back_value, back_out, back_gate, back_up, back_down = back_weights
    keys_again = keys_back.reshape(seqs_here, seq_total, kv_heads, head_dim)
    values_again = values_back.reshape(seqs_here, seq_total, kv_heads, head_dim)
    grad_rows = cotangent.reshape(row_count, model_width)
    down_grad = back_dot(grad_rows, back_down)
    grad_gate = (
        down_grad * up_pre * sigmoid_gate * (1.0 + gate_pre * (1.0 - sigmoid_gate))
    ).astype(jnp.bfloat16)
    grad_up = (down_grad * silu_gate).astype(jnp.bfloat16)
    grad_mlp_in = back_dot(grad_gate, back_gate) + back_dot(grad_up, back_up)
    grad_norm_two, mlp_gain_terms = norm_back(grad_mlp_in, mlp_gain, normed_two, inverse_two)
    grad_mid = grad_rows.astype(jnp.float32) + grad_norm_two
    grad_proj = grad_mid.astype(jnp.bfloat16)
    grad_attn = back_dot(grad_proj, back_out).astype(jnp.bfloat16)
    grad_five = grad_attn.reshape(seqs_here, block_len, kv_heads, groups, head_dim)
    delta = jnp.einsum("sqkgd,sqkgd->skgq", grad_five.astype(jnp.float32), attn_f32)

    def grad_step(block_idx, carry_grads):
        grad_query, grad_keys, grad_values = carry_grads
        scores, key_block = block_scores(keys_again, block_idx)
        probs = jnp.exp(scores - row_max[..., None]) / row_sum[..., None]
        value_block = lax.dynamic_slice_in_dim(values_again, block_idx * block_len, block_len, 1)
        grad_probs = jnp.einsum(
            "sqkgd,spkd->skgqp", grad_five, value_block, preferred_element_type=jnp.float32
        )
        grad_scores = (probs * (grad_probs - delta[..., None])).astype(jnp.bfloat16)
        grad_query = (
            grad_query
            + jnp.einsum(
                "skgqp,spkd->sqkgd", grad_scores, key_block, preferred_element_type=jnp.float32
            )
            * scale_val
        )
        key_part = (
            jnp.einsum(
                "skgqp,sqkgd->spkd", grad_scores, query_five, preferred_element_type=jnp.float32
            )
            * scale_val
        )
        value_part = jnp.einsum(
            "skgqp,sqkgd->spkd",
            probs.astype(jnp.bfloat16),
            grad_five,
            preferred_element_type=jnp.float32,
        )
        grad_keys = lax.dynamic_update_slice_in_dim(grad_keys, key_part, block_idx * block_len, 1)
        grad_values = lax.dynamic_update_slice_in_dim(
            grad_values, value_part, block_idx * block_len, 1
        )
        return (grad_query, grad_keys, grad_values)

    whole_shape = (seqs_here, seq_total, kv_heads, head_dim)
    grad_query, grad_keys, grad_values = lax.fori_loop(
        0,
        ctx_rank + 1,
        grad_step,
        (
            jnp.zeros((seqs_here, block_len, kv_heads, groups, head_dim), jnp.float32),
            jnp.zeros(whole_shape, jnp.float32),
            jnp.zeros(whole_shape, jnp.float32),
        ),
    )
    key_grad_own, value_grad_own = (
        lax.psum_scatter(
            grad_keys.reshape(seqs_here, seq_total, kv_heads * head_dim).astype(jnp.bfloat16),
            "ctx",
            scatter_dimension=1,
            tiled=True,
        ).astype(jnp.float32),
        lax.psum_scatter(
            grad_values.reshape(seqs_here, seq_total, kv_heads * head_dim).astype(jnp.bfloat16),
            "ctx",
            scatter_dimension=1,
            tiled=True,
        ).astype(jnp.float32),
    )
    key_unrot = rotate_back(key_grad_own.reshape(row_count, kv_heads, head_dim), cosine, sine_tab)
    key_raw_grad, key_gain_terms = norm_back(key_unrot, key_gain, key_normed, key_inverse)
    key_raw_bf = key_raw_grad.reshape(row_count, kv_heads * head_dim).astype(jnp.bfloat16)
    query_unrot = rotate_back(grad_query.reshape(row_count, q_heads, head_dim), cosine, sine_tab)
    query_raw_grad, query_gain_terms = norm_back(
        query_unrot, query_gain, query_normed, query_inverse
    )
    query_raw_bf = query_raw_grad.reshape(row_count, q_heads * head_dim).astype(jnp.bfloat16)
    value_raw_bf = value_grad_own.reshape(row_count, kv_heads * head_dim).astype(jnp.bfloat16)
    grad_attn_in = (
        back_dot(query_raw_bf, back_query)
        + back_dot(key_raw_bf, back_key)
        + back_dot(value_raw_bf, back_value)
    )
    grad_norm_one, norm_gain_terms = norm_back(grad_attn_in, norm_gain, normed_one, inverse_one)
    grad_input = (
        (grad_mid + grad_norm_one).astype(jnp.bfloat16).reshape(seqs_here, block_len, model_width)
    )
    gain_one, gain_query, gain_key, gain_two = lax.psum(
        (
            jnp.sum(norm_gain_terms, axis=0),
            jnp.sum(query_gain_terms, axis=(0, 1)),
            jnp.sum(key_gain_terms, axis=(0, 1)),
            jnp.sum(mlp_gain_terms, axis=0),
        ),
        ("fsdp", "ctx"),
    )
    weight_pairs = (
        (attn_in, query_raw_bf),
        (attn_in, key_raw_bf),
        (attn_in, value_raw_bf),
        (attn_bf, grad_proj),
        (mlp_in, grad_gate),
        (mlp_in, grad_up),
        (hidden_bf, grad_rows),
    )
    pieces = tuple(
        (
            lax.psum_scatter(
                weight_term(acts_in, grad_out).astype(jnp.bfloat16),
                "fsdp",
                scatter_dimension=0,
                tiled=True,
            ).astype(jnp.float32)
            for acts_in, grad_out in weight_pairs
        )
    )
    weight_grads = jax.tree.map(
        lambda part: part.astype(jnp.float32), lax.psum(as_sent(pieces), "ctx")
    )
    grad_wq, grad_wk, grad_wv, grad_wo, grad_wg, grad_wu, grad_wd = weight_grads
    return (
        output,
        grad_input,
        gain_one,
        grad_wq,
        grad_wk,
        grad_wv,
        gain_query,
        gain_key,
        grad_wo,
        gain_two,
        grad_wg,
        grad_wu,
        grad_wd,
    )


def grid_device(hidden_in, positions, cotangent, norm_gain, w_query, w_key, w_value, query_gain, key_gain, w_out, mlp_gain, w_gate, w_up, w_down):
    rows, width = hidden_in.shape[1:]
    head_dim = query_gain.shape[0]
    hid, cot = hidden_in.reshape(rows, width), cotangent.reshape(rows, width)
    half = theta_base ** (-np.arange(0, head_dim, 2) / head_dim)
    freq = jnp.asarray(np.concatenate([half, half])[None], jnp.float32)
    gains = [g[None, :] for g in (norm_gain, query_gain, key_gain, mlp_gain)]
    shards = (w_query, w_key, w_value, w_out, w_gate, w_up, w_down)
    saved = forward(hid, positions, freq, gains, shards)
    done = placed(backward(hid, cot, gains, saved, shards))
    gq, gk, gv, go, gg, gu, gd, out, grad_in, norm, query, key, mlp = done
    return (out[None], grad_in[None], norm[0], gq, gk, gv, query[0], key[0], go, mlp[0], gg, gu, gd)


def is_grid(mesh):
    if dict(mesh.shape) != {"fsdp": 16, "ctx": 2}:
        return False
    for f in range(16):
        for x in range(2):
            device = mesh.devices[f, x]
            if tuple(device.coords) != (x, (f // 2) % 2, f // 4) or device.core_on_chip != f % 2:
                return False
    return True


def solution(mesh):
    in_specs = (
        P("fsdp", "ctx", None),
        P("fsdp", "ctx"),
        P("fsdp", "ctx", None),
        P(),
        P("fsdp", None),
        P("fsdp", None),
        P("fsdp", None),
        P(),
        P(),
        P("fsdp", None),
        P(),
        P("fsdp", None),
        P("fsdp", None),
        P("fsdp", None),
    )
    out_specs = (
        P("fsdp", "ctx", None),
        P("fsdp", "ctx", None),
        P(),
        P("fsdp", None),
        P("fsdp", None),
        P("fsdp", None),
        P(),
        P(),
        P("fsdp", None),
        P(),
        P("fsdp", None),
        P("fsdp", None),
        P("fsdp", None),
    )
    return jax.shard_map(
        grid_device if is_grid(mesh) else per_device, mesh=mesh, in_specs=in_specs, out_specs=out_specs, check_vma=False
    )
```

```python
import functools

import jax
import jax.numpy as jnp
import numpy as np
from jax import lax
from jax.experimental import pallas as pl
from jax.experimental.pallas import tpu as pltpu
from jax.sharding import PartitionSpec as P

MESH = pl.DeviceIdType.MESH

epsilon = 1e-06
theta_base = 1000000.0
log2e = 1.4426950408889634
bf16, f32 = jnp.bfloat16, jnp.float32
HBM = pl.BlockSpec(memory_space=pl.ANY)
VMEM = pl.BlockSpec(memory_space=pltpu.VMEM)

FORWARD_PLAN = (
    ((1, 16, 4, 5), (1, 8, 2, 3), (1, 8, 3, 3), (1, 8, 3, 3), (1, 24, 6, 8), (1, 24, 9, 8), (0, 12, 4, 3)),
    (0, 1, 4, 8, 11, 13, 18),
    (0, 2, 4, 6, 5, 7, 9, 9, 11, 11, 11, 11, 11),
    (1, 3, 0, 7, 2, 0, 0, 2, 4, 3, 0, 2, 2, 0, 1, 0, 1, 4, 0, 0, 4, 10, 1, 1, 0, 1, 0, 0, 2, 2, 28, 46, 18, 19, 23, 19),
    1,
    4,
)

BACKWARD_PLAN = (
    ((1, 1), (1, 1), (1, 1), (1, 1), (1, 1), (1, 1), (1, 1), (1, 1), (1, 1), (1, 1), (1, 1), (1, 1), (1, 1), (1, 1), (1, 1), (1, 1), (1, 1), (1, 1), (1, 1), (1, 1), (1, 1), (1, 1), (1, 1), (1, 1), (1, 1), (1, 1), (0, 0), (0, 0), (0, 0), (0, 0)),
    (
        (0, 0, 0), (1, 0, 0), (1, 1, 0), (0, 0, 1), (0, 1, 0), (1, 2, 0), (1, 3, 0), (0, 1, 1), (1, 4, 0), (0, 0, 2),
        (0, 2, 0), (0, 3, 0), (0, 1, 2), (0, 2, 1), (1, 5, 0), (0, 3, 1), (0, 0, 3), (0, 4, 0), (1, 6, 0), (0, 2, 2),
        (1, 7, 0), (0, 4, 1), (0, 5, 0), (0, 1, 3), (1, 8, 0), (0, 0, 4), (0, 6, 0), (1, 9, 0), (0, 3, 2), (0, 5, 1),
        (0, 7, 0), (1, 10, 0), (0, 6, 1), (0, 2, 3), (0, 4, 2), (0, 0, 5), (0, 1, 4), (1, 11, 0), (0, 8, 0), (0, 7, 1),
        (0, 9, 0), (0, 3, 3), (0, 5, 2), (0, 0, 6), (0, 1, 5), (1, 12, 0), (1, 13, 0), (0, 1, 6), (0, 3, 4), (1, 14, 0),
        (0, 2, 4), (0, 6, 2), (0, 4, 3), (0, 3, 5), (0, 0, 8), (0, 8, 1), (0, 10, 0), (0, 7, 2), (1, 15, 0), (0, 5, 3),
        (1, 16, 0), (0, 3, 6), (0, 10, 1), (0, 4, 4), (0, 2, 5), (1, 17, 0), (0, 5, 4), (1, 18, 0), (0, 4, 5), (0, 1, 8),
        (0, 3, 8), (1, 19, 0), (0, 9, 1), (0, 6, 3), (0, 11, 0), (0, 12, 0), (0, 6, 4), (0, 5, 5), (0, 8, 2), (0, 2, 6),
        (0, 7, 3), (1, 20, 0), (0, 4, 6), (0, 11, 1), (0, 2, 8), (0, 13, 0), (0, 7, 4), (0, 9, 2), (1, 21, 0), (0, 6, 5),
        (1, 22, 0), (0, 10, 2), (0, 5, 6), (0, 4, 8), (0, 12, 1), (0, 8, 3), (1, 23, 0), (0, 14, 0), (0, 7, 5), (0, 11, 2),
        (1, 24, 0), (0, 5, 8), (0, 13, 1), (1, 25, 0), (0, 9, 3), (0, 6, 6), (0, 15, 0), (1, 26, 0), (0, 12, 2), (0, 8, 4),
        (1, 27, 0), (0, 14, 1), (1, 28, 0), (1, 29, 0), (0, 9, 4), (0, 7, 6), (0, 13, 2), (0, 10, 3), (1, 30, 0), (0, 8, 5),
        (1, 31, 0), (0, 10, 4), (0, 6, 8), (0, 16, 0), (0, 11, 3), (1, 32, 0), (0, 15, 1), (1, 33, 0), (0, 9, 5), (0, 11, 4),
        (0, 17, 0), (0, 14, 2), (0, 10, 5), (1, 34, 0), (0, 8, 6), (0, 12, 3), (1, 35, 0), (0, 16, 1), (1, 36, 0), (1, 37, 0),
        (0, 12, 4), (0, 17, 1), (0, 8, 8), (0, 7, 8), (0, 18, 0), (0, 11, 5), (0, 15, 2), (0, 13, 3), (0, 10, 6), (1, 38, 0),
        (0, 12, 5), (0, 9, 6), (1, 39, 0), (1, 40, 0), (0, 14, 3), (0, 13, 4), (0, 18, 1), (1, 41, 0), (0, 17, 2), (1, 42, 0),
        (0, 19, 0), (1, 43, 0), (0, 16, 2), (0, 14, 4), (1, 44, 0), (0, 10, 8), (0, 15, 3), (0, 11, 6), (0, 13, 5), (0, 9, 8),
        (0, 20, 0), (0, 19, 1), (1, 45, 0), (0, 18, 2), (0, 14, 5), (0, 21, 0), (0, 17, 3), (0, 12, 6), (1, 46, 0), (0, 17, 4),
        (0, 15, 4), (0, 20, 1), (1, 47, 0), (1, 48, 0), (1, 49, 0), (0, 13, 6), (0, 16, 3), (1, 50, 0), (0, 19, 2), (1, 51, 0),
        (0, 16, 4), (0, 21, 1), (0, 15, 5), (1, 52, 0), (0, 12, 8), (0, 11, 8), (0, 22, 0), (0, 20, 2), (0, 17, 5), (1, 53, 0),
        (0, 14, 6), (0, 13, 8), (0, 23, 0), (1, 54, 0), (0, 19, 3), (0, 16, 5), (0, 22, 1), (1, 55, 0), (0, 18, 3), (0, 14, 8),
        (0, 21, 2), (0, 24, 0), (0, 15, 6), (1, 56, 0), (0, 20, 3), (0, 23, 1), (1, 57, 0), (0, 22, 2), (0, 18, 4), (1, 58, 0),
        (0, 24, 1), (1, 59, 0), (0, 20, 4), (0, 16, 6), (0, 17, 6), (1, 60, 0), (0, 21, 3), (0, 23, 2), (0, 18, 5), (0, 19, 4),
        (0, 15, 8), (0, 25, 0), (1, 61, 0), (0, 22, 3), (0, 21, 4), (0, 24, 2), (0, 16, 8), (0, 26, 0), (0, 18, 6), (0, 22, 4),
        (0, 17, 8), (0, 25, 1), (0, 23, 3), (0, 20, 5), (2, 0, 0), (0, 27, 0), (2, 1, 0), (0, 26, 1), (0, 18, 8), (0, 25, 2),
        (0, 19, 5), (0, 23, 4), (0, 23, 5), (0, 22, 5), (2, 2, 0), (0, 27, 1), (0, 21, 5), (1, 62, 0), (0, 20, 6), (0, 26, 3),
        (0, 19, 6), (2, 3, 0), (0, 28, 0), (0, 26, 4), (1, 63, 0), (0, 28, 1), (0, 25, 3), (0, 19, 8), (1, 64, 0), (0, 21, 6),
        (0, 25, 4), (2, 4, 0), (0, 29, 0), (0, 22, 6), (1, 65, 0), (0, 27, 3), (0, 26, 5), (1, 66, 0), (0, 24, 3), (0, 29, 1),
        (2, 5, 0), (0, 24, 4), (2, 6, 0), (0, 27, 4), (0, 20, 8), (0, 25, 5), (0, 26, 6), (0, 21, 8), (0, 23, 6), (0, 24, 5),
        (0, 28, 3), (0, 22, 8), (0, 28, 4), (0, 29, 3), (0, 25, 6), (0, 24, 6), (0, 27, 5), (2, 7, 0), (1, 67, 0), (0, 29, 4),
        (1, 68, 0), (0, 29, 5), (0, 23, 8), (0, 28, 5), (0, 24, 8), (0, 27, 6), (0, 26, 8), (1, 69, 0), (0, 29, 6), (0, 28, 6),
        (1, 71, 0), (0, 29, 8), (0, 25, 8), (1, 70, 0), (0, 27, 8), (0, 28, 8),
    ),
)


def place():
    f = lax.axis_index("fsdp")
    return f // 4, (f // 2) % 2, f % 2, lax.axis_index("ctx")


def enter(z, y, c, x, ends=False):
    bar = pltpu.get_barrier_semaphore()

    def hail(z2, y2, c2, x2):
        pl.semaphore_signal(bar, inc=1, device_id=(z2 * 4 + y2 * 2 + c2, x2), device_id_type=MESH)

    hail(z, y, c, 1 - x)
    hail(z, 1 - y, c, x)
    hail(z, y, 1 - c, x)

    @pl.when(z > 0)
    def _():
        hail(z - 1, y, c, x)

    @pl.when(z < 3)
    def _():
        hail(z + 1, y, c, x)

    if ends:
        @pl.when(z % 3 == 0)
        def _():
            hail(3 - z, y, c, x)

    pl.semaphore_wait(bar, 5 if ends else 4 + (z * (3 - z)) // 2)


class Gather:
    def __init__(self, index, own, full, sems, at, cut):
        self.g, self.own, self.full = index, own, full
        self.zr, self.yr, self.xr, self.cr, self.zs, self.ys, self.xs, self.cs, self.ls = sems
        self.z, self.y, self.c, self.x = at
        self.rows, self.cols = own.shape
        self.dim, units, ones, twos = cut
        step = own.shape[self.dim] // units
        low, middle, high = (0, ones * step), (ones * step, (units - twos - ones) * step), ((units - twos) * step, twos * step)
        self.plans = ((0, low[1] + middle[1]), low, high), ((low[1], middle[1] + high[1]), high, low)
        self.all = None

    def step(self, name, *args):
        for x in (0, 1):
            @pl.when(self.x == x)
            def _():
                self.ywin, self.xwin, self.xgot = self.plans[x]
                getattr(self, name)(*args)

    def window(self, ref, row, win):
        if win is None:
            return ref.at[pl.ds(row, self.rows), :]
        if self.dim == 0:
            return ref.at[pl.ds(row + win[0], win[1]), :]
        return ref.at[pl.ds(row, self.rows), pl.ds(*win)]

    def part(self, z2, y2, c2, win):
        f2 = z2 * 4 + y2 * 2 + c2
        return self.window(self.full, pl.multiple_of(f2 * self.rows, 16), win)

    def mine(self):
        return self.window(self.own, 0, self.ywin)

    def send(self, src, dst, ssem, rsem, to):
        z2, y2, c2, x2 = to
        return pltpu.make_async_remote_copy(
            src_ref=src, dst_ref=dst, send_sem=ssem, recv_sem=rsem,
            device_id=(z2 * 4 + y2 * 2 + c2, x2), device_id_type=MESH)

    def z_copy(self, zs, up, first):
        dst = self.part(zs, self.y, self.c, self.ywin)
        src = self.mine() if first else dst
        z2 = self.z + 1 if up else self.z - 1
        return self.send(src, dst, self.zs.at[self.g, zs, 1 if up else 0], self.zr.at[self.g, zs], (z2, self.y, self.c, self.x))

    def y_copy(self, zs, first):
        dst = self.part(zs, self.y, self.c, self.ywin)
        src = self.mine() if first else dst
        return self.send(src, dst, self.ys.at[self.g, zs], self.yr.at[self.g, zs], (self.z, 1 - self.y, self.c, self.x))

    def x_copy(self, zs, y2):
        dst = self.part(zs, y2, self.c, self.xwin)
        s = zs * 2 + y2
        return self.send(dst, dst, self.xs.at[self.g, s], self.xr.at[self.g, s], (self.z, self.y, self.c, 1 - self.x))

    def c_copy(self, zs, y2, win, piece, first=False):
        dst = self.part(zs, y2, self.c, win)
        src = self.own if first else dst
        s = (zs * 2 + y2) * 2 + piece
        return self.send(src, dst, self.cs.at[self.g, s], self.cr.at[self.g, s], (self.z, self.y, 1 - self.c, self.x))

    def await_(self, dst, sem):
        pltpu.make_async_copy(dst, dst, sem).wait()

    def local(self):
        return pltpu.make_async_copy(self.own, self.part(self.z, self.y, self.c, self.all), self.ls.at[self.g])

    def begin(self):
        z = self.z

        @pl.when(z < 3)
        def _():
            self.z_copy(z, True, True).start()

        @pl.when(z > 0)
        def _():
            self.z_copy(z, False, True).start()

        self.y_copy(z, True).start()
        self.c_copy(z, self.y, self.all, 0, True).start()
        self.local().start()

    def spread(self, zs, up):
        self.await_(self.part(zs, self.y, self.c, self.ywin), self.zr.at[self.g, zs])

        @pl.when(self.z < 3 if up else self.z > 0)
        def _():
            self.z_copy(zs, up, False).start()

        self.y_copy(zs, False).start()
        self.x_copy(zs, self.y).start()
        self.c_copy(zs, self.y, self.ywin, 0).start()

    def along_z(self, k):
        @pl.when(self.z >= k)
        def _():
            self.spread(self.z - k, True)

        @pl.when(self.z + k <= 3)
        def _():
            self.spread(self.z + k, False)

    def over_y(self, zs):
        self.await_(self.part(zs, 1 - self.y, self.c, self.ywin), self.yr.at[self.g, zs])
        self.x_copy(zs, 1 - self.y).start()
        self.c_copy(zs, 1 - self.y, self.ywin, 0).start()

    def along_y(self, k):
        if k == 0:
            self.over_y(self.z)
            return

        @pl.when(self.z >= k)
        def _():
            self.over_y(self.z - k)

        @pl.when(self.z + k <= 3)
        def _():
            self.over_y(self.z + k)

    def over_x(self, zs, y2):
        self.await_(self.part(zs, y2, self.c, self.xgot), self.xr.at[self.g, zs * 2 + y2])
        self.c_copy(zs, y2, self.xgot, 1).start()

    def along_x(self, k):
        if k == 0:
            self.over_x(self.z, 1 - self.y)
            return

        for y2 in (self.y, 1 - self.y):
            @pl.when(self.z >= k)
            def _():
                self.over_x(self.z - k, y2)

            @pl.when(self.z + k <= 3)
            def _():
                self.over_x(self.z + k, y2)

    def finish(self):
        z, y = self.z, self.y
        self.local().wait()
        c = 1 - self.c
        self.await_(self.part(z, y, c, self.all), self.cr.at[self.g, (z * 2 + y) * 2])
        for k in range(0, 4):
            for y2 in ((y, 1 - y) if k else (1 - y,)):
                for zs, ok in ((z - k, z >= k), (z + k, z + k <= 3))[: 2 if k else 1]:
                    @pl.when(ok)
                    def _():
                        s = (zs * 2 + y2) * 2
                        self.await_(self.part(zs, y2, c, self.ywin), self.cr.at[self.g, s])
                        self.await_(self.part(zs, y2, c, self.xgot), self.cr.at[self.g, s + 1])

    def drain(self):
        z, y = self.z, self.y

        @pl.when(z < 3)
        def _():
            self.z_copy(z, True, True).wait_send()

        @pl.when(z > 0)
        def _():
            self.z_copy(z, False, True).wait_send()

        self.y_copy(z, True).wait_send()
        self.c_copy(z, y, self.all, 0, True).wait_send()
        self.x_copy(z, 1 - y).wait_send()
        self.c_copy(z, 1 - y, self.ywin, 0).wait_send()
        self.c_copy(z, 1 - y, self.xgot, 1).wait_send()
        for k in range(1, 4):
            for zs, ok, more, up in ((z - k, z >= k, z < 3, True), (z + k, z + k <= 3, z > 0, False)):
                @pl.when(ok)
                def _():
                    @pl.when(more)
                    def _():
                        self.z_copy(zs, up, False).wait_send()

                    self.y_copy(zs, False).wait_send()
                    for y2 in (y, 1 - y):
                        self.x_copy(zs, y2).wait_send()
                        self.c_copy(zs, y2, self.ywin, 0).wait_send()
                        self.c_copy(zs, y2, self.xgot, 1).wait_send()


def gather_sems(n):
    return [pltpu.SemaphoreType.DMA(s) for s in ((n, 4), (n, 4), (n, 8), (n, 16), (n, 4, 2), (n, 4), (n, 8), (n, 16), (n,))]


def dot_nn(a, b):
    return lax.dot_general(a, b, (((1,), (0,)), ((), ())), preferred_element_type=f32)


def dot_nt(a, b):
    return lax.dot_general(a, b, (((1,), (1,)), ((), ())), preferred_element_type=f32)


def dot_tn(a, b):
    return lax.dot_general(a, b, (((0,), (0,)), ((), ())), preferred_element_type=f32)


def rows_loop(count, step, body):
    @pl.loop(0, count // step)
    def _(i):
        body(pl.multiple_of(i * step, step), step)


class Writes:
    def __init__(self, sem):
        self.sem, self.all, self.open = sem, [], set()

    def start(self, src, dst):
        copy = pltpu.make_async_copy(src, dst, self.sem.at[len(self.all)])
        copy.start()
        self.open.add(len(self.all))
        self.all.append(copy)
        return len(self.all) - 1

    def wait(self, i):
        if i in self.open:
            self.all[i].wait()
            self.open.remove(i)

    def wait_all(self):
        for i in sorted(self.open):
            self.wait(i)


def unit_heads(values):
    size = values.shape[-1]
    mean = dot_nn((values * values).astype(bf16), jnp.full((size, size), 1.0 / size, bf16))
    inverse = lax.rsqrt(mean + epsilon)
    return values * inverse, inverse


def unit_rows(values):
    inverse = lax.rsqrt(jnp.mean(values * values, axis=-1, keepdims=True) + epsilon)
    return values * inverse, inverse


def turn(u, cos, sin):
    return u * cos + pltpu.roll(u, u.shape[-1] // 2, 1) * sin


def turn_back(u, cos, sin):
    return u * cos - pltpu.roll(u, u.shape[-1] // 2, 1) * sin


def mask_bias(bias, start_ref, rows):
    block = 128

    @pl.loop(0, bias.shape[0] // block)
    def _(i):
        rr = pl.ds(pl.multiple_of(i * block, block), block)
        key = lax.broadcasted_iota(jnp.int32, (block, rows), 0) + i * block
        query = lax.broadcasted_iota(jnp.int32, (block, rows), 1) + rows
        ok = (key >= start_ref[...]) & (key <= query)
        bias[rr, :] = jnp.where(ok, 0.0, -1e30)


class Schedule:
    def __init__(self, gathers, starts, after):
        steps = [("begin",)] + [("along_z", k) for k in (1, 2, 3)] + [("along_y", k) for k in range(4)] + [("along_x", k) for k in range(4)] + [("finish",)]
        slots = {}
        for i, g in reversed(list(enumerate(gathers))):
            for j, s in zip(after, steps):
                slots.setdefault(starts[i] + j, []).append((i, g, s))
        self.steps = [step for t in sorted(slots) for step in slots[t]]

    def run(self, count):
        for i, g, s in self.steps[:count]:
            g.step(*s)
        self.steps = self.steps[count:]

    def until(self, weight):
        ends = [n for n, (i, g, s) in enumerate(self.steps) if i == weight and s[0] == "finish"]
        if ends:
            self.run(ends[0] + 1)


def forward_kernel(plan, hid, pos, freq, norm_gain, query_gain, key_gain, mlp_gain, *refs):
    owns, refs = refs[:7], refs[7:]
    outs, refs = refs[:7], refs[7:]
    (q_o, k_o, v_o, qraw_o, kraw_o, ain_o, attn_o, lse_o, mid_o, mlp_o, gate_o, up_o, hidden_o, cos_o, sin_o, start, bias_o), refs = refs[:17], refs[17:]
    fulls, refs = refs[:6] + (outs[6],), refs[6:]
    (ain, q, k, vt, attn, bias, tmp, mid, stage, cos, sin, pre, ain_sem, out_sem), sems = refs[:14], refs[14:]
    w_q, w_k, w_v, w_o, w_g, w_u = fulls[:6]
    cuts, starts, after, runs, early, _ = plan
    runs = list(runs)
    at = place()
    z, y, c, x = at
    rows, width = hid.shape
    hd = freq.shape[1]
    kv = w_k.shape[1] // hd
    qh = w_q.shape[1] // hd
    group = qh // kv
    span = tmp.shape[1]
    first, second = pl.ds(0, rows), pl.ds(rows, rows)
    enter(*at)
    gs = [Gather(i, owns[i], fulls[i], sems, at, cuts[i]) for i in range(7)]
    sched = Schedule(gs, starts, after)
    writes = Writes(out_sem)
    sched.run(1)

    def norm_one(r, n):
        unit, _ = unit_rows(hid[pl.ds(r, n), :].astype(f32))
        ain[pl.ds(pl.multiple_of(r + rows, n), n), :] = (unit * norm_gain[...]).astype(bf16)

    rows_loop(rows, 64, norm_one)
    count = ain_sem.shape[1]
    size = rows // count

    def handed(n):
        return pltpu.make_async_remote_copy(
            src_ref=ain.at[pl.ds(rows + n * size, size), :], dst_ref=ain.at[pl.ds(n * size, size), :],
            send_sem=ain_sem.at[0, n], recv_sem=ain_sem.at[1, n],
            device_id=(z * 4 + y * 2 + c, 1 - x), device_id_type=MESH)

    left = list(range(count))

    def hand():
        if left:
            n = left.pop(0)

            @pl.when(x == 0)
            def _():
                handed(n).start()

    def pump():
        sched.run(runs.pop(0))
        hand()

    hand()

    @pl.when(x == 0)
    def _():
        ain[first, :] = jnp.zeros((rows, width), bf16)

    index = lax.broadcasted_iota(jnp.int32, (1, rows), 1)
    head = jnp.sum(jnp.where(index == 0, pos[...], 0), axis=1, keepdims=True)
    own_start = index + rows - pos[...]
    start[...] = jnp.where(x == 0, jnp.maximum(own_start, rows), own_start)
    sign = jnp.where(lax.broadcasted_iota(jnp.int32, (rows, hd), 1) < hd // 2, -1.0, 1.0)
    for rr, row in ((second, pos[...]), (first, index - rows + head)):
        angle = jnp.broadcast_to(row.astype(f32), (hd, rows)).T * freq[...]
        cos[rr, :] = jnp.cos(angle)
        sin[rr, :] = jnp.sin(angle) * sign
    writes.start(cos, cos_o)
    writes.start(sin, sin_o)
    mask_bias(bias, start, rows)
    writes.start(bias, bias_o)
    for _ in range(early):
        sched.run(2)
        hand()
    sched.until(0)

    def heads(lhs, weight, base, count, gain, into, col):
        for r in range(0, count, rows):
            tmp[r:r + rows, :] = dot_nn(lhs[pl.ds(r, rows), :], weight)
            pump()
        for part in range(0, span // hd, 4):
            @pl.loop(part, part + 4)
            def _(h):
                cc = pl.ds(pl.multiple_of(h * hd, hd), hd)
                to = pl.ds(pl.multiple_of(col + h * hd, hd), hd)
                for r in range(0, count, 256):
                    raw = tmp[r:r + 256, cc]
                    stage[r:r + 256, cc] = raw.astype(bf16)
                    unit, _ = unit_heads(raw)
                    t = slice(base + r, base + r + 256)
                    into[r:r + 256, to] = turn(unit * gain[...], cos[t, :], sin[t, :]).astype(bf16)

            pump()

    last = None
    for b in range(w_q.shape[1] // span):
        if last is not None:
            writes.wait(last)
        heads(ain.at[second, :], w_q[:, b * span:(b + 1) * span], rows, rows, query_gain, q, b * span)
        last = writes.start(stage.at[first, :], qraw_o.at[:, pl.ds(b * span, span)])
    while left:
        hand()
    sched.until(1)

    @pl.when(x == 1)
    def _():
        for n in range(count):
            handed(n).wait_recv()

    writes.wait(last)
    heads(ain, w_k[...], 0, 2 * rows, key_gain, k, 0)
    last = writes.start(stage, kraw_o)
    writes.start(ain, ain_o)
    writes.start(q, q_o)
    writes.start(k, k_o)
    sched.until(2)
    for r in (first, second):
        tmp[r, :] = dot_nn(ain[r, :], w_v[...])
        pump()
    writes.wait(last)
    stage[...] = tmp[...].astype(bf16)
    last = writes.start(stage, v_o)

    @pl.loop(0, kv)
    def _(h):
        cc = pl.ds(pl.multiple_of(h * hd, hd), hd)
        vt[cc, :] = tmp[:, cc].astype(bf16).T

    pump()

    c2 = hd ** (-0.5) * log2e
    for part in range(kv):
        @pl.loop(part, part + 1)
        def _(h):
            cc = pl.ds(pl.multiple_of(h * hd, hd), hd)
            for g in range(group):
                n = h * group + g
                qc = pl.ds(pl.multiple_of(n * hd, hd), hd)
                p = jnp.exp2(dot_nt(k[:, cc], q[:, qc]) * c2 + bias[...])
                total = jnp.sum(p, axis=0, keepdims=True)
                o = dot_nn(vt[cc, :], p.astype(bf16))
                attn[qc, :] = (o * (1.0 / total)).astype(bf16)
                lse_o[pl.ds(n, 1), :] = jnp.log2(total)

        pump()
    writes.start(attn, attn_o)
    sched.until(3)
    for i in range(3):
        gs[i].step("drain")
    leaving = [writes.start(fulls[i], outs[i]) for i in range(3)]
    writes.start(w_o, outs[3])
    mid[...] = hid[...].astype(f32) + dot_tn(attn[...], w_o[...])
    pump()

    for n in leaving:
        writes.wait(n)
    writes.wait(last)
    blocks = w_g.shape[1] // span
    hidden = [w_q.at[first, pl.ds(0, span)], w_q.at[second, pl.ds(0, span)], w_q.at[first, pl.ds(span, span)]]
    mlp_in = w_q.at[second, pl.ds(span, span)]
    gates = [w_k.at[first, :], w_v.at[first, :], stage.at[first, :]]
    ups = [w_k.at[second, :], w_v.at[second, :], stage.at[second, :]]

    def norm_two(r, n):
        unit, _ = unit_rows(mid[pl.ds(r, n), :])
        mlp_in[pl.ds(r, n), :] = (unit * mlp_gain[...]).astype(bf16)

    rows_loop(rows, 64, norm_two)
    writes.start(mid, mid_o)
    writes.start(mlp_in, mlp_o)
    sched.until(4)
    for j in range(blocks):
        cols = pl.ds(j * span, span)
        pre[:, cols] = dot_nn(mlp_in[...], w_g[:, cols])
        pump()
    writes.start(w_g, outs[4])
    sched.until(5)
    writes.start(w_u, outs[5])
    for j in range(blocks):
        cols = pl.ds(j * span, span)
        tmp[first, :] = dot_nn(mlp_in[...], w_u[:, cols])
        pump()

        def act(r, n):
            rr = pl.ds(r, n)
            gate, up = pre[rr, cols], tmp[rr, :]
            sig = jax.nn.sigmoid(gate)
            silu = gate * sig
            hidden[j][rr, :] = (silu * up).astype(bf16)
            gates[j][rr, :] = (up * (sig + silu * (1.0 - sig))).astype(bf16)
            ups[j][rr, :] = silu.astype(bf16)

        rows_loop(rows, 64, act)
        writes.start(gates[j], gate_o.at[:, cols])
        writes.start(ups[j], up_o.at[:, cols])
        writes.start(hidden[j], hidden_o.at[:, cols])
        pump()
    sched.until(6)
    sched.run(len(sched.steps))
    for g in gs[3:]:
        g.step("drain")

    @pl.when(x == 0)
    def _():
        for n in range(count):
            handed(n).wait_send()

    writes.wait_all()


def forward(hid, pos, freq, gains, shards):
    rows, width = hid.shape
    hd = freq.shape[1]
    fulls = [(s.shape[0] * 16, s.shape[1]) for s in shards]
    heads, keys, ff = shards[0].shape[1], shards[1].shape[1], shards[4].shape[1]
    shape = jax.ShapeDtypeStruct
    vm = pltpu.VMEM
    outs = [shape(s, bf16) for s in fulls] + [
        shape((rows, heads), bf16), shape((2 * rows, keys), bf16), shape((2 * rows, keys), bf16),
        shape((rows, heads), bf16), shape((2 * rows, keys), bf16), shape((2 * rows, width), bf16), shape((heads, rows), bf16),
        shape((heads // hd, rows), f32), shape((rows, width), f32), shape((rows, width), bf16),
        shape((rows, ff), bf16), shape((rows, ff), bf16), shape((rows, ff), bf16),
        shape((2 * rows, hd), f32), shape((2 * rows, hd), f32), shape((1, rows), jnp.int32), shape((2 * rows, rows), f32)]
    specs = [HBM] * 7 + [VMEM if i in (7, 15) else HBM for i in range(17)]
    return pl.pallas_call(
        functools.partial(forward_kernel, FORWARD_PLAN),
        out_shape=outs,
        in_specs=[VMEM] * 7 + [HBM] * 7,
        out_specs=specs,
        scratch_shapes=[vm(s, bf16) for s in fulls[:6]] + [
            vm((2 * rows, width), bf16), vm((rows, heads), bf16), vm((2 * rows, keys), bf16), vm((keys, 2 * rows), bf16),
            vm((heads, rows), bf16), vm((2 * rows, rows), f32), vm((2 * rows, keys), f32), vm((rows, width), f32),
            vm((2 * rows, keys), bf16), vm((2 * rows, hd), f32), vm((2 * rows, hd), f32), vm((rows, ff), f32), pltpu.SemaphoreType.DMA((2, FORWARD_PLAN[5])), pltpu.SemaphoreType.DMA((32,))] + gather_sems(7),
        compiler_params=pltpu.CompilerParams(collective_id=1, has_side_effects=True, vmem_limit_bytes=62 * 2**20),
        name="forward_gather",
    )(hid, pos, freq, *gains, *shards)


class Chunk:
    def __init__(self, index, bufs, sems, at, out, ones, twos):
        self.i, self.out, self.ones, self.twos = index, out, ones, twos
        ring = [index % b.shape[0] for b in bufs]
        self.g, self.cb, self.xb, self.yb, self.zb, self.fb, self.st = [b.at[r] for b, r in zip(bufs, ring)]
        self.sc, self.sx, self.sy, self.zs, self.zr, self.sf, self.so = [s.at[index] for s in sems]
        self.z, self.y, self.c, self.x = at
        self.unit = self.g.shape[3] // 4

    def step(self, name, *args):
        u = self.unit
        if self.ones == self.twos and name != "finish":
            t = self.ones
            self.first = self.x * t
            self.keep, self.send_x, self.got_x, self.theirs = 4 - t, t, t, 4 - t
            self.ywin = pl.ds(pl.multiple_of(self.first * u, 16), self.keep * u)
            self.xsend = pl.ds(pl.multiple_of((1 - self.x) * (4 - t) * u, 16), t * u)
            self.xgot = pl.ds(pl.multiple_of(self.x * (4 - t) * u, 16), t * u)
            getattr(self, name)(*args)
            return
        for x in (0, 1):
            @pl.when(self.x == x)
            def _():
                spans = ((0, 4 - self.twos), (self.ones, 4))
                lows, highs = (0, self.ones), (4 - self.twos, 4)
                self.span, self.other = spans[x], spans[1 - x]
                self.keep, self.theirs = self.span[1] - self.span[0], self.other[1] - self.other[0]
                out, into = (highs, lows) if x == 0 else (lows, highs)
                self.send_x, self.got_x = out[1] - out[0], into[1] - into[0]
                self.ywin = pl.ds(self.span[0] * u, self.keep * u)
                self.xsend, self.xgot = pl.ds(out[0] * u, self.send_x * u), pl.ds(into[0] * u, self.got_x * u)
                getattr(self, name)(*args)

    def send(self, src, dst, ssem, rsem, z2, y2, c2, x2):
        return pltpu.make_async_remote_copy(
            src_ref=src, dst_ref=dst, send_sem=ssem, recv_sem=rsem,
            device_id=(z2 * 4 + y2 * 2 + c2, x2), device_id_type=MESH)

    def c_copy(self):
        return self.send(self.g.at[:, :, 1 - self.c], self.cb, self.sc.at[0], self.sc.at[1], self.z, self.y, 1 - self.c, self.x)

    def x_copy(self):
        return self.send(
            self.g.at[:, :, self.c, self.xsend], self.xb.at[:, :, pl.ds(0, self.send_x * self.unit)], self.sx.at[0], self.sx.at[1],
            self.z, self.y, self.c, 1 - self.x)

    def y_copy(self):
        return self.send(
            self.g.at[:, 1 - self.y, self.c, self.ywin], self.yb.at[:, pl.ds(0, self.keep * self.unit)], self.sy.at[0], self.sy.at[1],
            self.z, 1 - self.y, self.c, self.x)

    def z_slot(self, slot):
        return self.zb.at[slot, pl.ds(0, self.keep * self.unit)]

    def z_copy(self, here, to, up):
        there = here + 1 if up else here - 1
        slot = 4 if to == there and not up else to
        return self.send(
            self.g.at[to, self.y, self.c, self.ywin], self.z_slot(slot), self.zs.at[to], self.zr.at[slot], there, self.y, self.c, self.x)

    def f_copy(self):
        return self.send(
            self.g.at[self.z, self.y, self.c, self.ywin], self.fb.at[pl.ds(0, self.keep * self.unit)], self.sf.at[0], self.sf.at[1],
            self.z, self.y, self.c, 1 - self.x)

    def o_copy(self):
        return pltpu.make_async_copy(self.st, self.out, self.so)

    def arrived(self, dst, sem):
        pltpu.make_async_copy(dst, dst, sem).wait()

    def add(self, zz, yy, win, src):
        dst = self.g.at[zz, yy, self.c, win]
        dst[...] = dst[...] + src[...]

    def go(self):
        self.c_copy().start()

    def over_c(self):
        self.c_copy().wait_recv()

        @pl.loop(0, 4)
        def _(zz):
            for yy in (0, 1):
                self.add(zz, yy, slice(None), self.cb.at[zz, yy])

        if self.send_x:
            self.x_copy().start()
        if not self.ones and not self.twos:
            self.y_copy().start()

    def over_x(self):
        if self.got_x:
            got = self.xb.at[:, :, pl.ds(0, self.got_x * self.unit)]
            self.arrived(got, self.sx.at[1])

            @pl.loop(0, 4)
            def _(zz):
                for yy in (0, 1):
                    self.add(zz, yy, self.xgot, got.at[zz, yy])

        self.y_copy().start()

    def over_y(self):
        self.y_copy().wait_recv()

        @pl.loop(0, 4)
        def _(zz):
            self.add(zz, self.y, self.ywin, self.yb.at[zz, pl.ds(0, self.keep * self.unit)])

    def take(self, zz, slot):
        self.arrived(self.z_slot(slot), self.zr.at[slot])
        self.add(zz, self.y, self.ywin, self.z_slot(slot))

    def over_z(self, k):
        for up in (True, False):
            here = k if up else 3 - k

            @pl.when(self.z == here)
            def _():
                for to in (range(3, here, -1) if up else range(here)):
                    if k:
                        self.take(to, to)
                    self.z_copy(here, to, up).start()
                if k:
                    self.take(here, here if up else 4)

    def hand(self):
        self.f_copy().start()

    def finish(self, before):
        u = self.unit
        self.arrived(self.fb.at[pl.ds(0, self.theirs * u)], self.sf.at[1])
        if before is not None:
            before.o_copy().wait()
        own = self.g.at[self.z, self.y, self.c]
        (a, b), (c, d) = self.span, self.other
        for lo, hi in ((0, max(a, c)), (max(a, c), min(b, d)), (min(b, d), 4)):
            if lo < hi:
                mine, theirs = own[lo * u:hi * u, :].astype(f32), None
                if c <= lo and hi <= d:
                    theirs = self.fb[(lo - c) * u:(hi - c) * u, :].astype(f32)
                held = a <= lo and hi <= b
                self.st[lo * u:hi * u, :] = theirs if not held else mine if theirs is None else mine + theirs
        self.o_copy().start()
        self.c_copy().wait_send()
        if self.send_x:
            self.x_copy().wait_send()
        self.y_copy().wait_send()
        self.f_copy().wait_send()
        for here in range(4):
            @pl.when(self.z == here)
            def _():
                for to in range(4):
                    if to != here:
                        self.z_copy(here, to, to > here).wait_send()


def chunk_bufs(rows, cols):
    part = rows // 4
    sizes = ((11, 4, 2, 2, rows, cols), (4, 4, 2, rows, cols), (6, 4, 2, part, cols), (6, 4, rows, cols), (6, 5, rows, cols), (8, rows, cols))
    return [pltpu.VMEM(s, bf16) for s in sizes] + [pltpu.VMEM((2, rows, cols), f32)]


def chunk_sems(n):
    return [pltpu.SemaphoreType.DMA(s) for s in ((n, 2), (n, 2), (n, 2), (n, 4), (n, 5), (n, 2), (n,))]


class Totals:
    def __init__(self, mine, got, sem, at):
        self.mine, self.got, self.sem = mine, got, sem
        z, y, c, x = at
        self.to = [(z, y, 1 - c, x), (z, y, c, 1 - x), (z, 1 - y, c, x), (z + 1 - 2 * (z % 2), y, c, x), (3 - z, y, c, x)]

    def copy(self, s):
        z, y, c, x = self.to[s]
        return pltpu.make_async_remote_copy(
            src_ref=self.mine.at[s], dst_ref=self.got.at[s], send_sem=self.sem.at[s, 0], recv_sem=self.sem.at[s, 1],
            device_id=(z * 4 + y * 2 + c, x), device_id_type=MESH)

    def step(self, s):
        if s > 0:
            self.copy(s - 1).wait()
            self.mine[s] = self.mine[s - 1] + self.got[s - 1]
        if s < 5:
            self.copy(s).start()


def backward_kernel(plan, cot, cos, sin, norm_gain, query_gain, key_gain, mlp_gain, lse, *refs):
    full, refs = refs[:7], refs[7:]
    (hid_i, q_i, k_i, v_i, qraw_i, kraw_i, ain_i, attn_i, mid_i, mlp_i, gate_i, up_i, hidden_i, bias_i), refs = refs[:14], refs[14:]
    grads, refs = refs[:7], refs[7:]
    (out_o, gin_o, norm_o, query_o, key_o, mlp_o), refs = refs[:6], refs[6:]
    (hidden, mlp, ggate, gup, mid, acc, gproj, attn, q, k, v, qraw, kraw, ain, dk, dv, kt, bias, wbuf, earlier, sum_one, sum_two, sum_q, sum_k,
     gain_mine, gain_got, gain_sem, load_sem, w_sem, early_sem), refs = refs[:30], refs[30:]
    bufs, sems = refs[:7], refs[7:]
    at = place()
    z, y, c, x = at
    rows, width = cot.shape
    hd = cos.shape[1]
    kv, qh = k.shape[1] // hd, q.shape[1] // hd
    group = qh // kv
    span = wbuf.shape[1]
    ff = ggate.shape[1]
    cols = bufs[0].shape[-1]
    first, second = pl.ds(0, rows), pl.ds(rows, rows)
    scale = hd ** (-0.5)
    enter(*at, True)

    loads = Writes(load_sem)
    wide = hidden.shape[1] // 4
    hidden_l = [loads.start(hidden_i.at[:, pl.ds(b * wide, wide)], hidden.at[:, pl.ds(b * wide, wide)]) for b in range(4)]
    blocks = [full[6].at[pl.ds(j * span, span), :] for j in range(ff // span)]
    for j in range(ff // span):
        blocks += [full[4].at[:, pl.ds(j * span, span)], full[5].at[:, pl.ds(j * span, span)]]
    blocks += [full[3].at[pl.ds(j * span, span), :] for j in range(qh * hd // span)]
    blocks += [full[1], full[2]] + [full[0].at[:, pl.ds(j * span, span)] for j in range(qh * hd // span)]

    def fetch(n):
        return pltpu.make_async_copy(blocks[n], wbuf.at[n % 2], w_sem.at[n % 2])

    def weight(n):
        fetch(n).wait()
        return wbuf[n % 2]

    def used(n):
        if n + 2 < len(blocks):
            fetch(n + 2).start()

    fetch(0).start()
    fetch(1).start()
    gate_l = loads.start(gate_i, ggate)
    up_l = loads.start(up_i, gup)
    mlp_l, mid_l, attn_l = loads.start(mlp_i, mlp), loads.start(mid_i, mid), loads.start(attn_i, attn)
    later = []

    todo = []

    def put(val, spot, subs, shards_from):
        size = bufs[0].shape[4]
        for f in range(val.shape[0] // (size * subs)):
            for s in range(subs):
                owner = shards_from + f
                lo = (f * subs + s) * size
                bufs[0][(spot + s) % bufs[0].shape[0], owner // 4, owner // 2 % 2, owner % 2] = val[lo:lo + size, :].astype(bf16)

    def make_down(j):
        def run(spot):
            for b in range(4):
                loads.wait(hidden_l[b])
                put(dot_tn(hidden[:, b * wide:(b + 1) * wide], cot[:, j * cols:(j + 1) * cols]), spot, wide // 256, b * 4)
        return run

    def make_out(j):
        def run(spot):
            loads.wait(attn_l)
            tall = attn.shape[0] // 4
            for b in range(4):
                put(dot_nn(attn[b * tall:(b + 1) * tall, :], gproj[:, j * cols:(j + 1) * cols]), spot, tall // 256, b * 4)
        return run

    def make(lhs, rhs, j):
        def run(spot):
            put(dot_tn(lhs(), rhs[:, j * cols:(j + 1) * cols]), spot, 1, 0)
        return run

    def mlp_all():
        loads.wait(mlp_l)
        return mlp[...]

    def ain_own():
        return ain[second, :]

    def ain_all():
        return ain[...]

    def add_weight(w, subs, maker, count):
        for j in range(count):
            for s in range(subs):
                out = grads[w].at[pl.ds(s * 64, 64), pl.ds(j * cols, cols)]
                todo.append((maker(j) if s == 0 else None, out))

    add_weight(6, hidden.shape[1] // (64 * 16), make_down, width // cols)
    add_weight(4, 1, lambda j: make(mlp_all, ggate, j), ff // cols)
    add_weight(5, 1, lambda j: make(mlp_all, gup, j), ff // cols)
    add_weight(3, attn.shape[0] // (64 * 16), make_out, width // cols)
    add_weight(0, 1, lambda j: make(ain_own, q, j), qh * hd // cols)
    add_weight(1, 1, lambda j: make(ain_all, k, j), kv * hd // cols)
    add_weight(2, 1, lambda j: make(ain_all, v, j), kv * hd // cols)
    kinds, order = plan
    chunks = [Chunk(i, bufs, sems, at, out, *kinds[i]) for i, (_, out) in enumerate(todo)]

    nb = ff // span

    def piece_down(j):
        block = weight(j)
        acc[...] = dot_nt(cot[...], block)
        cc = slice(j * span, (j + 1) * span)
        for part in range(2):
            more = dot_nn(hidden[:, cc], wbuf[j % 2, :, part * rows:(part + 1) * rows])
            rr = pl.ds(part * rows, rows)
            bias[rr, :] = more if j == 0 else bias[rr, :] + more
        used(j)

    def piece_act(j, part):
        cc = slice(j * span, (j + 1) * span)
        loads.wait(gate_l)
        loads.wait(up_l)

        def act(r, n):
            rr = pl.ds(pl.multiple_of(r + part * (rows // 2), n), n)
            grad = acc[rr, :]
            ggate[rr, cc] = (grad * ggate[rr, cc].astype(f32)).astype(bf16)
            gup[rr, cc] = (grad * gup[rr, cc].astype(f32)).astype(bf16)

        rows_loop(rows // 2, 64, act)

    def piece_output():
        loads.wait(mid_l)
        for part in range(2):
            cc = slice(part * rows, (part + 1) * rows)
            gproj[:, cc] = (mid[:, cc] + bias[part * rows:(part + 1) * rows, :]).astype(bf16)
        later.append(loads.start(gproj, out_o))
        later.append(loads.start(bias_i, bias))

    def piece_mlp(j, part):
        n = nb + 2 * j + part
        cc = slice(j * span, (j + 1) * span)
        one = dot_nt((gup if part else ggate)[:, cc], weight(n))
        acc[...] = one if n == nb else acc[...] + one
        used(n)

    def fold(into, terms):
        into[...] += jnp.sum(terms.reshape(terms.shape[0] // 8, 8, terms.shape[1]), axis=0)

    def norm_back(grad, unit, inverse, gain):
        scaled = grad * gain
        return inverse * (scaled - unit * jnp.mean(scaled * unit, axis=-1, keepdims=True))

    def piece_mid(part):
        if part == 0:
            loads.wait(later[0])
            sum_two[...] = jnp.zeros_like(sum_two)

        def body(r, n):
            rr = pl.ds(pl.multiple_of(r + part * (rows // 2), n), n)
            unit, inverse = unit_rows(mid[rr, :])
            grad = acc[rr, :]
            fold(sum_two, grad * unit)
            out = cot[rr, :].astype(f32) + norm_back(grad, unit, inverse, mlp_gain[...])
            mid[rr, :] = out
            gproj[rr, :] = out.astype(bf16)

        rows_loop(rows // 2, 64, body)

    at_out = 3 * nb
    n_out = qh * hd // span

    def piece_attn_grad(j):
        hidden[:, j * span:(j + 1) * span] = dot_nt(gproj[...], weight(at_out + j)).astype(bf16)
        used(at_out + j)

    def piece_ready():
        loads.wait(later[1])
        sum_q[...] = jnp.zeros_like(sum_q)
        sum_k[...] = jnp.zeros_like(sum_k)
        loads.wait(attn_l)
        for n in head_l:
            loads.wait(n)
        loads.wait(ain_l)

    c2 = scale * log2e
    tile = rows // 2

    def norm_back_heads(grad, unit, inverse, gain):
        scaled = grad * gain
        mean = dot_nn((scaled * unit).astype(bf16), jnp.full((hd, hd), 1.0 / hd, bf16))
        return inverse * (scaled - unit * mean)

    def piece_head(h, g, i):
        cc = slice(h * hd, (h + 1) * hd)
        n = h * group + g
        qc = slice(n * hd, (n + 1) * hd)
        if g == 0 and i == 0:
            kt[...] = k[:, cc].T
            dk[...] = jnp.zeros_like(dk)
            dv[...] = jnp.zeros_like(dv)
        rs = slice(i * tile, (i + 1) * tile)
        kk = rows + (i + 1) * tile
        query, grad = q[rs, qc], hidden[rs, qc]
        delta = jnp.sum(attn[qc, rs].astype(f32) * grad.T.astype(f32), axis=0, keepdims=True)
        p = jnp.exp2(dot_nt(k[:kk, cc], query) * c2 + (bias[:kk, rs] - lse[n:n + 1, rs]))
        gp = dot_nt(v[:kk, cc], grad)
        ds = (p * (gp - delta)).astype(bf16)
        dv[:kk, :] += dot_nn(p.astype(bf16), grad)
        dk[:kk, :] += dot_nn(ds, query)
        dq = dot_nn(kt[:, :kk], ds).T * scale
        unit, inverse = unit_heads(qraw[rs, qc].astype(f32))
        t = slice(rows + i * tile, rows + (i + 1) * tile)
        back = turn_back(dq, cos[t, :], sin[t, :])
        fold(sum_q, back * unit)
        q[rs, qc] = norm_back_heads(back, unit, inverse, query_gain[...]).astype(bf16)

    def piece_keys(h):
        cc = slice(h * hd, (h + 1) * hd)
        for r in range(0, 2 * rows, tile):
            rr = slice(r, r + tile)
            unit, inverse = unit_heads(kraw[rr, cc].astype(f32))
            back = turn_back(dk[rr, :] * scale, cos[rr, :], sin[rr, :])
            fold(sum_k, back * unit)
            k[rr, cc] = norm_back_heads(back, unit, inverse, key_gain[...]).astype(bf16)
            v[rr, cc] = dv[rr, :].astype(bf16)

    at_kv = at_out + n_out
    early_rows = rows // 8

    def handed(n):
        part = pl.ds(n * early_rows, early_rows)
        return pltpu.make_async_remote_copy(
            src_ref=gproj.at[part, :], dst_ref=earlier.at[part, :], send_sem=early_sem.at[0, n], recv_sem=early_sem.at[1, n],
            device_id=(z * 4 + y * 2 + c, 1 - x), device_id_type=MESH)

    def piece_hand(n):
        @pl.when(x == 1)
        def _():
            handed(n).start()

    def piece_queries(j):
        acc[...] += dot_nt(q[:, j * span:(j + 1) * span], weight(at_kv + 2 + j))
        used(at_kv + 2 + j)

    x_in, x_out = mlp, ggate.at[:, pl.ds(0, span)]
    late = []

    def piece_gain():
        loads.wait(late[0])
        sum_one[...] = jnp.zeros_like(sum_one)

        def body(r, n):
            rr = pl.ds(r, n)
            unit, _ = unit_rows(x_in[rr, :].astype(f32))
            fold(sum_one, acc[rr, :] * unit)

        rows_loop(rows, 64, body)

        @pl.when(x == 1)
        def _():
            def more(r, n):
                rr = pl.ds(r, n)
                fold(sum_one, gproj[rr, :].astype(f32) * ain[rr, :].astype(f32) / norm_gain[...])

            rows_loop(rows, 64, more)

        gain_mine[0] = jnp.zeros_like(gain_mine[0])
        gain_mine[0, 0:1, :] = jnp.sum(sum_one[...], axis=0, keepdims=True)
        gain_mine[0, 1:2, :] = jnp.sum(sum_two[...], axis=0, keepdims=True)
        gain_mine[0, 2:3, 0:hd] = jnp.sum(sum_q[...], axis=0, keepdims=True)
        gain_mine[0, 3:4, 0:hd] = jnp.sum(sum_k[...], axis=0, keepdims=True)

    def piece_last():
        @pl.when(x == 0)
        def _():
            for n in range(8):
                handed(n).wait_recv()

            def more(r, n):
                rr = pl.ds(r, n)
                acc[rr, :] += earlier[rr, :].astype(f32)

            rows_loop(rows, 64, more)

        def body(r, n):
            rr = pl.ds(r, n)
            unit, inverse = unit_rows(x_in[rr, :].astype(f32))
            x_out[rr, :] = (mid[rr, :] + norm_back(acc[rr, :], unit, inverse, norm_gain[...])).astype(bf16)

        rows_loop(rows, 64, body)
        loads.start(x_out, gin_o)

    def piece_earlier():
        w_k, w_v = weight(at_kv), weight(at_kv + 1)

        @pl.when(x == 1)
        def _():
            gproj[...] = (dot_nt(k[first, :], w_k) + dot_nt(v[first, :], w_v)).astype(bf16)

    def piece_own():
        acc[...] = dot_nt(k[second, :], wbuf[at_kv % 2]) + dot_nt(v[second, :], wbuf[(at_kv + 1) % 2])
        used(at_kv)
        used(at_kv + 1)
        late.append(loads.start(hid_i, x_in))

    totals = Totals(gain_mine, gain_got, gain_sem, at)
    chain = []
    for j in range(nb):
        chain += [(piece_down, j), (piece_act, j, 0), (piece_act, j, 1)]
    for j in range(nb):
        chain += [(piece_mlp, j, 0), (piece_mlp, j, 1)]
    chain += [(piece_mid, 0), (piece_mid, 1)] + [(piece_attn_grad, j) for j in range(n_out)] + [(piece_ready,)]
    for h in range(kv):
        chain += [(piece_head, h, g, i) for g in range(group) for i in range(2)] + [(piece_keys, h)]
    chain += [(piece_earlier,), (piece_own,)] + [(piece_queries, j) for j in range(n_out)] + [(piece_gain,)]
    chain += [(totals.step, s) for s in range(6)] + [(piece_last,)]
    made, ended = 0, []
    for kind, index, name in order:
        if kind == 0:
            if name == 0:
                if todo[index][0] is not None:
                    todo[index][0](index)
                    if made == 0:
                        head_l = [loads.start(a, b) for a, b in ((q_i, q), (k_i, k), (v_i, v), (qraw_i, qraw), (kraw_i, kraw))]
                        ain_l = loads.start(ain_i, ain)
                        made = 1
                chunks[index].step("go")
            elif name <= 2:
                chunks[index].step(("over_c", "over_x")[name - 1])
            elif name == 8:
                chunks[index].st = bufs[6].at[len(ended) % 2]
                chunks[index].step("finish", ended[-2] if len(ended) > 1 else None)
                ended.append(chunks[index])
            else:
                if name == 3:
                    chunks[index].step("over_y")
                chunks[index].step("over_z", name - 3)
                if name == 6:
                    chunks[index].step("hand")
        elif kind == 1:
            chain[index][0](*chain[index][1:])
            if index == 3 * nb - 1:
                piece_output()
        else:
            piece_hand(index)
    for ch in ended[-2:]:
        ch.o_copy().wait()

    @pl.when(x == 1)
    def _():
        for n in range(8):
            handed(n).wait_send()

    loads.wait_all()
    norm_o[...] = gain_mine[5, 0:1, :]
    mlp_o[...] = gain_mine[5, 1:2, :]
    query_o[...] = gain_mine[5, 2:3, 0:hd]
    key_o[...] = gain_mine[5, 3:4, 0:hd]


def backward(hid, cot, gains, saved, shards):
    rows, width = hid.shape
    full = saved[:7]
    q, k, v, qraw, kraw, ain, attn, lse, mid, mlp, gate, up, hidden, cos, sin, _, bias = saved[7:]
    hd = cos.shape[1]
    shape, vm, dma = jax.ShapeDtypeStruct, pltpu.VMEM, pltpu.SemaphoreType.DMA
    heads, keys, ff = q.shape[1], k.shape[1], gate.shape[1]
    span = keys
    outs = [shape(s.shape, f32) for s in shards] + [
        shape((rows, width), bf16), shape((rows, width), bf16), shape((1, width), f32), shape((1, hd), f32), shape((1, hd), f32), shape((1, width), f32)]
    n = sum(s.shape[0] // 64 * (s.shape[1] // 512) for s in shards)
    return pl.pallas_call(
        functools.partial(backward_kernel, BACKWARD_PLAN),
        out_shape=outs,
        in_specs=[VMEM] * 8 + [HBM] * 21,
        out_specs=[HBM] * 9 + [VMEM] * 4,
        scratch_shapes=[
            vm((rows, ff), bf16), vm((rows, width), bf16), vm((rows, ff), bf16), vm((rows, ff), bf16), vm((rows, width), f32), vm((rows, width), f32),
            vm((rows, width), bf16), vm((heads, rows), bf16), vm((rows, heads), bf16), vm((2 * rows, keys), bf16), vm((2 * rows, keys), bf16),
            vm((rows, heads), bf16), vm((2 * rows, keys), bf16), vm((2 * rows, width), bf16), vm((2 * rows, hd), f32), vm((2 * rows, hd), f32),
            vm((hd, 2 * rows), bf16), vm((2 * rows, rows), f32), vm((2, span, span), bf16), vm((rows, width), bf16),
            vm((8, width), f32), vm((8, width), f32), vm((8, hd), f32), vm((8, hd), f32), vm((6, 8, width), f32), vm((5, 8, width), f32),
            dma((5, 2)), dma((32,)), dma((2,)), dma((2, 8))] + chunk_bufs(64, 512) + chunk_sems(n),
        compiler_params=pltpu.CompilerParams(collective_id=2, has_side_effects=True, vmem_limit_bytes=63 * 2**20),
        name="backward_reduce",
    )(cot, cos, sin, *gains, lse, *full, hid, q, k, v, qraw, kraw, ain, attn, mid, mlp, gate, up, hidden, bias)


def place_kernel(*refs):
    n = (len(refs) - 1) // 3
    first = [pltpu.make_async_copy(refs[i], refs[2 * n + i], refs[-1].at[0, i]) for i in range(n)]
    second = [pltpu.make_async_copy(refs[2 * n + i], refs[n + i], refs[-1].at[1, i]) for i in range(n)]
    for copy in first:
        copy.start()
    for i in range(n):
        first[i].wait()
        second[i].start()
    for copy in second:
        copy.wait()


def placed(arrays):
    n = len(arrays)
    return pl.pallas_call(
        place_kernel,
        out_shape=[jax.ShapeDtypeStruct(a.shape, a.dtype) for a in arrays],
        in_specs=[HBM] * n,
        out_specs=[HBM] * n,
        scratch_shapes=[pltpu.VMEM(a.shape, a.dtype) for a in arrays] + [pltpu.SemaphoreType.DMA((2, n))],
        compiler_params=pltpu.CompilerParams(vmem_limit_bytes=62 * 2**20),
        name="place_results",
    )(*arrays)


def as_sent(shard):

    def short(part):
        return part.astype(jnp.bfloat16) if part.dtype == jnp.float32 else part

    return jax.tree.map(short, shard)


def norm_rows(values, gain_vec):
    inverse = lax.rsqrt(jnp.mean(values * values, axis=-1, keepdims=True) + epsilon)
    normed = values * inverse
    return (normed * gain_vec, normed, inverse)


def norm_back(grad_out, gain_vec, normed, inverse):
    scaled = grad_out * gain_vec
    grad_in = inverse * (scaled - normed * jnp.mean(scaled * normed, axis=-1, keepdims=True))
    return (grad_in, grad_out * normed)


def rope_tables(positions, head_dim):
    frequency = theta_base ** (-jnp.arange(0, head_dim, 2).astype(jnp.float32) / head_dim)
    angles = positions.astype(jnp.float32)[:, None] * frequency[None, :]
    angles = jnp.concatenate([angles, angles], axis=-1)
    return (jnp.cos(angles), jnp.sin(angles))


def rotate(values, cosine, sine_tab):
    half_dim = values.shape[-1] // 2
    turned = jnp.concatenate([-values[..., half_dim:], values[..., :half_dim]], axis=-1)
    return values * cosine[:, None, :] + turned * sine_tab[:, None, :]


def rotate_back(grad_out, cosine, sine_tab):
    half_dim = grad_out.shape[-1] // 2
    weighted = grad_out * sine_tab[:, None, :]
    turned = jnp.concatenate([weighted[..., half_dim:], -weighted[..., :half_dim]], axis=-1)
    return grad_out * cosine[:, None, :] + turned


def back_dot(grad_rows, weight):
    return lax.dot_general(
        grad_rows, weight, (((1,), (1,)), ((), ())), preferred_element_type=jnp.float32
    )


def weight_term(acts_in, grad_out):
    return lax.dot_general(
        acts_in, grad_out, (((0,), (0,)), ((), ())), preferred_element_type=jnp.float32
    )


def per_device(
    hidden_in,
    positions,
    cotangent,
    norm_gain,
    w_query,
    w_key,
    w_value,
    query_gain,
    key_gain,
    w_out,
    mlp_gain,
    w_gate,
    w_up,
    w_down,
):
    seqs_here, block_len, model_width = hidden_in.shape
    head_dim = query_gain.shape[0]
    kv_heads = w_key.shape[1] // head_dim
    q_heads = w_query.shape[1] // head_dim
    groups = q_heads // kv_heads
    ctx_count = lax.axis_size("ctx")
    ctx_rank = lax.axis_index("ctx")
    seq_total = block_len * ctx_count
    row_count = seqs_here * block_len
    scale_val = head_dim ** (-0.5)
    shards = (w_query, w_key, w_value, w_out, w_gate, w_up, w_down)
    full_weights = (
        lax.all_gather(shards[0], "fsdp", axis=0, tiled=True),
        lax.all_gather(shards[1], "fsdp", axis=0, tiled=True),
        lax.all_gather(shards[2], "fsdp", axis=0, tiled=True),
        lax.all_gather(shards[3], "fsdp", axis=0, tiled=True),
        lax.all_gather(shards[4], "fsdp", axis=0, tiled=True),
        lax.all_gather(shards[5], "fsdp", axis=0, tiled=True),
        lax.all_gather(shards[6], "fsdp", axis=0, tiled=True),
    )
    full_query, full_key, full_value, full_out, full_gate, full_up, full_down = full_weights
    residual = hidden_in.astype(jnp.float32).reshape(row_count, model_width)
    scaled_one, normed_one, inverse_one = norm_rows(residual, norm_gain)
    attn_in = scaled_one.astype(jnp.bfloat16)
    query_raw = jnp.dot(attn_in, full_query, preferred_element_type=jnp.float32).reshape(
        row_count, q_heads, head_dim
    )
    key_raw = jnp.dot(attn_in, full_key, preferred_element_type=jnp.float32).reshape(
        row_count, kv_heads, head_dim
    )
    value_bf = jnp.dot(attn_in, full_value, preferred_element_type=jnp.float32).astype(jnp.bfloat16)
    flat_pos = positions.reshape(row_count)
    cosine, sine_tab = rope_tables(flat_pos, head_dim)
    query_scaled, query_normed, query_inverse = norm_rows(query_raw, query_gain)
    query_bf = rotate(query_scaled, cosine, sine_tab).astype(jnp.bfloat16)
    key_scaled, key_normed, key_inverse = norm_rows(key_raw, key_gain)
    key_bf = rotate(key_scaled, cosine, sine_tab).astype(jnp.bfloat16)
    key_flat = key_bf.reshape(seqs_here, block_len, kv_heads * head_dim)
    value_flat = value_bf.reshape(seqs_here, block_len, kv_heads * head_dim)
    keys_all, values_all = (
        lax.all_gather(key_flat, "ctx", axis=1, tiled=True),
        lax.all_gather(value_flat, "ctx", axis=1, tiled=True),
    )
    query_five = query_bf.reshape(seqs_here, block_len, kv_heads, groups, head_dim)
    query_index = ctx_rank * block_len + jnp.arange(block_len, dtype=jnp.int32)
    doc_start = query_index[None, :] - positions

    def block_scores(key_source, block_idx):
        key_block = lax.dynamic_slice_in_dim(key_source, block_idx * block_len, block_len, 1)
        scores = (
            jnp.einsum(
                "sqkgd,spkd->skgqp", query_five, key_block, preferred_element_type=jnp.float32
            )
            * scale_val
        )
        key_index = block_idx * block_len + jnp.arange(block_len, dtype=jnp.int32)
        allowed = (key_index[None, None, :] <= query_index[None, :, None]) & (
            key_index[None, None, :] >= doc_start[:, :, None]
        )
        return (jnp.where(allowed[:, None, None, :, :], scores, -1e30), key_block)

    keys_four = keys_all.reshape(seqs_here, seq_total, kv_heads, head_dim)
    values_four = values_all.reshape(seqs_here, seq_total, kv_heads, head_dim)

    def stats_step(block_idx, carry_stats):
        running_max, running_sum = carry_stats
        scores, key_block = block_scores(keys_four, block_idx)
        new_max = jnp.maximum(running_max, jnp.max(scores, axis=-1))
        running_sum = running_sum * jnp.exp(running_max - new_max) + jnp.sum(
            jnp.exp(scores - new_max[..., None]), axis=-1
        )
        return (new_max, running_sum)

    stat_shape = (seqs_here, kv_heads, groups, block_len)
    row_max, row_sum = lax.fori_loop(
        0,
        ctx_rank + 1,
        stats_step,
        (jnp.full(stat_shape, -1e30, jnp.float32), jnp.zeros(stat_shape, jnp.float32)),
    )

    def output_step(block_idx, accum):
        scores, key_block = block_scores(keys_four, block_idx)
        probs_bf = (jnp.exp(scores - row_max[..., None]) / row_sum[..., None]).astype(jnp.bfloat16)
        value_block = lax.dynamic_slice_in_dim(values_four, block_idx * block_len, block_len, 1)
        return accum + jnp.einsum(
            "skgqp,spkd->sqkgd", probs_bf, value_block, preferred_element_type=jnp.float32
        )

    attn_f32 = lax.fori_loop(
        0,
        ctx_rank + 1,
        output_step,
        jnp.zeros((seqs_here, block_len, kv_heads, groups, head_dim), jnp.float32),
    )
    attn_bf = attn_f32.reshape(row_count, q_heads * head_dim).astype(jnp.bfloat16)
    middle = residual + jnp.dot(attn_bf, full_out, preferred_element_type=jnp.float32)
    scaled_two, normed_two, inverse_two = norm_rows(middle, mlp_gain)
    mlp_in = scaled_two.astype(jnp.bfloat16)
    gate_pre = jnp.dot(mlp_in, full_gate, preferred_element_type=jnp.float32)
    up_pre = jnp.dot(mlp_in, full_up, preferred_element_type=jnp.float32)
    sigmoid_gate = jax.nn.sigmoid(gate_pre)
    silu_gate = gate_pre * sigmoid_gate
    hidden_bf = (silu_gate * up_pre).astype(jnp.bfloat16)
    layer_out = middle + jnp.dot(hidden_bf, full_down, preferred_element_type=jnp.float32)
    output = layer_out.astype(jnp.bfloat16).reshape(seqs_here, block_len, model_width)
    back_weights = full_weights
    keys_back, values_back = (
        lax.all_gather(key_flat, "ctx", axis=1, tiled=True),
        lax.all_gather(value_flat, "ctx", axis=1, tiled=True),
    )
    back_query, back_key, back_value, back_out, back_gate, back_up, back_down = back_weights
    keys_again = keys_back.reshape(seqs_here, seq_total, kv_heads, head_dim)
    values_again = values_back.reshape(seqs_here, seq_total, kv_heads, head_dim)
    grad_rows = cotangent.reshape(row_count, model_width)
    down_grad = back_dot(grad_rows, back_down)
    grad_gate = (
        down_grad * up_pre * sigmoid_gate * (1.0 + gate_pre * (1.0 - sigmoid_gate))
    ).astype(jnp.bfloat16)
    grad_up = (down_grad * silu_gate).astype(jnp.bfloat16)
    grad_mlp_in = back_dot(grad_gate, back_gate) + back_dot(grad_up, back_up)
    grad_norm_two, mlp_gain_terms = norm_back(grad_mlp_in, mlp_gain, normed_two, inverse_two)
    grad_mid = grad_rows.astype(jnp.float32) + grad_norm_two
    grad_proj = grad_mid.astype(jnp.bfloat16)
    grad_attn = back_dot(grad_proj, back_out).astype(jnp.bfloat16)
    grad_five = grad_attn.reshape(seqs_here, block_len, kv_heads, groups, head_dim)
    delta = jnp.einsum("sqkgd,sqkgd->skgq", grad_five.astype(jnp.float32), attn_f32)

    def grad_step(block_idx, carry_grads):
        grad_query, grad_keys, grad_values = carry_grads
        scores, key_block = block_scores(keys_again, block_idx)
        probs = jnp.exp(scores - row_max[..., None]) / row_sum[..., None]
        value_block = lax.dynamic_slice_in_dim(values_again, block_idx * block_len, block_len, 1)
        grad_probs = jnp.einsum(
            "sqkgd,spkd->skgqp", grad_five, value_block, preferred_element_type=jnp.float32
        )
        grad_scores = (probs * (grad_probs - delta[..., None])).astype(jnp.bfloat16)
        grad_query = (
            grad_query
            + jnp.einsum(
                "skgqp,spkd->sqkgd", grad_scores, key_block, preferred_element_type=jnp.float32
            )
            * scale_val
        )
        key_part = (
            jnp.einsum(
                "skgqp,sqkgd->spkd", grad_scores, query_five, preferred_element_type=jnp.float32
            )
            * scale_val
        )
        value_part = jnp.einsum(
            "skgqp,sqkgd->spkd",
            probs.astype(jnp.bfloat16),
            grad_five,
            preferred_element_type=jnp.float32,
        )
        grad_keys = lax.dynamic_update_slice_in_dim(grad_keys, key_part, block_idx * block_len, 1)
        grad_values = lax.dynamic_update_slice_in_dim(
            grad_values, value_part, block_idx * block_len, 1
        )
        return (grad_query, grad_keys, grad_values)

    whole_shape = (seqs_here, seq_total, kv_heads, head_dim)
    grad_query, grad_keys, grad_values = lax.fori_loop(
        0,
        ctx_rank + 1,
        grad_step,
        (
            jnp.zeros((seqs_here, block_len, kv_heads, groups, head_dim), jnp.float32),
            jnp.zeros(whole_shape, jnp.float32),
            jnp.zeros(whole_shape, jnp.float32),
        ),
    )
    key_grad_own, value_grad_own = (
        lax.psum_scatter(
            grad_keys.reshape(seqs_here, seq_total, kv_heads * head_dim).astype(jnp.bfloat16),
            "ctx",
            scatter_dimension=1,
            tiled=True,
        ).astype(jnp.float32),
        lax.psum_scatter(
            grad_values.reshape(seqs_here, seq_total, kv_heads * head_dim).astype(jnp.bfloat16),
            "ctx",
            scatter_dimension=1,
            tiled=True,
        ).astype(jnp.float32),
    )
    key_unrot = rotate_back(key_grad_own.reshape(row_count, kv_heads, head_dim), cosine, sine_tab)
    key_raw_grad, key_gain_terms = norm_back(key_unrot, key_gain, key_normed, key_inverse)
    key_raw_bf = key_raw_grad.reshape(row_count, kv_heads * head_dim).astype(jnp.bfloat16)
    query_unrot = rotate_back(grad_query.reshape(row_count, q_heads, head_dim), cosine, sine_tab)
    query_raw_grad, query_gain_terms = norm_back(
        query_unrot, query_gain, query_normed, query_inverse
    )
    query_raw_bf = query_raw_grad.reshape(row_count, q_heads * head_dim).astype(jnp.bfloat16)
    value_raw_bf = value_grad_own.reshape(row_count, kv_heads * head_dim).astype(jnp.bfloat16)
    grad_attn_in = (
        back_dot(query_raw_bf, back_query)
        + back_dot(key_raw_bf, back_key)
        + back_dot(value_raw_bf, back_value)
    )
    grad_norm_one, norm_gain_terms = norm_back(grad_attn_in, norm_gain, normed_one, inverse_one)
    grad_input = (
        (grad_mid + grad_norm_one).astype(jnp.bfloat16).reshape(seqs_here, block_len, model_width)
    )
    gain_one, gain_query, gain_key, gain_two = lax.psum(
        (
            jnp.sum(norm_gain_terms, axis=0),
            jnp.sum(query_gain_terms, axis=(0, 1)),
            jnp.sum(key_gain_terms, axis=(0, 1)),
            jnp.sum(mlp_gain_terms, axis=0),
        ),
        ("fsdp", "ctx"),
    )
    weight_pairs = (
        (attn_in, query_raw_bf),
        (attn_in, key_raw_bf),
        (attn_in, value_raw_bf),
        (attn_bf, grad_proj),
        (mlp_in, grad_gate),
        (mlp_in, grad_up),
        (hidden_bf, grad_rows),
    )
    pieces = tuple(
        (
            lax.psum_scatter(
                weight_term(acts_in, grad_out).astype(jnp.bfloat16),
                "fsdp",
                scatter_dimension=0,
                tiled=True,
            ).astype(jnp.float32)
            for acts_in, grad_out in weight_pairs
        )
    )
    weight_grads = jax.tree.map(
        lambda part: part.astype(jnp.float32), lax.psum(as_sent(pieces), "ctx")
    )
    grad_wq, grad_wk, grad_wv, grad_wo, grad_wg, grad_wu, grad_wd = weight_grads
    return (
        output,
        grad_input,
        gain_one,
        grad_wq,
        grad_wk,
        grad_wv,
        gain_query,
        gain_key,
        grad_wo,
        gain_two,
        grad_wg,
        grad_wu,
        grad_wd,
    )


def grid_device(hidden_in, positions, cotangent, norm_gain, w_query, w_key, w_value, query_gain, key_gain, w_out, mlp_gain, w_gate, w_up, w_down):
    rows, width = hidden_in.shape[1:]
    head_dim = query_gain.shape[0]
    hid, cot = hidden_in.reshape(rows, width), cotangent.reshape(rows, width)
    half = theta_base ** (-np.arange(0, head_dim, 2) / head_dim)
    freq = jnp.asarray(np.concatenate([half, half])[None], jnp.float32)
    gains = [g[None, :] for g in (norm_gain, query_gain, key_gain, mlp_gain)]
    shards = (w_query, w_key, w_value, w_out, w_gate, w_up, w_down)
    saved = forward(hid, positions, freq, gains, shards)
    done = placed(backward(hid, cot, gains, saved, shards))
    gq, gk, gv, go, gg, gu, gd, out, grad_in, norm, query, key, mlp = done
    return (out[None], grad_in[None], norm[0], gq, gk, gv, query[0], key[0], go, mlp[0], gg, gu, gd)


def is_grid(mesh):
    if dict(mesh.shape) != {"fsdp": 16, "ctx": 2}:
        return False
    for f in range(16):
        for x in range(2):
            device = mesh.devices[f, x]
            if tuple(device.coords) != (x, (f // 2) % 2, f // 4) or device.core_on_chip != f % 2:
                return False
    return True


def solution(mesh):
    in_specs = (
        P("fsdp", "ctx", None),
        P("fsdp", "ctx"),
        P("fsdp", "ctx", None),
        P(),
        P("fsdp", None),
        P("fsdp", None),
        P("fsdp", None),
        P(),
        P(),
        P("fsdp", None),
        P(),
        P("fsdp", None),
        P("fsdp", None),
        P("fsdp", None),
    )
    out_specs = (
        P("fsdp", "ctx", None),
        P("fsdp", "ctx", None),
        P(),
        P("fsdp", None),
        P("fsdp", None),
        P("fsdp", None),
        P(),
        P(),
        P("fsdp", None),
        P(),
        P("fsdp", None),
        P("fsdp", None),
        P("fsdp", None),
    )
    return jax.shard_map(
        grid_device if is_grid(mesh) else per_device, mesh=mesh, in_specs=in_specs, out_specs=out_specs, check_vma=False
    )
```
